128 devices in a mesh: dp: 16 (over z, x), ctx: 2 (over core), tensor: 4 (over y).
Axes of the slice: x: 4, y: 4, z: 4, core: 2. Of those that a mesh axis runs over, the one named last changes fastest.
Arguments:
- inputs: float32 [16, 1024, 1088], P('dp', ('ctx', 'tensor')), may hold values from -6 to 6
- cotangent: float32 [16, 1024, 1088], P('dp', ('ctx', 'tensor')), may hold values from -6 to 6
- prenorm: float32 [1, 1088], P(None, ('dp', 'ctx')), may hold values from 0.25 to 1.75
- qkv_weight: float32 [1, 1088, 3264], P(None, ('dp', 'ctx')), may hold values from -0.1875 to 0.1875
- merge_weight: float32 [1, 1088, 1088], P(None, ('dp', 'ctx')), may hold values from -3 to 3
- midnorm: float32 [1, 1088], P(None, ('dp', 'ctx')), may hold values from 0.25 to 1.75
- up_weight: float32 [1, 1088, 4352], P(None, ('dp', 'ctx'), 'tensor'), may hold values from -0.1875 to 0.1875
- down_weight: float32 [1, 4352, 1088], P(None, 'tensor', ('dp', 'ctx')), may hold values from -0.09375 to 0.09375
- prenorm_mean: float32 [1, 1088], P(None, ('dp', 'ctx')), may hold values from -448 to 448
- prenorm_square: float32 [1, 1088], P(None, ('dp', 'ctx')), may hold values from 1310.72 to 13107.2
- qkv_mean: float32 [1, 1088, 3264], P(None, ('dp', 'ctx')), may hold values from -320 to 320
- qkv_square: float32 [1, 1088, 3264], P(None, ('dp', 'ctx')), may hold values from 655.36 to 6553.6
- merge_mean: float32 [1, 1088, 1088], P(None, ('dp', 'ctx')), may hold values from -32 to 32
- merge_square: float32 [1, 1088, 1088], P(None, ('dp', 'ctx')), may hold values from 7.3728 to 73.728
- midnorm_mean: float32 [1, 1088], P(None, ('dp', 'ctx')), may hold values from -128 to 128
- midnorm_square: float32 [1, 1088], P(None, ('dp', 'ctx')), may hold values from 117.9648 to 1179.648
- up_mean: float32 [1, 1088, 4352], P(None, ('dp', 'ctx'), 'tensor'), may hold values from -64 to 64
- up_square: float32 [1, 1088, 4352], P(None, ('dp', 'ctx'), 'tensor'), may hold values from 29.4912 to 294.912
- down_mean: float32 [1, 4352, 1088], P(None, 'tensor', ('dp', 'ctx')), may hold values from -224 to 224
- down_square: float32 [1, 4352, 1088], P(None, 'tensor', ('dp', 'ctx')), may hold values from 327.68 to 3276.8
Outputs:
- block_output: float32 [16, 1024, 1088], P('dp', ('ctx', 'tensor'))
- input_grad: float32 [16, 1024, 1088], P('dp', ('ctx', 'tensor'))
- prenorm_grad: float32 [1, 1088], P(None, ('dp', 'ctx'))
- qkv_grad: float32 [1, 1088, 3264], P(None, ('dp', 'ctx'))
- merge_grad: float32 [1, 1088, 1088], P(None, ('dp', 'ctx'))
- midnorm_grad: float32 [1, 1088], P(None, ('dp', 'ctx'))
- up_grad: float32 [1, 1088, 4352], P(None, ('dp', 'ctx'), 'tensor')
- down_grad: float32 [1, 4352, 1088], P(None, 'tensor', ('dp', 'ctx'))
- prenorm_next: float32 [1, 1088], P(None, ('dp', 'ctx'))
- qkv_next: float32 [1, 1088, 3264], P(None, ('dp', 'ctx'))
- merge_next: float32 [1, 1088, 1088], P(None, ('dp', 'ctx'))
- midnorm_next: float32 [1, 1088], P(None, ('dp', 'ctx'))
- up_next: float32 [1, 1088, 4352], P(None, ('dp', 'ctx'), 'tensor')
- down_next: float32 [1, 4352, 1088], P(None, 'tensor', ('dp', 'ctx'))
- prenorm_mean_next: float32 [1, 1088], P(None, ('dp', 'ctx'))
- qkv_mean_next: float32 [1, 1088, 3264], P(None, ('dp', 'ctx'))
- merge_mean_next: float32 [1, 1088, 1088], P(None, ('dp', 'ctx'))
- midnorm_mean_next: float32 [1, 1088], P(None, ('dp', 'ctx'))
- up_mean_next: float32 [1, 1088, 4352], P(None, ('dp', 'ctx'), 'tensor')
- down_mean_next: float32 [1, 4352, 1088], P(None, 'tensor', ('dp', 'ctx'))
- prenorm_square_next: float32 [1, 1088], P(None, ('dp', 'ctx'))
- qkv_square_next: float32 [1, 1088, 3264], P(None, ('dp', 'ctx'))
- merge_square_next: float32 [1, 1088, 1088], P(None, ('dp', 'ctx'))
- midnorm_square_next: float32 [1, 1088], P(None, ('dp', 'ctx'))
- up_square_next: float32 [1, 1088, 4352], P(None, ('dp', 'ctx'), 'tensor')
- down_square_next: float32 [1, 4352, 1088], P(None, 'tensor', ('dp', 'ctx'))
The draws below stay inside these ranges and needn't reach their ends.
All inputs are finite; a program needn't handle non-finite values.
Results may differ from the reference program's by a relative error of at most 0.014.
The reference program's roundings to bfloat16 on the way count: a program that leaves them out, or rounds other values in their place, can miss the bound.
Values may be sent and summed in bfloat16 or wider, within the bound.
No kernel may reach another device: no remote copies, remote signals or barrier semaphores. Data moves between devices by JAX's collectives and lax.ppermute only.
A program may use at most 192 MiB of HBM per device.

```python
import math
import jax
import jax.numpy as jnp
from jax import lax

H = 17
HD = 64
D = 1088
FF = 4352
L = 1
LEN = 1024
SEQS = 16


def draw_inputs(key, part):
    shape = (SEQS, LEN, D)
    values = jax.random.normal(key, shape, jnp.float32)
    return jnp.clip(values, -6.0, 6.0)


def block_scale(stream_key, extent, shards, least, high):
    def one(position, shards_of):
        draws = jax.random.uniform(jax.random.fold_in(jax.random.fold_in(stream_key, 6), position), (shards_of,), jnp.float32, least / len(shards), high / len(shards))
        return jnp.repeat(jnp.exp(draws), extent[position] // shards_of).reshape((-1,) + (1,) * (len(extent) - position - 1))

    level = one(*shards[0])
    for cut in shards[1:]:
        level = level * one(*cut)
    return level


def gaussian(stream_key, dims, deviation, bound, cuts=(), kind=jnp.bfloat16):
    entries = deviation * jax.random.normal(stream_key, dims, jnp.float32)
    if cuts:
        entries = entries * block_scale(stream_key, dims, cuts, -0.22, 0.18)
    return jnp.clip(entries, -bound, bound).astype(kind)


def setup_inputs(seed: int = 0) -> dict:
    splits = jax.random.split(jax.random.key(seed), 21)
    return {
        "inputs": draw_inputs(jax.random.fold_in(splits[20], 71), 0),
        "cotangent": gaussian(splits[1], (SEQS, LEN, D), 1.0, 6.0, ((0, 16), (1, 8)), jnp.float32),
        "prenorm": jnp.clip(1.0 + 0.15 * jax.random.normal(splits[2], (L, D), jnp.float32), 0.25, 1.75),
        "qkv_weight": gaussian(splits[3], (L, D, 3 * D), D ** -0.5, 0.1875, ((1, 32),), jnp.float32),
        "merge_weight": gaussian(splits[4], (L, D, D), (max(1, D // 256)) ** -0.5, 3.0, ((1, 32),), jnp.float32),
        "midnorm": jnp.clip(1.0 + 0.15 * jax.random.normal(splits[5], (L, D), jnp.float32), 0.25, 1.75),
        "up_weight": gaussian(splits[6], (L, D, FF), D ** -0.5, 0.1875, ((1, 32), (2, 4)), jnp.float32),
        "down_weight": gaussian(splits[7], (L, FF, D), FF ** -0.5, 0.09375, ((1, 4), (2, 32)), jnp.float32),
        "prenorm_mean": gaussian(splits[8], (L, D), (0.6 * (SEQS * LEN) ** 0.5), 448.0, ((1, 32),), jnp.float32),
        "prenorm_square": jnp.clip(jnp.exp(math.log(13107.2) - 2.3025851 * jax.random.uniform(splits[9], (L, D), jnp.float32) ** block_scale(splits[9], (L, D), ((1, 32),), -0.2, 0.2)), 1310.72, 13107.2),
        "qkv_mean": gaussian(splits[10], (L, D, 3 * D), (0.42 * (SEQS * LEN) ** 0.5), 320.0, ((1, 32),), jnp.float32),
        "qkv_square": jnp.clip(jnp.exp(math.log(6553.6) - 2.3025851 * jax.random.uniform(splits[11], (L, D, 3 * D), jnp.float32) ** block_scale(splits[11], (L, D, 3 * D), ((1, 32),), -0.2, 0.2)), 655.36, 6553.6),
        "merge_mean": gaussian(splits[12], (L, D, D), (0.045 * (SEQS * LEN) ** 0.5), 32.0, ((1, 32),), jnp.float32),
        "merge_square": jnp.clip(jnp.exp(math.log(73.728) - 2.3025851 * jax.random.uniform(splits[13], (L, D, D), jnp.float32) ** block_scale(splits[13], (L, D, D), ((1, 32),), -0.2, 0.2)), 7.3728, 73.728),
        "midnorm_mean": gaussian(splits[14], (L, D), (0.18 * (SEQS * LEN) ** 0.5), 128.0, ((1, 32),), jnp.float32),
        "midnorm_square": jnp.clip(jnp.exp(math.log(1179.648) - 2.3025851 * jax.random.uniform(splits[15], (L, D), jnp.float32) ** block_scale(splits[15], (L, D), ((1, 32),), -0.2, 0.2)), 117.9648, 1179.648),
        "up_mean": gaussian(splits[16], (L, D, FF), (0.09 * (SEQS * LEN) ** 0.5), 64.0, ((1, 32), (2, 4)), jnp.float32),
        "up_square": jnp.clip(jnp.exp(math.log(294.912) - 2.3025851 * jax.random.uniform(splits[17], (L, D, FF), jnp.float32) ** block_scale(splits[17], (L, D, FF), ((1, 32), (2, 4)), -0.2, 0.2)), 29.4912, 294.912),
        "down_mean": gaussian(splits[18], (L, FF, D), (0.3 * (SEQS * LEN) ** 0.5), 224.0, ((1, 4), (2, 32)), jnp.float32),
        "down_square": jnp.clip(jnp.exp(math.log(3276.8) - 2.3025851 * jax.random.uniform(splits[19], (L, FF, D), jnp.float32) ** block_scale(splits[19], (L, FF, D), ((1, 4), (2, 32)), -0.2, 0.2)), 327.68, 3276.8),
    }


norm_eps = 1e-05
beta_one = 0.9
beta_two = 0.95
adam_eps = 1e-08
decay_rate = 0.1
step_count = 3.0

def rounded(values):
    return lax.optimization_barrier(values.astype(jnp.bfloat16)).astype(jnp.float32)

def smooth_gate(values):
    return jax.nn.gelu(values, approximate=True)

def gelu_back(hidden, grad):
    value, pullback = jax.vjp(smooth_gate, hidden)
    return pullback(grad)[0]

def norm_forward(resid, gain):
    center = resid - lax.optimization_barrier(jnp.mean(resid, axis=-1, keepdims=True))
    invstd = lax.rsqrt(lax.optimization_barrier(jnp.mean(center * center, axis=-1, keepdims=True)) + norm_eps)
    normed = center * invstd
    return (normed, invstd, (normed * gain).astype(jnp.bfloat16))

def norm_backward(grad, normed, invstd, gain):
    scaled = grad * gain
    back = invstd * (scaled - lax.optimization_barrier(jnp.mean(scaled, axis=-1, keepdims=True)) - normed * lax.optimization_barrier(jnp.mean(scaled * normed, axis=-1, keepdims=True)))
    return (back, lax.optimization_barrier(jnp.sum((grad * normed).reshape(-1, grad.shape[-1]), axis=0)))

def masked_scores(query_part, key_full, first):
    score = jnp.einsum('qhd,khd->hqk', query_part, key_full) * HD ** (-0.5)
    rows = query_part.shape[0]
    length = key_full.shape[0]
    row_pos = first + lax.broadcasted_iota(jnp.int32, (rows, length), 0)
    col_pos = lax.broadcasted_iota(jnp.int32, (rows, length), 1)
    return jnp.where((col_pos <= row_pos)[None], score, -jnp.inf)

def attend_forward(query, keys, values):
    total = query.shape[0]
    block = min(512, total)
    query_full = query.astype(jnp.float32)
    key_full = keys.astype(jnp.float32)
    value_full = values.astype(jnp.float32)
    outs = []
    sums = []
    for first in range(0, total, block):
        score = masked_scores(query_full[first:first + block], key_full, first)
        top = lax.optimization_barrier(jnp.max(score, axis=-1, keepdims=True))
        lse = top + jnp.log(lax.optimization_barrier(jnp.sum(jnp.exp(score - top), axis=-1, keepdims=True)))
        probs = rounded(jnp.exp(score - lse))
        outs.append(jnp.einsum('hqk,khd->qhd', probs, value_full).astype(jnp.bfloat16))
        sums.append(lse)
    return (jnp.concatenate(outs, axis=0), jnp.concatenate(sums, axis=1))

def attend_backward(query, keys, values, mixed, lse, mixed_grad):
    total = query.shape[0]
    block = min(512, total)
    query_full = query.astype(jnp.float32)
    key_full = keys.astype(jnp.float32)
    value_full = values.astype(jnp.float32)
    grad_full = mixed_grad.astype(jnp.float32)
    delta = lax.optimization_barrier(jnp.sum(grad_full * mixed.astype(jnp.float32), axis=-1))
    key_grad = jnp.zeros(keys.shape, jnp.float32)
    value_grad = jnp.zeros(values.shape, jnp.float32)
    query_parts = []
    for first in range(0, total, block):
        query_part = query_full[first:first + block]
        grad_part = grad_full[first:first + block]
        score = masked_scores(query_part, key_full, first)
        probs = jnp.exp(score - lse[:, first:first + block])
        value_grad = value_grad + jnp.einsum('hqk,qhd->khd', rounded(probs), grad_part)
        prob_grad = jnp.einsum('qhd,khd->hqk', grad_part, value_full)
        score_grad = rounded(probs * (prob_grad - delta[first:first + block].T[:, :, None]) * HD ** (-0.5))
        query_parts.append(jnp.einsum('hqk,khd->qhd', score_grad, key_full))
        key_grad = key_grad + jnp.einsum('hqk,qhd->khd', score_grad, query_part)
    return (jnp.concatenate(query_parts, axis=0), key_grad, value_grad)

def split_heads(flat):
    return flat.reshape(flat.shape[0], H, HD)

def layer_forward(resid, params):
    pregain, attn_in, attn_out, midgain, ffn_up, ffn_down = params
    pre_normed, pre_invstd, pre_act = norm_forward(resid, pregain.astype(jnp.float32))
    qkv = jnp.dot(pre_act, attn_in, preferred_element_type=jnp.float32).astype(jnp.bfloat16)
    query = split_heads(qkv[:, :D])
    keys = split_heads(qkv[:, D:2 * D])
    values = split_heads(qkv[:, 2 * D:])
    mixed, lse = attend_forward(query, keys, values)
    mixed_flat = mixed.reshape(-1, D)
    middle = resid + jnp.dot(mixed_flat, attn_out, preferred_element_type=jnp.float32)
    mid_normed, mid_invstd, mid_act = norm_forward(middle, midgain.astype(jnp.float32))
    hidden = jnp.dot(mid_act, ffn_up, preferred_element_type=jnp.float32)
    gated = smooth_gate(hidden).astype(jnp.bfloat16)
    output = middle + jnp.dot(gated, ffn_down, preferred_element_type=jnp.float32)
    saved = (pre_normed, pre_invstd, pre_act, query, keys, values, mixed, lse, mid_normed, mid_invstd, mid_act, hidden, gated)
    return (output, saved)

def layer_backward(grad, params, saved):
    pregain, attn_in, attn_out, midgain, ffn_up, ffn_down = params
    pre_normed, pre_invstd, pre_act, query, keys, values, mixed, lse, mid_normed, mid_invstd, mid_act, hidden, gated = saved
    grad_rounded = grad.astype(jnp.bfloat16)
    down_sum = jnp.dot(gated.T, grad_rounded, preferred_element_type=jnp.float32)
    gated_grad = jnp.dot(grad_rounded, ffn_down.T, preferred_element_type=jnp.float32)
    hidden_grad = gelu_back(hidden, gated_grad).astype(jnp.bfloat16)
    up_sum = jnp.dot(mid_act.T, hidden_grad, preferred_element_type=jnp.float32)
    mid_act_grad = jnp.dot(hidden_grad, ffn_up.T, preferred_element_type=jnp.float32)
    mid_back, midgain_sum = norm_backward(mid_act_grad, mid_normed, mid_invstd, midgain.astype(jnp.float32))
    mid_grad = grad + mid_back
    mid_rounded = mid_grad.astype(jnp.bfloat16)
    mixed_flat = mixed.reshape(-1, D)
    merge_sum = jnp.dot(mixed_flat.T, mid_rounded, preferred_element_type=jnp.float32)
    mixed_grad = jnp.dot(mid_rounded, attn_out.T, preferred_element_type=jnp.float32).astype(jnp.bfloat16)
    query_grad, key_grad, value_grad = attend_backward(query, keys, values, mixed, lse, split_heads(mixed_grad))
    qkv_grad = jnp.concatenate([query_grad.reshape(-1, D), key_grad.reshape(-1, D), value_grad.reshape(-1, D)], axis=1).astype(jnp.bfloat16)
    qkv_sum = jnp.dot(pre_act.T, qkv_grad, preferred_element_type=jnp.float32)
    pre_act_grad = jnp.dot(qkv_grad, attn_in.T, preferred_element_type=jnp.float32)
    pre_back, pregain_sum = norm_backward(pre_act_grad, pre_normed, pre_invstd, pregain.astype(jnp.float32))
    return (mid_grad + pre_back, (pregain_sum, qkv_sum, merge_sum, midgain_sum, up_sum, down_sum))

def adam_step(weight, grad, mean, square, rate, decay):
    mean_next = beta_one * mean + (1.0 - beta_one) * grad
    square_next = beta_two * square + (1.0 - beta_two) * grad * grad
    mean_hat = mean_next / (1.0 - beta_one ** step_count)
    square_hat = square_next / (1.0 - beta_two ** step_count)
    weight_next = weight - rate * (mean_hat / (jnp.sqrt(square_hat) + adam_eps) + decay * weight)
    return (weight_next, mean_next, square_next)

def learning_rates():
    return (0.2, 0.3 * D ** (-0.5), 0.3 * max(1, D // 256) ** (-0.5), 0.2, 0.3 * D ** (-0.5), 0.3 * FF ** (-0.5))

def reference(inputs, cotangent, prenorm, qkv_weight, merge_weight, midnorm, up_weight, down_weight, prenorm_mean, prenorm_square, qkv_mean, qkv_square, merge_mean, merge_square, midnorm_mean, midnorm_square, up_mean, up_square, down_mean, down_square):
    masters = (prenorm, qkv_weight, merge_weight, midnorm, up_weight, down_weight)
    means = (prenorm_mean, qkv_mean, merge_mean, midnorm_mean, up_mean, down_mean)
    squares = (prenorm_square, qkv_square, merge_square, midnorm_square, up_square, down_square)
    working = lax.optimization_barrier(tuple((master.astype(jnp.bfloat16) for master in masters)))

    def one_sequence(totals, pair):
        resid, grad = pair
        saves = []
        for layer in range(L):
            layer_params = tuple((param[layer] for param in working))
            resid, saved = layer_forward(resid, layer_params)
            saves.append(saved)
        layer_grads = [None] * L
        for layer in reversed(range(L)):
            layer_params = tuple((param[layer] for param in working))
            grad, layer_grads[layer] = layer_backward(grad, layer_params, saves[layer])
        totals = tuple((totals[index] + jnp.stack([layer_grads[layer][index] for layer in range(L)]) for index in range(6)))
        return (totals, (resid, grad))
    start = tuple((jnp.zeros(master.shape, jnp.float32) for master in masters))
    grads, outputs = lax.scan(one_sequence, start, (inputs, cotangent))
    block_output, input_grad = outputs
    rates = learning_rates()
    decays = (0.0, decay_rate, decay_rate, 0.0, decay_rate, decay_rate)
    stepped = [adam_step(masters[index], grads[index], means[index], squares[index], rates[index], decays[index]) for index in range(6)]
    return (block_output, input_grad, grads[0], grads[1], grads[2], grads[3], grads[4], grads[5], stepped[0][0], stepped[1][0], stepped[2][0], stepped[3][0], stepped[4][0], stepped[5][0], stepped[0][1], stepped[1][1], stepped[2][1], stepped[3][1], stepped[4][1], stepped[5][1], stepped[0][2], stepped[1][2], stepped[2][2], stepped[3][2], stepped[4][2], stepped[5][2])
```

```python
import jax
import jax.numpy as jnp
from jax import lax
from jax.sharding import PartitionSpec as P

H = 17
HD = 64
D = 1088
FF = 4352
PAIRS = 8
ROWS = 128
LEN = 1024

f32 = jnp.float32
bf16 = jnp.bfloat16

norm_eps = 1e-05
beta_one = 0.9
beta_two = 0.95
adam_eps = 1e-08
decay_rate = 0.1
step_count = 3.0

OWNERS = ("dp", "ctx")
TOKENS = ("ctx", "tensor")


def smooth_gate(values):
    return jax.nn.gelu(values, approximate=True)


def gelu_both(hidden, grad):
    value, pullback = jax.vjp(smooth_gate, hidden)
    return value, pullback(grad)[0]


def normalize(resid):
    center = resid - jnp.mean(resid, axis=-1, keepdims=True)
    invstd = lax.rsqrt(jnp.mean(center * center, axis=-1, keepdims=True) + norm_eps)
    return center * invstd, invstd


def normalize_back(scaled, normed, invstd):
    return invstd * (
        scaled
        - jnp.mean(scaled, axis=-1, keepdims=True)
        - normed * jnp.mean(scaled * normed, axis=-1, keepdims=True)
    )


def dot(left, right, dims):
    return lax.dot_general(left, right, (dims, ((), ())), preferred_element_type=f32)


def heads_of(flat):
    return jnp.transpose(flat.reshape(flat.shape[0], -1, HD), (1, 0, 2))


def flat_of(heads):
    return jnp.transpose(heads, (1, 0, 2)).reshape(heads.shape[1], -1)


def bdot(left, right, left_dim, right_dim):
    return lax.dot_general(
        left, right, (((left_dim,), (right_dim,)), ((0,), (0,))), preferred_element_type=f32
    )


def causal_scores(query, keys, first_row):
    score = bdot(query, keys, 2, 2) * HD ** (-0.5)
    shape = score.shape[1:]
    row_pos = first_row + lax.broadcasted_iota(jnp.int32, shape, 0)
    col_pos = lax.broadcasted_iota(jnp.int32, shape, 1)
    return jnp.where((col_pos <= row_pos)[None], score, -jnp.inf)


def attend_forward(query, keys, values, first_row):
    score = causal_scores(query, keys, first_row)
    top = jnp.max(score, axis=-1, keepdims=True)
    lse = top + jnp.log(jnp.sum(jnp.exp(score - top), axis=-1, keepdims=True))
    probs = jnp.exp(score - lse).astype(bf16)
    return bdot(probs, values, 2, 1).astype(bf16), lse


def attend_backward(query, keys, values, mixed, lse, grad, first_row):
    delta = jnp.sum(grad.astype(f32) * mixed.astype(f32), axis=-1, keepdims=True)
    probs = jnp.exp(causal_scores(query, keys, first_row) - lse)
    value_grad = bdot(probs.astype(bf16), grad, 1, 1)
    prob_grad = bdot(grad, values, 2, 2)
    score_grad = (probs * (prob_grad - delta) * HD ** (-0.5)).astype(bf16)
    query_grad = bdot(score_grad, keys, 2, 1)
    key_grad = bdot(score_grad, query, 1, 1)
    return query_grad.astype(bf16), key_grad.astype(bf16), value_grad.astype(bf16)


def exchange(values, axes):
    return lax.all_to_all(values, axes, 0, 0)


def adam_step(weight, grad, mean, square, rate, decay):
    mean_next = beta_one * mean + (1.0 - beta_one) * grad
    square_next = beta_two * square + (1.0 - beta_two) * grad * grad
    mean_hat = mean_next / (1.0 - beta_one**step_count)
    square_hat = square_next / (1.0 - beta_two**step_count)
    weight_next = weight - rate * (mean_hat / (jnp.sqrt(square_hat) + adam_eps) + decay * weight)
    return (weight_next, mean_next, square_next)


def learning_rates():
    return (
        0.2,
        0.3 * D ** (-0.5),
        0.3 * max(1, D // 256) ** (-0.5),
        0.2,
        0.3 * D ** (-0.5),
        0.3 * FF ** (-0.5),
    )


def body(
    inputs,
    cotangent,
    prenorm,
    qkv_weight,
    merge_weight,
    midnorm,
    up_weight,
    down_weight,
    prenorm_mean,
    prenorm_square,
    qkv_mean,
    qkv_square,
    merge_mean,
    merge_square,
    midnorm_mean,
    midnorm_square,
    up_mean,
    up_square,
    down_mean,
    down_square,
):
    means = (prenorm_mean, qkv_mean, merge_mean, midnorm_mean, up_mean, down_mean)
    squares = (prenorm_square, qkv_square, merge_square, midnorm_square, up_square, down_square)
    masters = (prenorm, qkv_weight, merge_weight, midnorm, up_weight, down_weight)
    shard = prenorm.shape[1]
    owners = D // shard
    tensor_at = lax.axis_index("tensor")
    group = lax.axis_index("ctx") * 4 + tensor_at
    first_row = group * ROWS

    pregain = prenorm[0].astype(bf16).astype(f32)[:, None]
    midgain = midnorm[0].astype(bf16).astype(f32)[:, None]
    qkv_work = qkv_weight[0].astype(bf16).astype(f32)
    up_work = up_weight[0].astype(bf16).astype(f32)
    qkv_scaled = (pregain * qkv_work).astype(bf16)
    up_scaled = (midgain * up_work).astype(bf16)
    merge_work = merge_weight[0].astype(bf16)
    down_work = jnp.transpose(down_weight[0]).astype(bf16)

    resid = inputs[0]
    pre_normed, pre_invstd = normalize(resid)
    rows_all = lax.all_gather(pre_normed.astype(bf16), TOKENS, axis=0, tiled=True)

    split = qkv_scaled.reshape(shard, 3, D)
    paired = split[:, :, : 2 * PAIRS * HD].reshape(shard, 3, 2, 4, 2 * HD)
    mine = lax.dynamic_index_in_dim(paired, tensor_at, axis=3, keepdims=False)
    shared = split[:, :, 2 * PAIRS * HD :].reshape(shard, 3 * HD)
    sends = jnp.concatenate(
        [
            jnp.transpose(mine, (2, 0, 1, 3)).reshape(2, shard, 6 * HD),
            jnp.broadcast_to(shared[None], (2, shard, 3 * HD)),
        ],
        axis=2,
    )
    width = 9 * HD
    sends = jnp.broadcast_to(sends[None], (owners // 2, 2, shard, width))
    head_weight = exchange(sends.reshape(owners, shard, width), OWNERS).reshape(D, width)

    others = lax.all_gather(
        jnp.concatenate([merge_work, up_scaled, down_work], axis=1), OWNERS, axis=0, tiled=True
    )
    merge_full = others[:, :D]
    up_full = others[:, D : 2 * D]
    down_full = others[:, 2 * D :]
    grad = cotangent[0]
    grad_rows = lax.all_gather(grad.astype(bf16), "tensor", axis=0, tiled=True)

    qkv = dot(rows_all, head_weight, ((1,), (0,))).astype(bf16)
    query = heads_of(qkv[:, : 2 * HD])
    keys = heads_of(qkv[:, 2 * HD : 4 * HD])
    values = heads_of(qkv[:, 4 * HD : 6 * HD])
    last_query = lax.dynamic_slice_in_dim(qkv[:, 6 * HD : 7 * HD], first_row, ROWS, 0)[None]
    last_keys = qkv[:, 7 * HD : 8 * HD][None]
    last_values = qkv[:, 8 * HD :][None]
    mixed, lse = attend_forward(query, keys, values, 0)
    last_mixed, last_lse = attend_forward(last_query, last_keys, last_values, first_row)
    arrived = exchange(flat_of(mixed).reshape(PAIRS, ROWS, 2 * HD), TOKENS)
    heads = jnp.concatenate(
        [jnp.transpose(arrived, (1, 0, 2)).reshape(ROWS, 2 * PAIRS * HD), last_mixed[0]], axis=1
    )

    middle = resid + dot(heads, merge_full, ((1,), (0,)))
    mid_normed, mid_invstd = normalize(middle)
    mid_rows = lax.all_gather(mid_normed.astype(bf16), "tensor", axis=0, tiled=True)

    hidden = dot(mid_rows, up_full, ((1,), (0,)))
    gated_grad = dot(grad_rows, down_full, ((1,), (0,)))
    gated, hidden_grad = gelu_both(hidden, gated_grad)
    gated = gated.astype(bf16)
    hidden_grad = hidden_grad.astype(bf16)
    mid_terms = dot(hidden_grad, up_full, ((1,), (1,))).astype(bf16)
    mid_scaled = jnp.sum(
        exchange(mid_terms.reshape(4, ROWS, D), "tensor").astype(f32), axis=0
    )
    out_terms = dot(gated, down_full, ((1,), (1,))).astype(bf16)
    output = middle + jnp.sum(
        exchange(out_terms.reshape(4, ROWS, D), "tensor").astype(f32), axis=0
    )
    up_terms = dot(mid_rows, hidden_grad, ((0,), (0,))).astype(bf16)
    down_terms = dot(grad_rows, gated, ((0,), (0,))).astype(bf16)
    ffn_sum = lax.psum_scatter(
        jnp.concatenate([up_terms, down_terms], axis=1).reshape(owners, shard, 2 * D),
        OWNERS,
        scatter_dimension=0,
    ).astype(f32)

    mid_grad = grad + normalize_back(mid_scaled, mid_normed, mid_invstd)
    mid_rounded = mid_grad.astype(bf16)
    heads_grad = dot(mid_rounded, merge_full, ((1,), (1,))).astype(bf16)
    merge_terms = dot(heads, mid_rounded, ((0,), (0,))).astype(bf16)
    merge_part = jnp.sum(
        exchange(merge_terms.reshape(owners, shard, D), OWNERS).astype(f32), axis=0
    )

    paired_grad = jnp.transpose(
        heads_grad[:, : 2 * PAIRS * HD].reshape(ROWS, PAIRS, 2 * HD), (1, 0, 2)
    )
    mixed_grad = heads_of(exchange(paired_grad, TOKENS).reshape(LEN, 2 * HD))
    last_grad = heads_grad[:, 2 * PAIRS * HD :][None]
    query_grad, key_grad, value_grad = attend_backward(
        query, keys, values, mixed, lse, mixed_grad, 0
    )
    last_query_grad, last_key_grad, last_value_grad = attend_backward(
        last_query, last_keys, last_values, last_mixed, last_lse, last_grad, first_row
    )
    last_placed = lax.dynamic_update_slice(
        jnp.zeros((LEN, HD), bf16), last_query_grad[0], (first_row, 0)
    )
    qkv_grad = jnp.concatenate(
        [
            flat_of(query_grad),
            flat_of(key_grad),
            flat_of(value_grad),
            last_placed,
            last_key_grad[0],
            last_value_grad[0],
        ],
        axis=1,
    )
    weight_terms = dot(rows_all, qkv_grad, ((0,), (0,))).astype(bf16)
    weight_part = jnp.sum(
        exchange(weight_terms.reshape(owners, shard, width), OWNERS)
        .astype(f32)
        .reshape(owners // 2, 2, shard, width),
        axis=0,
    )
    pre_terms = dot(qkv_grad, head_weight, ((1,), (1,))).astype(bf16)
    pre_scaled = jnp.sum(
        exchange(pre_terms.reshape(PAIRS, ROWS, D), TOKENS).astype(f32), axis=0
    )
    input_grad = mid_grad + normalize_back(pre_scaled, pre_normed, pre_invstd)

    up_sum = ffn_sum[:, :D]
    down_sum = ffn_sum[:, D:]
    midgain_part = jnp.sum(up_work * up_sum, axis=1)
    merge_parts = lax.all_gather(
        jnp.concatenate([merge_part, jnp.broadcast_to(midgain_part[:, None], (shard, 64))], axis=1),
        "tensor",
        axis=0,
    )
    merge_sum = jnp.sum(merge_parts[:, :, :D], axis=0)
    midgain_sum = jnp.sum(merge_parts[:, :, D], axis=0)
    qkv_parts = lax.all_gather(
        jnp.concatenate(
            [
                weight_part[0, :, : 6 * HD],
                weight_part[1, :, : 6 * HD],
                weight_part[0, :, 6 * HD :] + weight_part[1, :, 6 * HD :],
            ],
            axis=1,
        ),
        "tensor",
        axis=0,
    )
    pairs_sum = jnp.transpose(
        qkv_parts[:, :, : 12 * HD].reshape(4, shard, 2, 3, 2 * HD), (1, 3, 2, 0, 4)
    ).reshape(shard, 3, 2 * PAIRS * HD)
    last_sum = jnp.sum(qkv_parts[:, :, 12 * HD :], axis=0).reshape(shard, 3, HD)
    qkv_sum = jnp.concatenate([pairs_sum, last_sum], axis=2).reshape(shard, 3 * D)

    grads = [
        jnp.sum(qkv_work * qkv_sum, axis=1)[None],
        (pregain * qkv_sum)[None],
        merge_sum[None],
        midgain_sum[None],
        (midgain * up_sum)[None],
        jnp.transpose(down_sum)[None],
    ]
    rates = learning_rates()
    decays = (0.0, decay_rate, decay_rate, 0.0, decay_rate, decay_rate)
    stepped = [
        adam_step(
            masters[index], grads[index], means[index], squares[index], rates[index], decays[index]
        )
        for index in range(6)
    ]
    return (
        output[None],
        input_grad[None],
        *grads,
        *[step[0] for step in stepped],
        *[step[1] for step in stepped],
        *[step[2] for step in stepped],
    )


def solution(mesh):
    rows = P("dp", ("ctx", "tensor"), None)
    gain = P(None, ("dp", "ctx"))
    whole = P(None, ("dp", "ctx"), None)
    wide = P(None, ("dp", "ctx"), "tensor")
    tall = P(None, "tensor", ("dp", "ctx"))
    weights = (gain, whole, whole, gain, wide, tall)
    moments = tuple(spec for spec in weights for _ in range(2))
    return jax.shard_map(
        body,
        mesh=mesh,
        in_specs=(rows, rows) + weights + moments,
        out_specs=(rows, rows) + weights * 4,
        check_vma=False,
    )
```

```python
import jax
import jax.numpy as jnp
from jax import lax
from jax.experimental import pallas as pl
from jax.experimental.pallas import tpu as pltpu
from jax.sharding import PartitionSpec as P

H = 17
HD = 64
D = 1088
FF = 4352
PAIRS = 8
ROWS = 128
LEN = 1024

f32 = jnp.float32
bf16 = jnp.bfloat16

norm_eps = 1e-05
beta_one = 0.9
beta_two = 0.95
adam_eps = 1e-08
decay_rate = 0.1
step_count = 3.0

OWNERS = ("dp", "ctx")
TOKENS = ("ctx", "tensor")


def smooth_gate(values):
    return jax.nn.gelu(values, approximate=True)


def gelu_both(hidden, grad):
    value, pullback = jax.vjp(smooth_gate, hidden)
    return value, pullback(grad)[0]


def normalize(resid):
    center = resid - jnp.mean(resid, axis=-1, keepdims=True)
    invstd = lax.rsqrt(jnp.mean(center * center, axis=-1, keepdims=True) + norm_eps)
    return center * invstd, invstd


def normalize_back(scaled, normed, invstd):
    return invstd * (
        scaled
        - jnp.mean(scaled, axis=-1, keepdims=True)
        - normed * jnp.mean(scaled * normed, axis=-1, keepdims=True)
    )


def dot(left, right, dims):
    return lax.dot_general(left, right, (dims, ((), ())), preferred_element_type=f32)


def heads_of(flat):
    return jnp.transpose(flat.reshape(flat.shape[0], -1, HD), (1, 0, 2))


def flat_of(heads):
    return jnp.transpose(heads, (1, 0, 2)).reshape(heads.shape[1], -1)


def bdot(left, right, left_dim, right_dim):
    return lax.dot_general(
        left, right, (((left_dim,), (right_dim,)), ((0,), (0,))), preferred_element_type=f32
    )


def causal_scores(query, keys, first_row):
    score = bdot(query, keys, 2, 2) * HD ** (-0.5)
    shape = score.shape[1:]
    row_pos = first_row + lax.broadcasted_iota(jnp.int32, shape, 0)
    col_pos = lax.broadcasted_iota(jnp.int32, shape, 1)
    return jnp.where((col_pos <= row_pos)[None], score, -jnp.inf)


def attend_forward(query, keys, values, first_row):
    score = causal_scores(query, keys, first_row)
    top = jnp.max(score, axis=-1, keepdims=True)
    lse = top + jnp.log(jnp.sum(jnp.exp(score - top), axis=-1, keepdims=True))
    probs = jnp.exp(score - lse).astype(bf16)
    return bdot(probs, values, 2, 1).astype(bf16), lse


def attend_backward(query, keys, values, mixed, lse, grad, first_row):
    delta = jnp.sum(grad.astype(f32) * mixed.astype(f32), axis=-1, keepdims=True)
    probs = jnp.exp(causal_scores(query, keys, first_row) - lse)
    value_grad = bdot(probs.astype(bf16), grad, 1, 1)
    prob_grad = bdot(grad, values, 2, 2)
    score_grad = (probs * (prob_grad - delta) * HD ** (-0.5)).astype(bf16)
    query_grad = bdot(score_grad, keys, 2, 1)
    key_grad = bdot(score_grad, query, 1, 1)
    return query_grad.astype(bf16), key_grad.astype(bf16), value_grad.astype(bf16)


def exchange(values, axes):
    return lax.all_to_all(values, axes, 0, 0)


def shifted(values, axis, step):
    size = lax.axis_size(axis)
    return lax.ppermute(values, axis, [(at, (at + step) % size) for at in range(size)])


def swapped(values):
    return shifted(values, "ctx", 1)


def along_z(values, step):
    return lax.ppermute(
        values, "dp", [(at, (at // 4 + step) % 4 * 4 + at % 4) for at in range(16)]
    )


def along_x(values, step):
    return lax.ppermute(
        values, "dp", [(at, at // 4 * 4 + (at % 4 + step) % 4) for at in range(16)]
    )


def pick(values, index):
    return lax.dynamic_index_in_dim(values, index, axis=0, keepdims=False)


def gather_ring(values):
    return [values] + [shifted(values, "tensor", step) for step in (1, 2, 3)]


def placed(blocks, at):
    whole = jnp.zeros((4,) + blocks[0].shape, blocks[0].dtype)
    for step, block in enumerate(blocks):
        whole = lax.dynamic_update_index_in_dim(whole, block, (at - step) % 4, 0)
    return whole


def return_ring(blocks):
    total = blocks[0]
    for step in (1, 2, 3):
        total = total + shifted(blocks[step].astype(bf16), "tensor", -step).astype(f32)
    return total


def scatter_blocks(values, at, send):
    total = pick(values, at).astype(f32)
    for step in (1, 2, 3):
        total = total + send(pick(values, (at + step) % 4), step).astype(f32)
    return total


def owner_sum(terms):
    rows, columns = terms.shape[1:]
    core = lax.axis_index("ctx")
    place = lax.axis_index("dp")
    cut = jnp.swapaxes(terms.reshape(16, 2, rows, columns), 0, 1)
    part = pick(cut, core).astype(f32) + swapped(pick(cut, 1 - core)).astype(f32)
    part = scatter_blocks(
        part.astype(bf16).reshape(4, 4, rows, columns), place // 4, along_z
    )
    return scatter_blocks(part.astype(bf16), place % 4, along_x)


def ffn_terms_kernel(mid_ref, hidden_grad_ref, grad_ref, gated_ref, out_ref):
    rows = out_ref.shape[1] // 2
    up = jnp.dot(mid_ref[...], hidden_grad_ref[...], preferred_element_type=f32)
    down = jnp.dot(grad_ref[...], gated_ref[...], preferred_element_type=f32)
    for block in range(out_ref.shape[0]):
        cut = slice(block * rows, (block + 1) * rows)
        out_ref[block] = jnp.concatenate([up[cut], down[cut]], axis=0).astype(bf16)


def ffn_terms(mid_rows, hidden_grad, grad_rows, gated, owners, shard):
    steps = 4
    tokens, units = hidden_grad.shape
    tall = pl.BlockSpec((D // steps, tokens), lambda step: (step, 0))
    wide = pl.BlockSpec((tokens, units), lambda step: (0, 0))
    return pl.pallas_call(
        ffn_terms_kernel,
        grid=(steps,),
        in_specs=[tall, wide, tall, wide],
        out_specs=pl.BlockSpec((owners // steps, 2 * shard, units), lambda step: (step, 0, 0)),
        out_shape=jax.ShapeDtypeStruct((owners, 2 * shard, units), bf16),
        compiler_params=pltpu.CompilerParams(vmem_limit_bytes=48 * 2**20),
        cost_estimate=pl.CostEstimate(
            flops=4 * D * tokens * units, bytes_accessed=10 * 2**20, transcendentals=0
        ),
    )(mid_rows.T, hidden_grad, grad_rows.T, gated)


def adam_step(weight, grad, mean, square, rate, decay):
    mean_next = beta_one * mean + (1.0 - beta_one) * grad
    square_next = beta_two * square + (1.0 - beta_two) * grad * grad
    mean_hat = mean_next / (1.0 - beta_one**step_count)
    square_hat = square_next / (1.0 - beta_two**step_count)
    weight_next = weight - rate * (mean_hat / (jnp.sqrt(square_hat) + adam_eps) + decay * weight)
    return (weight_next, mean_next, square_next)


def learning_rates():
    return (
        0.2,
        0.3 * D ** (-0.5),
        0.3 * max(1, D // 256) ** (-0.5),
        0.2,
        0.3 * D ** (-0.5),
        0.3 * FF ** (-0.5),
    )


def body(
    inputs,
    cotangent,
    prenorm,
    qkv_weight,
    merge_weight,
    midnorm,
    up_weight,
    down_weight,
    prenorm_mean,
    prenorm_square,
    qkv_mean,
    qkv_square,
    merge_mean,
    merge_square,
    midnorm_mean,
    midnorm_square,
    up_mean,
    up_square,
    down_mean,
    down_square,
):
    means = (prenorm_mean, qkv_mean, merge_mean, midnorm_mean, up_mean, down_mean)
    squares = (prenorm_square, qkv_square, merge_square, midnorm_square, up_square, down_square)
    masters = (prenorm, qkv_weight, merge_weight, midnorm, up_weight, down_weight)
    shard = prenorm.shape[1]
    owners = D // shard
    tensor_at = lax.axis_index("tensor")
    core_at = lax.axis_index("ctx")
    group = core_at * 4 + tensor_at
    first_row = group * ROWS

    pregain = prenorm[0].astype(bf16).astype(f32)[:, None]
    midgain = midnorm[0].astype(bf16).astype(f32)[:, None]
    qkv_work = qkv_weight[0].astype(bf16).astype(f32)
    up_work = up_weight[0].astype(bf16).astype(f32)
    qkv_scaled = (pregain * qkv_work).astype(bf16)
    up_scaled = (midgain * up_work).astype(bf16)
    merge_work = merge_weight[0].astype(bf16)
    down_work = jnp.transpose(down_weight[0]).astype(bf16)

    resid = inputs[0]
    pre_normed, pre_invstd = normalize(resid)
    half = placed(gather_ring(pre_normed.astype(bf16)), tensor_at)
    rows_all = jnp.zeros((2,) + half.shape, bf16)
    rows_all = lax.dynamic_update_index_in_dim(rows_all, half, core_at, 0)
    rows_all = lax.dynamic_update_index_in_dim(rows_all, swapped(half), 1 - core_at, 0)
    rows_all = rows_all.reshape(LEN, D)

    split = qkv_scaled.reshape(shard, 3, D)
    paired = split[:, :, : 2 * PAIRS * HD].reshape(shard, 3, 2, 4, 2 * HD)
    mine = lax.dynamic_index_in_dim(paired, tensor_at, axis=3, keepdims=False)
    shared = split[:, :, 2 * PAIRS * HD :].reshape(shard, 3 * HD)
    sends = jnp.concatenate(
        [
            jnp.transpose(mine, (2, 0, 1, 3)).reshape(2, shard, 6 * HD),
            jnp.broadcast_to(shared[None], (2, shard, 3 * HD)),
        ],
        axis=2,
    )
    width = 9 * HD
    sends = jnp.broadcast_to(sends[None], (owners // 2, 2, shard, width))
    head_weight = exchange(sends.reshape(owners, shard, width), OWNERS).reshape(D, width)

    others = lax.all_gather(
        jnp.concatenate([merge_work, up_scaled, down_work], axis=1), OWNERS, axis=0, tiled=True
    )
    merge_full = others[:, :D]
    up_full = others[:, D : 2 * D]
    down_full = others[:, 2 * D :]
    grad = cotangent[0]
    grad_rows = jnp.concatenate(gather_ring(grad.astype(bf16)))

    qkv = dot(rows_all, head_weight, ((1,), (0,))).astype(bf16)
    query = heads_of(qkv[:, : 2 * HD])
    keys = heads_of(qkv[:, 2 * HD : 4 * HD])
    values = heads_of(qkv[:, 4 * HD : 6 * HD])
    last_query = lax.dynamic_slice_in_dim(qkv[:, 6 * HD : 7 * HD], first_row, ROWS, 0)[None]
    last_keys = qkv[:, 7 * HD : 8 * HD][None]
    last_values = qkv[:, 8 * HD :][None]
    mixed, lse = attend_forward(query, keys, values, 0)
    last_mixed, last_lse = attend_forward(last_query, last_keys, last_values, first_row)
    arrived = exchange(flat_of(mixed).reshape(PAIRS, ROWS, 2 * HD), TOKENS)
    heads = jnp.concatenate(
        [jnp.transpose(arrived, (1, 0, 2)).reshape(ROWS, 2 * PAIRS * HD), last_mixed[0]], axis=1
    )

    middle = resid + dot(heads, merge_full, ((1,), (0,)))
    mid_normed, mid_invstd = normalize(middle)
    mid_rows = jnp.concatenate(gather_ring(mid_normed.astype(bf16)))

    hidden = dot(mid_rows, up_full, ((1,), (0,)))
    gated_grad = dot(grad_rows, down_full, ((1,), (0,)))
    gated, hidden_grad = gelu_both(hidden, gated_grad)
    gated = gated.astype(bf16)
    hidden_grad = hidden_grad.astype(bf16)
    mid_terms = dot(hidden_grad, up_full, ((1,), (1,)))
    mid_scaled = return_ring(mid_terms.reshape(4, ROWS, D))
    out_terms = dot(gated, down_full, ((1,), (1,)))
    output = middle + return_ring(out_terms.reshape(4, ROWS, D))
    ffn_sum = lax.psum_scatter(
        ffn_terms(mid_rows, hidden_grad, grad_rows, gated, owners, shard),
        OWNERS,
        scatter_dimension=0,
    ).astype(f32)

    mid_grad = grad + normalize_back(mid_scaled, mid_normed, mid_invstd)
    mid_rounded = mid_grad.astype(bf16)
    heads_grad = dot(mid_rounded, merge_full, ((1,), (1,))).astype(bf16)
    merge_terms = dot(heads, mid_rounded, ((0,), (0,))).astype(bf16)
    merge_part = owner_sum(merge_terms.reshape(owners, shard, D))
    merge_sum = sum(gather_ring(merge_part))

    paired_grad = jnp.transpose(
        heads_grad[:, : 2 * PAIRS * HD].reshape(ROWS, PAIRS, 2 * HD), (1, 0, 2)
    )
    mixed_grad = heads_of(exchange(paired_grad, TOKENS).reshape(LEN, 2 * HD))
    last_grad = heads_grad[:, 2 * PAIRS * HD :][None]
    query_grad, key_grad, value_grad = attend_backward(
        query, keys, values, mixed, lse, mixed_grad, 0
    )
    last_query_grad, last_key_grad, last_value_grad = attend_backward(
        last_query, last_keys, last_values, last_mixed, last_lse, last_grad, first_row
    )
    last_placed = lax.dynamic_update_slice(
        jnp.zeros((LEN, HD), bf16), last_query_grad[0], (first_row, 0)
    )
    qkv_grad = jnp.concatenate(
        [
            flat_of(query_grad),
            flat_of(key_grad),
            flat_of(value_grad),
            last_placed,
            last_key_grad[0],
            last_value_grad[0],
        ],
        axis=1,
    )
    weight_terms = dot(rows_all, qkv_grad, ((0,), (0,))).astype(bf16)
    weight_part = jnp.sum(
        exchange(weight_terms.reshape(owners, shard, width), OWNERS)
        .astype(f32)
        .reshape(owners // 2, 2, shard, width),
        axis=0,
    )
    pre_terms = dot(qkv_grad, head_weight, ((1,), (1,))).astype(bf16)
    pre_cut = pre_terms.reshape(2, 4, ROWS, D)
    pre_half = pick(pre_cut, core_at).astype(f32) + swapped(pick(pre_cut, 1 - core_at)).astype(f32)
    pre_scaled = scatter_blocks(
        pre_half.astype(bf16), tensor_at, lambda block, step: shifted(block, "tensor", step)
    )
    input_grad = mid_grad + normalize_back(pre_scaled, pre_normed, pre_invstd)

    up_sum = ffn_sum[:shard]
    down_sum = ffn_sum[shard:]
    midgain_part = jnp.sum(up_work * up_sum, axis=1)
    parts = placed(
        gather_ring(
            jnp.concatenate(
                [
                    weight_part[0, :, : 6 * HD],
                    weight_part[1, :, : 6 * HD],
                    weight_part[0, :, 6 * HD :] + weight_part[1, :, 6 * HD :],
                    jnp.broadcast_to(midgain_part[:, None], (shard, HD)),
                ],
                axis=1,
            )
        ),
        tensor_at,
    )
    midgain_sum = jnp.sum(parts[:, :, 15 * HD], axis=0)
    qkv_parts = parts[:, :, : 15 * HD]
    pairs_sum = jnp.transpose(
        qkv_parts[:, :, : 12 * HD].reshape(4, shard, 2, 3, 2 * HD), (1, 3, 2, 0, 4)
    ).reshape(shard, 3, 2 * PAIRS * HD)
    last_sum = jnp.sum(qkv_parts[:, :, 12 * HD :], axis=0).reshape(shard, 3, HD)
    qkv_sum = jnp.concatenate([pairs_sum, last_sum], axis=2).reshape(shard, 3 * D)

    grads = [
        jnp.sum(qkv_work * qkv_sum, axis=1)[None],
        (pregain * qkv_sum)[None],
        merge_sum[None],
        midgain_sum[None],
        (midgain * up_sum)[None],
        jnp.transpose(down_sum)[None],
    ]
    rates = learning_rates()
    decays = (0.0, decay_rate, decay_rate, 0.0, decay_rate, decay_rate)
    stepped = [
        adam_step(
            masters[index], grads[index], means[index], squares[index], rates[index], decays[index]
        )
        for index in range(6)
    ]
    return (
        output[None],
        input_grad[None],
        *grads,
        *[step[0] for step in stepped],
        *[step[1] for step in stepped],
        *[step[2] for step in stepped],
    )


def solution(mesh):
    rows = P("dp", ("ctx", "tensor"), None)
    gain = P(None, ("dp", "ctx"))
    whole = P(None, ("dp", "ctx"), None)
    wide = P(None, ("dp", "ctx"), "tensor")
    tall = P(None, "tensor", ("dp", "ctx"))
    weights = (gain, whole, whole, gain, wide, tall)
    moments = tuple(spec for spec in weights for _ in range(2))
    return jax.shard_map(
        body,
        mesh=mesh,
        in_specs=(rows, rows) + weights + moments,
        out_specs=(rows, rows) + weights * 4,
        check_vma=False,
    )
```

```python
import jax
import jax.numpy as jnp
from jax import lax
from jax.experimental import pallas as pl
from jax.experimental.pallas import tpu as pltpu
from jax.sharding import PartitionSpec as P

H = 17
HD = 64
D = 1088
FF = 4352
PAIRS = 8
ROWS = 128
LEN = 1024

f32 = jnp.float32
bf16 = jnp.bfloat16

norm_eps = 1e-05
beta_one = 0.9
beta_two = 0.95
adam_eps = 1e-08
decay_rate = 0.1
step_count = 3.0

OWNERS = ("dp", "ctx")
TOKENS = ("ctx", "tensor")


def normalize(resid):
    center = resid - jnp.mean(resid, axis=-1, keepdims=True)
    invstd = lax.rsqrt(jnp.mean(center * center, axis=-1, keepdims=True) + norm_eps)
    return center * invstd, invstd


def normalize_back(scaled, normed, invstd):
    return invstd * (
        scaled
        - jnp.mean(scaled, axis=-1, keepdims=True)
        - normed * jnp.mean(scaled * normed, axis=-1, keepdims=True)
    )


def dot(left, right, dims):
    return lax.dot_general(left, right, (dims, ((), ())), preferred_element_type=f32)


def exchange(values, axes):
    return lax.all_to_all(values, axes, 0, 0)


def shifted(values, axis, step):
    size = lax.axis_size(axis)
    return lax.ppermute(values, axis, [(at, (at + step) % size) for at in range(size)])


def swapped(values):
    return shifted(values, "ctx", 1)


def along_z(values, step):
    return lax.ppermute(
        values, "dp", [(at, (at // 4 + step) % 4 * 4 + at % 4) for at in range(16)]
    )


def along_x(values, step):
    return lax.ppermute(
        values, "dp", [(at, at // 4 * 4 + (at % 4 + step) % 4) for at in range(16)]
    )


def pick(values, index):
    return lax.dynamic_index_in_dim(values, index, axis=0, keepdims=False)


def gather_ring(values):
    return [values] + [shifted(values, "tensor", step) for step in (1, 2, 3)]


def placed(blocks, at):
    return [lax.select_n((at - owner) % 4, *blocks) for owner in range(4)]


def return_ring(own, others):
    total = own
    for step in (1, 2, 3):
        total = total + shifted(others[step - 1], "tensor", -step).astype(f32)
    return total


def scatter_blocks(values, at, send):
    total = pick(values, at).astype(f32)
    for step in (1, 2, 3):
        total = total + send(pick(values, (at + step) % 4), step).astype(f32)
    return total


def owner_sum(own, sent):
    place = lax.axis_index("dp")
    part = (own.astype(f32) + swapped(sent).astype(f32)).astype(bf16)
    part = scatter_blocks(part.reshape((4, 4) + part.shape[1:]), place // 4, along_z)
    return scatter_blocks(part.astype(bf16), place % 4, along_x)


def mm(left, right):
    return lax.dot_general(left, right, (((1,), (0,)), ((), ())), preferred_element_type=f32)


def mm_nt(left, right):
    return lax.dot_general(left, right, (((1,), (1,)), ((), ())), preferred_element_type=f32)


def mm_tn(left, right):
    return lax.dot_general(left, right, (((0,), (0,)), ((), ())), preferred_element_type=f32)


TILE = 256
SCALE = HD ** (-0.5)
BIG = 2.0**100
params = pltpu.CompilerParams(vmem_limit_bytes=56 * 2**20)


def estimate(flops, size):
    return pl.CostEstimate(flops=flops, bytes_accessed=size, transcendentals=0)


def in_memory(count, scalar=False):
    specs = [pl.BlockSpec(memory_space=pltpu.VMEM)] * count
    return ([pl.BlockSpec(memory_space=pltpu.SMEM)] if scalar else []) + specs


def causal_mask(shape, first_row, first_col):
    row_pos = first_row + lax.broadcasted_iota(jnp.int32, shape, 0)
    col_pos = first_col + lax.broadcasted_iota(jnp.int32, shape, 1)
    return col_pos <= row_pos


def column(part, head):
    at = part * 2 * HD + head * HD
    return slice(at, at + HD)


LAST_Q, LAST_K, LAST_V = (slice(6 * HD + part * HD, 7 * HD + part * HD) for part in range(3))


def soften(scores, values):
    top = scores[0].max(axis=1, keepdims=True)
    for score in scores[1:]:
        top = jnp.maximum(top, score.max(axis=1, keepdims=True))
    raised = [jnp.exp(score - top) for score in scores]
    total = sum(part.sum(axis=1, keepdims=True) for part in raised)
    inverse = 1.0 / total
    mixed = sum(mm((part * inverse).astype(bf16), value) for part, value in zip(raised, values))
    return mixed.astype(bf16), top + jnp.log(total)


def attend_kernel(
    first_ref, rows_ref, weight_ref, qkv_ref, mixed_ref, lse_ref, last_mixed_ref, last_lse_ref
):
    for start in range(0, LEN, TILE):
        cut = slice(start, start + TILE)
        qkv_ref[cut] = mm(rows_ref[cut], weight_ref[...]).astype(bf16)
    keep = causal_mask((TILE, TILE), 0, 0)
    for start in range(0, LEN, TILE):
        cut = slice(start, start + TILE)
        mixes, sums = [], []
        for head in range(2):
            query = qkv_ref[cut, column(0, head)] * SCALE
            scores, values = [], []
            for other in range(0, start + TILE, TILE):
                key_cut = slice(other, other + TILE)
                score = mm_nt(query, qkv_ref[key_cut, column(1, head)])
                scores.append(jnp.where(keep, score, -BIG) if other == start else score)
                values.append(qkv_ref[key_cut, column(2, head)])
            mixed, lse = soften(scores, values)
            mixes.append(mixed)
            sums.append(lse)
        mixed_ref[cut] = jnp.concatenate(mixes, axis=1)
        lse_ref[cut] = jnp.concatenate(sums, axis=1)
    first = pl.multiple_of(first_ref[0], ROWS)
    query = qkv_ref[pl.ds(first, ROWS), LAST_Q] * SCALE
    score = mm_nt(query, qkv_ref[:, LAST_K])
    score = jnp.where(causal_mask((ROWS, LEN), first, 0), score, -BIG)
    mixed, lse = soften([score], [qkv_ref[:, LAST_V]])
    last_mixed_ref[...] = mixed
    last_lse_ref[...] = lse


def attend(first_row, rows_all, head_weight):
    width = head_weight.shape[1]
    return pl.pallas_call(
        attend_kernel,
        in_specs=in_memory(2, True),
        out_specs=in_memory(5),
        out_shape=[
            jax.ShapeDtypeStruct((LEN, width), bf16),
            jax.ShapeDtypeStruct((LEN, 2 * HD), bf16),
            jax.ShapeDtypeStruct((LEN, 2), f32),
            jax.ShapeDtypeStruct((ROWS, HD), bf16),
            jax.ShapeDtypeStruct((ROWS, 1), f32),
        ],
        compiler_params=params,
        cost_estimate=estimate(2 * 10**9, 8 * 2**20),
        name="attend",
    )(first_row, rows_all, head_weight)


def score_back(query, keys, values, grad, lse, delta, keep):
    score = mm_nt(query, keys)
    probs = jnp.exp((score if keep is None else jnp.where(keep, score, -BIG)) - lse)
    score_grad = probs * (mm_nt(grad, values) - delta)
    return probs.astype(bf16), score_grad.astype(bf16)


def attend_back_kernel(
    first_ref,
    rows_ref,
    qkv_ref,
    mixed_ref,
    lse_ref,
    grad_ref,
    last_mixed_ref,
    last_lse_ref,
    last_grad_ref,
    out_ref,
    terms_ref,
    query_sum,
    key_sum,
    value_sum,
):
    keep = causal_mask((TILE, TILE), 0, 0)
    for head in range(2):
        lanes = slice(head * HD, (head + 1) * HD)
        for start in range(0, LEN, TILE):
            cut = slice(start, start + TILE)
            query = qkv_ref[cut, column(0, head)]
            grad = grad_ref[cut, lanes]
            delta = jnp.sum(
                grad.astype(f32) * mixed_ref[cut, lanes].astype(f32), axis=1, keepdims=True
            )
            lse = lse_ref[cut, head : head + 1]
            query_grad = None
            for other in range(0, start + TILE, TILE):
                key_cut = slice(other, other + TILE)
                keys = qkv_ref[key_cut, column(1, head)]
                probs, score_grad = score_back(
                    query * SCALE,
                    keys,
                    qkv_ref[key_cut, column(2, head)],
                    grad,
                    lse,
                    delta,
                    keep if other == start else None,
                )
                value_term = mm_tn(probs, grad)
                key_term = mm_tn(score_grad, query)
                query_term = mm(score_grad, keys)
                query_grad = query_term if query_grad is None else query_grad + query_term
                if other == start:
                    value_sum[key_cut, lanes] = value_term
                    key_sum[key_cut, lanes] = key_term
                else:
                    value_sum[key_cut, lanes] += value_term
                    key_sum[key_cut, lanes] += key_term
            query_sum[cut, lanes] = query_grad
    pair = 2 * HD
    out_ref[:, :pair] = (query_sum[...] * SCALE).astype(bf16)
    out_ref[:, pair : 2 * pair] = (key_sum[...] * SCALE).astype(bf16)
    out_ref[:, 2 * pair : 3 * pair] = value_sum[...].astype(bf16)

    first = pl.multiple_of(first_ref[0], ROWS)
    query = qkv_ref[pl.ds(first, ROWS), LAST_Q]
    keys = qkv_ref[:, LAST_K]
    grad = last_grad_ref[...]
    delta = jnp.sum(
        grad.astype(f32) * last_mixed_ref[...].astype(f32), axis=1, keepdims=True
    )
    probs, score_grad = score_back(
        query * SCALE,
        keys,
        qkv_ref[:, LAST_V],
        grad,
        last_lse_ref[...],
        delta,
        causal_mask((ROWS, LEN), first, 0),
    )
    query_sum[:, :HD] = jnp.zeros((LEN, HD), f32)
    query_sum[pl.ds(first, ROWS), :HD] = mm(score_grad, keys)
    key_term = mm_tn(score_grad, query)
    out_ref[:, 3 * pair : 4 * pair] = (
        jnp.concatenate([query_sum[:, :HD], key_term], axis=1) * SCALE
    ).astype(bf16)
    out_ref[:, 4 * pair :] = mm_tn(probs, grad).astype(bf16)

    owners, shard = terms_ref.shape[:2]
    for start in range(0, owners, 8):
        terms = mm(rows_ref[start * shard : (start + 8) * shard], out_ref[...])
        for block in range(8):
            terms_ref[start + block] = terms[block * shard : (block + 1) * shard].astype(bf16)


def attend_back(first_row, rows_turned, qkv, mixed, lse, grad, last, owners, shard):
    width = qkv.shape[1]
    return pl.pallas_call(
        attend_back_kernel,
        in_specs=in_memory(8, True),
        out_specs=in_memory(2),
        out_shape=[
            jax.ShapeDtypeStruct((LEN, width), bf16),
            jax.ShapeDtypeStruct((owners, shard, width), bf16),
        ],
        scratch_shapes=[pltpu.VMEM((LEN, 2 * HD), f32)] * 3,
        compiler_params=params,
        cost_estimate=estimate(3 * 10**9, 10 * 2**20),
        name="attend_back",
    )(first_row, rows_turned, qkv, mixed, lse, grad, *last)


def pre_terms_kernel(core_ref, qkv_grad_ref, weight_ref, own_ref, sent_ref):
    half = LEN // 2
    core = core_ref[0]
    mine = pl.multiple_of(core * half, half)
    other = pl.multiple_of((1 - core) * half, half)
    sent_ref[...] = mm_nt(qkv_grad_ref[pl.ds(other, half)], weight_ref[...]).astype(bf16)
    own_ref[...] = mm_nt(qkv_grad_ref[pl.ds(mine, half)], weight_ref[...]).astype(bf16)


def pre_terms(core, qkv_grad, head_weight):
    half = jax.ShapeDtypeStruct((LEN // 2, D), bf16)
    return pl.pallas_call(
        pre_terms_kernel,
        in_specs=in_memory(2, True),
        out_specs=in_memory(2),
        out_shape=[half, half],
        compiler_params=params,
        cost_estimate=estimate(2 * LEN * D * 9 * HD, 5 * 2**20),
        name="pre_terms",
    )(core, qkv_grad, head_weight)


def split_out(terms, own_ref, *others):
    own_ref[...] = terms[:ROWS]
    for step, ref in enumerate(others):
        ref[...] = terms[(step + 1) * ROWS : (step + 2) * ROWS].astype(bf16)


def ffn_kernel(*refs):
    mids, grads, (up_ref, down_ref) = refs[:4], refs[4:8], refs[8:10]
    gated_ref, hidden_grad_ref = refs[10:12]
    outs, mid_all, grad_all = refs[12:16], refs[16], refs[17]
    for step in range(4):
        cut = slice(step * ROWS, (step + 1) * ROWS)
        mid_all[cut] = mids[step][...]
        grad_all[cut] = grads[step][...]
    slope = (2.0 / 3.141592653589793) ** 0.5
    for low, high in ((0, 256), (256, 512), (512, 768), (768, 1088)):
        units = slice(low, high)
        hidden = mm(mid_all[...], up_ref[:, units])
        gated_grad = mm(grad_all[...], down_ref[:, units])
        square = hidden * hidden
        bent = jnp.tanh(slope * hidden * (1.0 + 0.044715 * square))
        half = 0.5 * (1.0 + bent)
        gated_ref[:, units] = (hidden * half).astype(bf16)
        back = half + 0.5 * hidden * (1.0 - bent * bent) * (
            slope * (1.0 + 3.0 * 0.044715 * square)
        )
        hidden_grad_ref[:, units] = (gated_grad * back).astype(bf16)
    split_out(mm_nt(hidden_grad_ref[...], up_ref[...]), *outs)


def ffn(mids, grads, up_full, down_full):
    units = up_full.shape[1]
    tokens = 4 * ROWS
    block = jax.ShapeDtypeStruct((ROWS, D), bf16)
    wide = jax.ShapeDtypeStruct((tokens, units), bf16)
    return pl.pallas_call(
        ffn_kernel,
        in_specs=in_memory(10),
        out_specs=in_memory(6),
        out_shape=[wide, wide, jax.ShapeDtypeStruct((ROWS, D), f32), block, block, block],
        scratch_shapes=[pltpu.VMEM((tokens, D), bf16)] * 2,
        compiler_params=params,
        cost_estimate=estimate(6 * tokens * D * units, 10 * 2**20),
        name="ffn",
    )(*mids, *grads, up_full, down_full)


def ffn_out_kernel(gated_ref, down_ref, *outs):
    split_out(mm_nt(gated_ref[...], down_ref[...]), *outs)


def ffn_out(gated, down_full):
    block = jax.ShapeDtypeStruct((ROWS, D), bf16)
    return pl.pallas_call(
        ffn_out_kernel,
        in_specs=in_memory(2),
        out_specs=in_memory(4),
        out_shape=[jax.ShapeDtypeStruct((ROWS, D), f32), block, block, block],
        compiler_params=params,
        cost_estimate=estimate(2 * gated.shape[0] * gated.shape[1] * D, 5 * 2**20),
        name="ffn_out",
    )(gated, down_full)


def ffn_terms_kernel(mid_ref, hidden_grad_ref, grad_ref, gated_ref, out_ref):
    rows = out_ref.shape[1] // 2
    up = mm(mid_ref[...], hidden_grad_ref[...])
    down = mm(grad_ref[...], gated_ref[...])
    for block in range(out_ref.shape[0]):
        cut = slice(block * rows, (block + 1) * rows)
        out_ref[block] = jnp.concatenate([up[cut], down[cut]], axis=0).astype(bf16)


def ffn_terms(mid_turned, hidden_grad, grad_turned, gated, owners, shard):
    steps = 4
    tokens, units = hidden_grad.shape
    tall = pl.BlockSpec((D // steps, tokens), lambda step: (step, 0))
    wide = pl.BlockSpec((tokens, units), lambda step: (0, 0))
    return pl.pallas_call(
        ffn_terms_kernel,
        grid=(steps,),
        in_specs=[tall, wide, tall, wide],
        out_specs=pl.BlockSpec((owners // steps, 2 * shard, units), lambda step: (step, 0, 0)),
        out_shape=jax.ShapeDtypeStruct((owners, 2 * shard, units), bf16),
        compiler_params=params,
        cost_estimate=estimate(4 * D * tokens * units, 10 * 2**20),
        name="ffn_terms",
    )(mid_turned, hidden_grad, grad_turned, gated)


def merge_terms_kernel(core_ref, heads_ref, grad_ref, own_ref, sent_ref):
    first = core_ref[0] == 0
    pairs, rows = own_ref.shape[:2]
    for start in range(0, pairs, 4):
        terms = mm(heads_ref[start * 2 * rows : (start + 4) * 2 * rows], grad_ref[...])
        for pair in range(4):
            low = terms[pair * 2 * rows : pair * 2 * rows + rows]
            high = terms[pair * 2 * rows + rows : (pair + 1) * 2 * rows]
            own_ref[start + pair] = jnp.where(first, low, high).astype(bf16)
            sent_ref[start + pair] = jnp.where(first, high, low).astype(bf16)


def merge_terms(core, heads_turned, mid_rounded, owners, shard):
    blocks = jax.ShapeDtypeStruct((owners // 2, shard, D), bf16)
    return pl.pallas_call(
        merge_terms_kernel,
        in_specs=in_memory(2, True),
        out_specs=in_memory(2),
        out_shape=[blocks, blocks],
        compiler_params=params,
        cost_estimate=estimate(2 * D * D * ROWS, 3 * 2**20),
        name="merge_terms",
    )(core, heads_turned, mid_rounded)


def after(values, earlier):
    return lax.optimization_barrier((values, earlier))[0]


def adam_step(weight, grad, mean, square, rate, decay):
    mean_next = beta_one * mean + (1.0 - beta_one) * grad
    square_next = beta_two * square + (1.0 - beta_two) * grad * grad
    mean_hat = mean_next / (1.0 - beta_one**step_count)
    square_hat = square_next / (1.0 - beta_two**step_count)
    weight_next = weight - rate * (mean_hat / (jnp.sqrt(square_hat) + adam_eps) + decay * weight)
    return (weight_next, mean_next, square_next)


def learning_rates():
    return (
        0.2,
        0.3 * D ** (-0.5),
        0.3 * max(1, D // 256) ** (-0.5),
        0.2,
        0.3 * D ** (-0.5),
        0.3 * FF ** (-0.5),
    )


def body(
    inputs,
    cotangent,
    prenorm,
    qkv_weight,
    merge_weight,
    midnorm,
    up_weight,
    down_weight,
    prenorm_mean,
    prenorm_square,
    qkv_mean,
    qkv_square,
    merge_mean,
    merge_square,
    midnorm_mean,
    midnorm_square,
    up_mean,
    up_square,
    down_mean,
    down_square,
):
    means = (prenorm_mean, qkv_mean, merge_mean, midnorm_mean, up_mean, down_mean)
    squares = (prenorm_square, qkv_square, merge_square, midnorm_square, up_square, down_square)
    masters = (prenorm, qkv_weight, merge_weight, midnorm, up_weight, down_weight)
    shard = prenorm.shape[1]
    owners = D // shard
    tensor_at = lax.axis_index("tensor")
    core_at = lax.axis_index("ctx")
    group = core_at * 4 + tensor_at
    first_row = group * ROWS

    pregain = prenorm[0].astype(bf16).astype(f32)[:, None]
    midgain = midnorm[0].astype(bf16).astype(f32)[:, None]
    qkv_work = qkv_weight[0].astype(bf16).astype(f32)
    up_work = up_weight[0].astype(bf16).astype(f32)
    qkv_scaled = (pregain * qkv_work).astype(bf16)
    up_scaled = (midgain * up_work).astype(bf16)
    merge_work = merge_weight[0].astype(bf16)
    down_work = jnp.transpose(down_weight[0]).astype(bf16)

    core_one = core_at[None].astype(jnp.int32)
    first_one = first_row[None].astype(jnp.int32)

    split = qkv_scaled.reshape(shard, 3, D)
    paired = split[:, :, : 2 * PAIRS * HD].reshape(shard, 3, 2, 4, 2 * HD)
    mine = lax.dynamic_index_in_dim(paired, tensor_at, axis=3, keepdims=False)
    shared = split[:, :, 2 * PAIRS * HD :].reshape(shard, 3 * HD)
    sends = jnp.concatenate(
        [
            jnp.transpose(mine, (2, 0, 1, 3)).reshape(2, shard, 6 * HD),
            jnp.broadcast_to(shared[None], (2, shard, 3 * HD)),
        ],
        axis=2,
    )
    width = 9 * HD
    sends = jnp.broadcast_to(sends[None], (owners // 2, 2, shard, width))
    sends = sends.reshape(owners, shard, width)
    resid, grad, sends = lax.optimization_barrier((inputs[0], cotangent[0], sends))
    head_weight = exchange(sends, OWNERS).reshape(D, width)

    pre_normed, pre_invstd = normalize(resid)
    half = jnp.concatenate(placed(gather_ring(pre_normed.astype(bf16)), tensor_at))
    other = swapped(half)
    rows_all = jnp.concatenate(
        [lax.select_n(core_at, half, other), lax.select_n(core_at, other, half)]
    )

    others = lax.all_gather(
        jnp.concatenate([up_scaled, down_work, merge_work], axis=0), OWNERS, axis=0
    )
    merge_full = others[:, 2 * shard :].reshape(D, D)
    grad_blocks = gather_ring(after(grad, rows_all).astype(bf16))

    qkv, mixed, lse, last_mixed, last_lse = attend(first_one, rows_all, head_weight)
    arrived = exchange(mixed.reshape(PAIRS, ROWS, 2 * HD), TOKENS)
    heads = jnp.concatenate(
        [jnp.transpose(arrived, (1, 0, 2)).reshape(ROWS, 2 * PAIRS * HD), last_mixed], axis=1
    )

    middle = resid + dot(heads, merge_full, ((1,), (0,)))
    mid_normed, mid_invstd = normalize(middle)
    mid_own, others = lax.optimization_barrier((mid_normed.astype(bf16), others))
    mid_blocks = gather_ring(mid_own)
    up_full = others[:, :shard].reshape(D, D)
    down_full = others[:, shard : 2 * shard].reshape(D, D)

    gated, hidden_grad, mid_terms, *mid_sent = ffn(mid_blocks, grad_blocks, up_full, down_full)
    mid_scaled = return_ring(mid_terms, mid_sent)
    ffn_sum = lax.psum_scatter(
        ffn_terms(
            jnp.concatenate([block.T for block in mid_blocks], axis=1),
            hidden_grad,
            jnp.concatenate([block.T for block in grad_blocks], axis=1),
            gated,
            owners,
            shard,
        ),
        OWNERS,
        scatter_dimension=0,
    ).astype(f32)

    mid_grad = grad + normalize_back(mid_scaled, mid_normed, mid_invstd)
    mid_rounded = mid_grad.astype(bf16)
    heads_grad = dot(mid_rounded, merge_full, ((1,), (1,))).astype(bf16)
    paired_grad = jnp.transpose(
        heads_grad[:, : 2 * PAIRS * HD].reshape(ROWS, PAIRS, 2 * HD), (1, 0, 2)
    )
    mixed_grad = exchange(paired_grad, TOKENS).reshape(LEN, 2 * HD)
    last_grad = heads_grad[:, 2 * PAIRS * HD :]
    merge_part = owner_sum(
        *merge_terms(core_one, heads.T, after(mid_rounded, paired_grad), owners, shard)
    )
    merge_sum = sum(gather_ring(merge_part))
    out_terms, *out_sent = ffn_out(after(gated, paired_grad), down_full)
    output = middle + return_ring(out_terms, out_sent)

    qkv_grad, weight_terms = attend_back(
        first_one,
        rows_all.T,
        qkv,
        mixed,
        lse,
        mixed_grad,
        (last_mixed, last_lse, last_grad),
        owners,
        shard,
    )
    weight_part = jnp.sum(
        exchange(weight_terms, OWNERS).astype(f32).reshape(owners // 2, 2, shard, width), axis=0
    )
    pre_own, pre_sent = pre_terms(core_one, qkv_grad, head_weight)
    pre_half = (pre_own.astype(f32) + swapped(pre_sent).astype(f32)).astype(bf16)
    pre_scaled = scatter_blocks(
        pre_half.reshape(4, ROWS, D), tensor_at, lambda block, step: shifted(block, "tensor", step)
    )
    input_grad = mid_grad + normalize_back(pre_scaled, pre_normed, pre_invstd)

    up_sum = ffn_sum[:shard]
    down_sum = ffn_sum[shard:]
    midgain_part = jnp.sum(up_work * up_sum, axis=1)
    parts = jnp.stack(placed(
        gather_ring(
            jnp.concatenate(
                [
                    weight_part[0, :, : 6 * HD],
                    weight_part[1, :, : 6 * HD],
                    weight_part[0, :, 6 * HD :] + weight_part[1, :, 6 * HD :],
                    jnp.broadcast_to(midgain_part[:, None], (shard, HD)),
                ],
                axis=1,
            )
        ),
        tensor_at,
    ))
    midgain_sum = jnp.sum(parts[:, :, 15 * HD], axis=0)
    qkv_parts = parts[:, :, : 15 * HD]
    pairs_sum = jnp.transpose(
        qkv_parts[:, :, : 12 * HD].reshape(4, shard, 2, 3, 2 * HD), (1, 3, 2, 0, 4)
    ).reshape(shard, 3, 2 * PAIRS * HD)
    last_sum = jnp.sum(qkv_parts[:, :, 12 * HD :], axis=0).reshape(shard, 3, HD)
    qkv_sum = jnp.concatenate([pairs_sum, last_sum], axis=2).reshape(shard, 3 * D)

    grads = [
        jnp.sum(qkv_work * qkv_sum, axis=1)[None],
        (pregain * qkv_sum)[None],
        merge_sum[None],
        midgain_sum[None],
        (midgain * up_sum)[None],
        jnp.transpose(down_sum)[None],
    ]
    rates = learning_rates()
    decays = (0.0, decay_rate, decay_rate, 0.0, decay_rate, decay_rate)
    stepped = [
        adam_step(
            masters[index], grads[index], means[index], squares[index], rates[index], decays[index]
        )
        for index in range(6)
    ]
    return (
        output[None],
        input_grad[None],
        *grads,
        *[step[0] for step in stepped],
        *[step[1] for step in stepped],
        *[step[2] for step in stepped],
    )


def solution(mesh):
    rows = P("dp", ("ctx", "tensor"), None)
    gain = P(None, ("dp", "ctx"))
    whole = P(None, ("dp", "ctx"), None)
    wide = P(None, ("dp", "ctx"), "tensor")
    tall = P(None, "tensor", ("dp", "ctx"))
    weights = (gain, whole, whole, gain, wide, tall)
    moments = tuple(spec for spec in weights for _ in range(2))
    return jax.shard_map(
        body,
        mesh=mesh,
        in_specs=(rows, rows) + weights + moments,
        out_specs=(rows, rows) + weights * 4,
        check_vma=False,
    )
```

```python
import functools

import jax
import jax.numpy as jnp
from jax import lax
from jax.experimental import layout
from jax.experimental import pallas as pl
from jax.experimental.pallas import tpu as pltpu
from jax.sharding import PartitionSpec as P

H = 17
HD = 64
D = 1088
FF = 4352
PAIRS = 8
ROWS = 128
LEN = 1024

f32 = jnp.float32
bf16 = jnp.bfloat16

norm_eps = 1e-05
beta_one = 0.9
beta_two = 0.95
adam_eps = 1e-08
decay_rate = 0.1
step_count = 3.0

OWNERS = ("dp", "ctx")
TOKENS = ("ctx", "tensor")


def normalize(resid):
    center = resid - jnp.mean(resid, axis=-1, keepdims=True)
    invstd = lax.rsqrt(jnp.mean(center * center, axis=-1, keepdims=True) + norm_eps)
    return center * invstd, invstd


def normalize_back(scaled, normed, invstd):
    return invstd * (
        scaled
        - jnp.mean(scaled, axis=-1, keepdims=True)
        - normed * jnp.mean(scaled * normed, axis=-1, keepdims=True)
    )


def by_rows(values):
    return layout.with_layout_constraint(
        values, layout.Layout(major_to_minor=tuple(range(values.ndim)))
    )


def exchange(values, axes):
    return by_rows(lax.all_to_all(by_rows(values), axes, 0, 0))


def permuted(values, axis, pairs):
    return by_rows(lax.ppermute(by_rows(values), axis, pairs))


def shifted(values, axis, step):
    size = lax.axis_size(axis)
    return permuted(values, axis, [(at, (at + step) % size) for at in range(size)])


def swapped(values):
    return shifted(values, "ctx", 1)


def along_z(values, step):
    return permuted(
        values, "dp", [(at, (at // 4 + step) % 4 * 4 + at % 4) for at in range(16)]
    )


def along_x(values, step):
    return permuted(
        values, "dp", [(at, at // 4 * 4 + (at % 4 + step) % 4) for at in range(16)]
    )


def gather_ring(values):
    return [values] + [shifted(values, "tensor", step) for step in (1, 2, 3)]


def placed(blocks, at):
    return [lax.select_n((at - owner) % 4, *blocks) for owner in range(4)]


def return_ring(own, others):
    total = own
    for step in (1, 2, 3):
        total = total + shifted(others[step - 1], "tensor", -step).astype(f32)
    return total


def mm(left, right):
    return lax.dot_general(left, right, (((1,), (0,)), ((), ())), preferred_element_type=f32)


def mm_nt(left, right):
    return lax.dot_general(left, right, (((1,), (1,)), ((), ())), preferred_element_type=f32)


def mm_tn(left, right):
    return lax.dot_general(left, right, (((0,), (0,)), ((), ())), preferred_element_type=f32)


TILE = 256
SCALE = HD ** (-0.5)
BIG = 2.0**100
LANES = 1152


def padded(lead, rows):
    return jax.ShapeDtypeStruct((*lead, -(-rows // 8) * 8, LANES), bf16)


params = pltpu.CompilerParams(vmem_limit_bytes=56 * 2**20)


def estimate(flops, size):
    return pl.CostEstimate(flops=flops, bytes_accessed=size, transcendentals=0)


def in_memory(count, scalar=False):
    specs = [pl.BlockSpec(memory_space=pltpu.VMEM)] * count
    return ([pl.BlockSpec(memory_space=pltpu.SMEM)] if scalar else []) + specs


def causal_mask(shape, first_row, first_col):
    row_pos = first_row + lax.broadcasted_iota(jnp.int32, shape, 0)
    col_pos = first_col + lax.broadcasted_iota(jnp.int32, shape, 1)
    return col_pos <= row_pos


def column(part, head):
    at = part * 2 * HD + head * HD
    return slice(at, at + HD)


LAST_Q, LAST_K, LAST_V = (slice(6 * HD + part * HD, 7 * HD + part * HD) for part in range(3))


def soften(scores, values):
    top = scores[0].max(axis=1, keepdims=True)
    for score in scores[1:]:
        top = jnp.maximum(top, score.max(axis=1, keepdims=True))
    raised = [jnp.exp(score - top) for score in scores]
    total = sum(part.sum(axis=1, keepdims=True) for part in raised)
    inverse = 1.0 / total
    mixed = sum(mm((part * inverse).astype(bf16), value) for part, value in zip(raised, values))
    return mixed.astype(bf16), top + jnp.log(total)


def attend_kernel(place_ref, *refs):
    blocks, weight_ref, rows_ref, qkv_ref, mixed_ref, lse_ref = refs[:8], *refs[8:13]
    last_mixed_ref, last_lse_ref = refs[13:]
    core, tensor = place_ref[1], place_ref[2]
    for at, block in enumerate(blocks):
        half = core if at < 4 else 1 - core
        row = half * (4 * ROWS) + ((tensor - at) & 3) * ROWS
        rows_ref[pl.ds(pl.multiple_of(row, ROWS), ROWS)] = block[...]
    for start in range(0, LEN, TILE):
        cut = slice(start, start + TILE)
        qkv_ref[cut] = mm(rows_ref[cut], weight_ref[...]).astype(bf16)
    keep = causal_mask((TILE, TILE), 0, 0)
    for start in range(0, LEN, TILE):
        cut = slice(start, start + TILE)
        mixes, sums = [], []
        for head in range(2):
            query = qkv_ref[cut, column(0, head)] * SCALE
            scores, values = [], []
            for other in range(0, start + TILE, TILE):
                key_cut = slice(other, other + TILE)
                score = mm_nt(query, qkv_ref[key_cut, column(1, head)])
                scores.append(jnp.where(keep, score, -BIG) if other == start else score)
                values.append(qkv_ref[key_cut, column(2, head)])
            mixed, lse = soften(scores, values)
            mixes.append(mixed)
            sums.append(lse)
        mixed_ref[cut] = jnp.concatenate(mixes, axis=1)
        lse_ref[cut] = jnp.concatenate(sums, axis=1)
    first = pl.multiple_of(place_ref[0], ROWS)
    query = qkv_ref[pl.ds(first, ROWS), LAST_Q] * SCALE
    score = mm_nt(query, qkv_ref[:, LAST_K])
    score = jnp.where(causal_mask((ROWS, LEN), first, 0), score, -BIG)
    mixed, lse = soften([score], [qkv_ref[:, LAST_V]])
    last_mixed_ref[...] = mixed
    last_lse_ref[...] = lse


def attend(place, blocks, head_weight):
    width = head_weight.shape[1]
    return pl.pallas_call(
        attend_kernel,
        in_specs=in_memory(9, True),
        out_specs=in_memory(6),
        out_shape=[
            jax.ShapeDtypeStruct((LEN, D), bf16),
            jax.ShapeDtypeStruct((LEN, width), bf16),
            jax.ShapeDtypeStruct((LEN, 2 * HD), bf16),
            jax.ShapeDtypeStruct((LEN, 2), f32),
            jax.ShapeDtypeStruct((ROWS, HD), bf16),
            jax.ShapeDtypeStruct((ROWS, 1), f32),
        ],
        compiler_params=params,
        cost_estimate=estimate(2 * 10**9, 8 * 2**20),
        name="attend",
    )(place, *blocks, head_weight)


def score_back(query, keys, values, grad, lse, delta, keep):
    score = mm_nt(query, keys)
    probs = jnp.exp((score if keep is None else jnp.where(keep, score, -BIG)) - lse)
    score_grad = probs * (mm_nt(grad, values) - delta)
    return probs.astype(bf16), score_grad.astype(bf16)


def attend_back_kernel(
    first_ref,
    rows_ref,
    qkv_ref,
    mixed_ref,
    lse_ref,
    grad_ref,
    last_mixed_ref,
    last_lse_ref,
    last_grad_ref,
    out_ref,
    terms_ref,
    query_sum,
    key_sum,
    value_sum,
):
    keep = causal_mask((TILE, TILE), 0, 0)
    for head in range(2):
        lanes = slice(head * HD, (head + 1) * HD)
        for start in range(0, LEN, TILE):
            cut = slice(start, start + TILE)
            query = qkv_ref[cut, column(0, head)]
            grad = grad_ref[cut, lanes]
            delta = jnp.sum(
                grad.astype(f32) * mixed_ref[cut, lanes].astype(f32), axis=1, keepdims=True
            )
            lse = lse_ref[cut, head : head + 1]
            query_grad = None
            for other in range(0, start + TILE, TILE):
                key_cut = slice(other, other + TILE)
                keys = qkv_ref[key_cut, column(1, head)]
                probs, score_grad = score_back(
                    query * SCALE,
                    keys,
                    qkv_ref[key_cut, column(2, head)],
                    grad,
                    lse,
                    delta,
                    keep if other == start else None,
                )
                value_term = mm_tn(probs, grad)
                key_term = mm_tn(score_grad, query)
                query_term = mm(score_grad, keys)
                query_grad = query_term if query_grad is None else query_grad + query_term
                if other == start:
                    value_sum[key_cut, lanes] = value_term
                    key_sum[key_cut, lanes] = key_term
                else:
                    value_sum[key_cut, lanes] += value_term
                    key_sum[key_cut, lanes] += key_term
            query_sum[cut, lanes] = query_grad
    pair = 2 * HD
    out_ref[:, :pair] = (query_sum[...] * SCALE).astype(bf16)
    out_ref[:, pair : 2 * pair] = (key_sum[...] * SCALE).astype(bf16)
    out_ref[:, 2 * pair : 3 * pair] = value_sum[...].astype(bf16)

    first = pl.multiple_of(first_ref[0], ROWS)
    query = qkv_ref[pl.ds(first, ROWS), LAST_Q]
    keys = qkv_ref[:, LAST_K]
    grad = last_grad_ref[...]
    delta = jnp.sum(
        grad.astype(f32) * last_mixed_ref[...].astype(f32), axis=1, keepdims=True
    )
    probs, score_grad = score_back(
        query * SCALE,
        keys,
        qkv_ref[:, LAST_V],
        grad,
        last_lse_ref[...],
        delta,
        causal_mask((ROWS, LEN), first, 0),
    )
    query_sum[:, :HD] = jnp.zeros((LEN, HD), f32)
    query_sum[pl.ds(first, ROWS), :HD] = mm(score_grad, keys)
    key_term = mm_tn(score_grad, query)
    out_ref[:, 3 * pair : 4 * pair] = (
        jnp.concatenate([query_sum[:, :HD], key_term], axis=1) * SCALE
    ).astype(bf16)
    out_ref[:, 4 * pair :] = mm_tn(probs, grad).astype(bf16)

    owners, shard = terms_ref.shape[:2]
    for start in range(0, owners, 8):
        terms = mm(rows_ref[start * shard : (start + 8) * shard], out_ref[...])
        for block in range(8):
            terms_ref[start + block] = terms[block * shard : (block + 1) * shard].astype(bf16)


def attend_back(first_row, rows_turned, qkv, mixed, lse, grad, last, owners, shard):
    width = qkv.shape[1]
    return pl.pallas_call(
        attend_back_kernel,
        in_specs=in_memory(8, True),
        out_specs=in_memory(2),
        out_shape=[
            jax.ShapeDtypeStruct((LEN, width), bf16),
            jax.ShapeDtypeStruct((owners, shard, width), bf16),
        ],
        scratch_shapes=[pltpu.VMEM((LEN, 2 * HD), f32)] * 3,
        compiler_params=params,
        cost_estimate=estimate(3 * 10**9, 10 * 2**20),
        name="attend_back",
    )(first_row, rows_turned, qkv, mixed, lse, grad, *last)


def pre_terms_kernel(core_ref, qkv_grad_ref, weight_ref, own_ref, sent_ref):
    half = LEN // 2
    core = core_ref[0]
    mine = pl.multiple_of(core * half, half)
    other = pl.multiple_of((1 - core) * half, half)
    sent_ref[:, :D] = mm_nt(qkv_grad_ref[pl.ds(other, half)], weight_ref[...]).astype(bf16)
    own_ref[...] = mm_nt(qkv_grad_ref[pl.ds(mine, half)], weight_ref[...]).astype(bf16)


def pre_terms(core, qkv_grad, head_weight):
    half = jax.ShapeDtypeStruct((LEN // 2, D), bf16)
    return pl.pallas_call(
        pre_terms_kernel,
        in_specs=in_memory(2, True),
        out_specs=in_memory(2),
        out_shape=[half, padded((), LEN // 2)],
        compiler_params=params,
        cost_estimate=estimate(2 * LEN * D * 9 * HD, 5 * 2**20),
        name="pre_terms",
    )(core, qkv_grad, head_weight)


def split_out(terms, own_ref, *others):
    own_ref[...] = terms[:ROWS]
    for step, ref in enumerate(others):
        ref[...] = terms[(step + 1) * ROWS : (step + 2) * ROWS].astype(bf16)


def ffn_kernel(*refs):
    mids, grads, (up_ref, down_ref) = refs[:4], refs[4:8], refs[8:10]
    gated_ref, hidden_grad_ref = refs[10:12]
    outs, mid_all, grad_all = refs[12:16], refs[16], refs[17]
    for step in range(4):
        cut = slice(step * ROWS, (step + 1) * ROWS)
        mid_all[cut] = mids[step][...]
        grad_all[cut] = grads[step][...]
    slope = (2.0 / 3.141592653589793) ** 0.5
    for low, high in ((0, 256), (256, 512), (512, 768), (768, 1088)):
        units = slice(low, high)
        hidden = mm(mid_all[...], up_ref[:, units])
        gated_grad = mm(grad_all[...], down_ref[:, units])
        square = hidden * hidden
        bent = jnp.tanh(slope * hidden * (1.0 + 0.044715 * square))
        half = 0.5 * (1.0 + bent)
        gated_ref[:, units] = (hidden * half).astype(bf16)
        back = half + 0.5 * hidden * (1.0 - bent * bent) * (
            slope * (1.0 + 3.0 * 0.044715 * square)
        )
        hidden_grad_ref[:, units] = (gated_grad * back).astype(bf16)
    split_out(mm_nt(hidden_grad_ref[...], up_ref[...]), *outs)


def ffn(mids, grads, up_full, down_full):
    units = up_full.shape[1]
    tokens = 4 * ROWS
    block = jax.ShapeDtypeStruct((ROWS, D), bf16)
    wide = jax.ShapeDtypeStruct((tokens, units), bf16)
    return pl.pallas_call(
        ffn_kernel,
        in_specs=in_memory(10),
        out_specs=in_memory(6),
        out_shape=[wide, wide, jax.ShapeDtypeStruct((ROWS, D), f32), block, block, block],
        scratch_shapes=[pltpu.VMEM((tokens, D), bf16)] * 2,
        compiler_params=params,
        cost_estimate=estimate(6 * tokens * D * units, 10 * 2**20),
        name="ffn",
    )(*mids, *grads, up_full, down_full)


def ffn_out_kernel(gated_ref, down_ref, *outs):
    split_out(mm_nt(gated_ref[...], down_ref[...]), *outs)


def ffn_out(gated, down_full):
    block = jax.ShapeDtypeStruct((ROWS, D), bf16)
    return pl.pallas_call(
        ffn_out_kernel,
        in_specs=in_memory(2),
        out_specs=in_memory(4),
        out_shape=[jax.ShapeDtypeStruct((ROWS, D), f32), block, block, block],
        compiler_params=params,
        cost_estimate=estimate(2 * gated.shape[0] * gated.shape[1] * D, 5 * 2**20),
        name="ffn_out",
    )(gated, down_full)


def by_core(first, low, high, own_ref, sent_ref, at):
    rows = low.shape[0]
    own_ref[at, :rows, :D] = jnp.where(first, low, high).astype(bf16)
    sent_ref[at, :rows, :D] = jnp.where(first, high, low).astype(bf16)


def ffn_terms_kernel(
    rows, core_ref, mid_ref, hidden_grad_ref, grad_ref, gated_ref, own_ref, sent_ref
):
    first = core_ref[0] == 0
    up = mm(mid_ref[...], hidden_grad_ref[...])
    down = mm(grad_ref[...], gated_ref[...])
    for pair in range(own_ref.shape[0]):
        low, high = (
            jnp.concatenate([up[cut], down[cut]], axis=0)
            for cut in (
                slice(at * rows, (at + 1) * rows) for at in (2 * pair, 2 * pair + 1)
            )
        )
        by_core(first, low, high, own_ref, sent_ref, pair)


def ffn_terms(core, mid_turned, hidden_grad, grad_turned, gated, owners, shard):
    steps = 4
    tokens, units = hidden_grad.shape
    tall = pl.BlockSpec((D // steps, tokens), lambda step: (step, 0))
    wide = pl.BlockSpec((tokens, units), lambda step: (0, 0))
    blocks = padded((owners // 2,), 2 * shard)
    cut = pl.BlockSpec((owners // 2 // steps, *blocks.shape[1:]), lambda step: (step, 0, 0))
    return pl.pallas_call(
        functools.partial(ffn_terms_kernel, shard),
        grid=(steps,),
        in_specs=[pl.BlockSpec(memory_space=pltpu.SMEM), tall, wide, tall, wide],
        out_specs=[cut, cut],
        out_shape=[blocks, blocks],
        compiler_params=params,
        cost_estimate=estimate(4 * D * tokens * units, 10 * 2**20),
        name="ffn_terms",
    )(core, mid_turned, hidden_grad, grad_turned, gated)


def merge_terms_kernel(rows, core_ref, heads_ref, grad_ref, own_ref, sent_ref):
    first = core_ref[0] == 0
    pairs = own_ref.shape[0]
    for start in range(0, pairs, 4):
        terms = mm(heads_ref[start * 2 * rows : (start + 4) * 2 * rows], grad_ref[...])
        for pair in range(4):
            low = terms[pair * 2 * rows : pair * 2 * rows + rows]
            high = terms[pair * 2 * rows + rows : (pair + 1) * 2 * rows]
            by_core(first, low, high, own_ref, sent_ref, start + pair)


def merge_terms(core, heads_turned, mid_rounded, owners, shard):
    blocks = padded((owners // 2,), shard)
    return pl.pallas_call(
        functools.partial(merge_terms_kernel, shard),
        in_specs=in_memory(2, True),
        out_specs=in_memory(2),
        out_shape=[blocks, blocks],
        compiler_params=params,
        cost_estimate=estimate(2 * D * D * ROWS, 3 * 2**20),
        name="merge_terms",
    )(core, heads_turned, mid_rounded)


def join_kernel(blocks_ref, *outs):
    owners = blocks_ref.shape[0]
    rows = blocks_ref.shape[1] // len(outs)
    for at, ref in enumerate(outs):
        cut = slice(at * rows, (at + 1) * rows)
        ref[...] = jnp.concatenate([blocks_ref[owner, cut] for owner in range(owners)], axis=0)


def join(blocks, count):
    owners, rows, columns = blocks.shape
    steps = 4
    whole = jax.ShapeDtypeStruct((owners * rows // count, columns), bf16)
    return pl.pallas_call(
        join_kernel,
        grid=(steps,),
        in_specs=[pl.BlockSpec((owners // steps, rows, columns), lambda step: (step, 0, 0))],
        out_specs=[pl.BlockSpec((whole.shape[0] // steps, columns), lambda step: (step, 0))]
        * count,
        out_shape=[whole] * count,
        compiler_params=params,
        cost_estimate=estimate(0, 14 * 2**20),
        name="join",
    )(blocks)


def merge_norm_kernel(
    resid_ref, arrived_ref, last_ref, merge_ref, heads_ref, middle_ref, normed_ref, invstd_ref, act_ref
):
    heads_ref[...] = jnp.concatenate(
        [arrived_ref[group] for group in range(PAIRS)] + [last_ref[...]], axis=1
    )
    middle = resid_ref[...] + mm(heads_ref[...], merge_ref[...])
    normed, invstd = normalize(middle)
    middle_ref[...] = middle
    normed_ref[...] = normed
    invstd_ref[...] = invstd
    act_ref[...] = normed.astype(bf16)


def merge_norm(resid, arrived, last_mixed, merge_full):
    rows = jax.ShapeDtypeStruct((ROWS, D), f32)
    short = jax.ShapeDtypeStruct((ROWS, D), bf16)
    return pl.pallas_call(
        merge_norm_kernel,
        in_specs=in_memory(4),
        out_specs=in_memory(5),
        out_shape=[short, rows, rows, jax.ShapeDtypeStruct((ROWS, 1), f32), short],
        compiler_params=params,
        cost_estimate=estimate(2 * ROWS * D * D, 4 * 2**20),
        name="merge_norm",
    )(resid, arrived, last_mixed, merge_full)


def norm_back_kernel(
    grad_ref, own_ref, one_ref, two_ref, three_ref, normed_ref, invstd_ref, merge_ref,
    mid_grad_ref, rounded_ref, paired_ref, last_ref,
):
    scaled = own_ref[...]
    for ref in (one_ref, two_ref, three_ref):
        scaled = scaled + ref[...].astype(f32)
    mid_grad = grad_ref[...] + normalize_back(scaled, normed_ref[...], invstd_ref[...])
    mid_grad_ref[...] = mid_grad
    rounded_ref[...] = mid_grad.astype(bf16)
    heads_grad = mm_nt(rounded_ref[...], merge_ref[...]).astype(bf16)
    for group in range(PAIRS):
        paired_ref[group] = heads_grad[:, group * 2 * HD : (group + 1) * 2 * HD]
    last_ref[...] = heads_grad[:, PAIRS * 2 * HD :]


def norm_back(grad, own, received, normed, invstd, merge_full):
    return pl.pallas_call(
        norm_back_kernel,
        in_specs=in_memory(8),
        out_specs=in_memory(4),
        out_shape=[
            jax.ShapeDtypeStruct((ROWS, D), f32),
            jax.ShapeDtypeStruct((ROWS, D), bf16),
            jax.ShapeDtypeStruct((PAIRS, ROWS, 2 * HD), bf16),
            jax.ShapeDtypeStruct((ROWS, HD), bf16),
        ],
        compiler_params=params,
        cost_estimate=estimate(2 * ROWS * D * D, 5 * 2**20),
        name="norm_back",
    )(grad, own, *received, normed, invstd, merge_full)


def cut_kernel(rows, sizes, at_ref, *refs):
    addends, outs = refs[:-4], refs[-4:]

    def block(*index):
        parts, first = [], 0
        for count, size in zip(rows, sizes):
            cut = (*index, slice(0, count), slice(0, D))
            parts.append(sum(ref[cut].astype(f32) for ref in addends[first : first + size]))
            first += size
        return parts[0] if len(parts) == 1 else jnp.concatenate(parts, axis=0)

    for step, out in enumerate(outs):
        index = (at_ref[0] + step) & 3
        if len(out.shape) == 2:
            out[: sum(rows), :D] = block(index).astype(out.dtype)
        else:
            for inner in range(out.shape[0]):
                out[inner, : sum(rows), :D] = block(index, inner).astype(out.dtype)


def sum_and_cut(at, rows, *groups):
    addends = [array for group in groups for array in group]
    lead = addends[0].shape[1:-2]
    send = padded(lead, sum(rows))
    return pl.pallas_call(
        functools.partial(cut_kernel, rows, [len(group) for group in groups]),
        in_specs=in_memory(len(addends), True),
        out_specs=in_memory(4),
        out_shape=[jax.ShapeDtypeStruct((*lead, sum(rows), D), f32), send, send, send],
        compiler_params=params,
        cost_estimate=estimate(0, 4 * 2**20),
        name="sum_and_cut",
    )(at, *addends)


def after(values, earlier):
    return lax.optimization_barrier((values, earlier))[0]


def adam_step(weight, grad, mean, square, rate, decay):
    mean_next = beta_one * mean + (1.0 - beta_one) * grad
    square_next = beta_two * square + (1.0 - beta_two) * grad * grad
    mean_hat = mean_next / (1.0 - beta_one**step_count)
    square_hat = square_next / (1.0 - beta_two**step_count)
    weight_next = weight - rate * (mean_hat / (jnp.sqrt(square_hat) + adam_eps) + decay * weight)
    return (weight_next, mean_next, square_next)


def learning_rates():
    return (
        0.2,
        0.3 * D ** (-0.5),
        0.3 * max(1, D // 256) ** (-0.5),
        0.2,
        0.3 * D ** (-0.5),
        0.3 * FF ** (-0.5),
    )


def body(
    inputs,
    cotangent,
    prenorm,
    qkv_weight,
    merge_weight,
    midnorm,
    up_weight,
    down_weight,
    prenorm_mean,
    prenorm_square,
    qkv_mean,
    qkv_square,
    merge_mean,
    merge_square,
    midnorm_mean,
    midnorm_square,
    up_mean,
    up_square,
    down_mean,
    down_square,
):
    means = (prenorm_mean, qkv_mean, merge_mean, midnorm_mean, up_mean, down_mean)
    squares = (prenorm_square, qkv_square, merge_square, midnorm_square, up_square, down_square)
    masters = (prenorm, qkv_weight, merge_weight, midnorm, up_weight, down_weight)
    shard = prenorm.shape[1]
    owners = D // shard
    tensor_at = lax.axis_index("tensor")
    core_at = lax.axis_index("ctx")
    group = core_at * 4 + tensor_at
    first_row = group * ROWS

    pregain = prenorm[0].astype(bf16).astype(f32)[:, None]
    midgain = midnorm[0].astype(bf16).astype(f32)[:, None]
    qkv_work = qkv_weight[0].astype(bf16).astype(f32)
    up_work = up_weight[0].astype(bf16).astype(f32)
    qkv_scaled = (pregain * qkv_work).astype(bf16)
    up_scaled = (midgain * up_work).astype(bf16)
    merge_work = merge_weight[0].astype(bf16)
    down_work = jnp.transpose(down_weight[0]).astype(bf16)

    first_one = first_row[None].astype(jnp.int32)
    place_at = lax.axis_index("dp")
    core_one, tensor_one, z_one, x_one = (
        at[None].astype(jnp.int32) for at in (core_at, tensor_at, place_at // 4, place_at % 4)
    )
    place = jnp.stack([first_row, core_at, tensor_at]).astype(jnp.int32)

    split = qkv_scaled.reshape(shard, 3, D)
    paired = split[:, :, : 2 * PAIRS * HD].reshape(shard, 3, 2, 4, 2 * HD)
    mine = lax.dynamic_index_in_dim(paired, tensor_at, axis=3, keepdims=False)
    shared = split[:, :, 2 * PAIRS * HD :].reshape(shard, 3 * HD)
    sends = jnp.concatenate(
        [
            jnp.transpose(mine, (2, 0, 1, 3)).reshape(2, shard, 6 * HD),
            jnp.broadcast_to(shared[None], (2, shard, 3 * HD)),
        ],
        axis=2,
    )
    width = 9 * HD
    sends = jnp.broadcast_to(sends[None], (owners // 2, 2, shard, width))
    sends = sends.reshape(owners, shard, width)
    resid, grad, sends = lax.optimization_barrier((inputs[0], cotangent[0], sends))
    head_weight = exchange(sends, OWNERS).reshape(D, width)

    pre_normed, pre_invstd = normalize(resid)
    pre_blocks = gather_ring(pre_normed.astype(bf16))
    other_blocks = [swapped(block) for block in pre_blocks]

    others = lax.all_gather(
        jnp.concatenate([up_scaled, down_work, merge_work], axis=0), OWNERS, axis=0
    )
    grad_blocks = gather_ring(after(grad, pre_blocks[3]).astype(bf16))

    rows_all, qkv, mixed, lse, last_mixed, last_lse = attend(
        place, pre_blocks + other_blocks, head_weight
    )
    arrived = exchange(mixed.reshape(PAIRS, ROWS, 2 * HD), TOKENS)
    up_full, down_full, merge_full = join(after(others, mixed), 3)
    heads, middle, mid_normed, mid_invstd, mid_own = merge_norm(
        resid, arrived, last_mixed, merge_full
    )
    mid_blocks = gather_ring(mid_own)

    gated, hidden_grad, mid_terms, *mid_sent = ffn(mid_blocks, grad_blocks, up_full, down_full)
    mid_received = [shifted(block, "tensor", -step - 1) for step, block in enumerate(mid_sent)]
    ffn_own, ffn_sent = ffn_terms(
        core_one,
        jnp.concatenate([block.T for block in mid_blocks], axis=1),
        hidden_grad,
        jnp.concatenate([block.T for block in grad_blocks], axis=1),
        gated,
        owners,
        shard,
    )
    ffn_other = swapped(ffn_sent)
    mid_grad, mid_rounded, paired_grad, last_grad = norm_back(
        grad, mid_terms, mid_received, mid_normed, mid_invstd, merge_full
    )
    mixed_grad = exchange(paired_grad, TOKENS).reshape(LEN, 2 * HD)
    merge_own, merge_sent = merge_terms(core_one, heads.T, mid_rounded, owners, shard)
    merge_other = swapped(merge_sent)

    qkv_grad, weight_terms = attend_back(
        first_one,
        rows_all.T,
        qkv,
        mixed,
        lse,
        mixed_grad,
        (last_mixed, last_lse, last_grad),
        owners,
        shard,
    )
    weight_part = jnp.sum(
        exchange(weight_terms, OWNERS).astype(f32).reshape(owners // 2, 2, shard, width), axis=0
    )

    def on_grid(values):
        return values.reshape((4, 4) + values.shape[1:])

    part, *sent = sum_and_cut(
        z_one,
        (2 * shard, shard),
        (on_grid(ffn_own), on_grid(ffn_other)),
        (on_grid(merge_own), on_grid(merge_other)),
    )
    received = [along_z(block, step + 1) for step, block in enumerate(sent)]
    pre_own, pre_sent = pre_terms(core_one, after(qkv_grad, part), head_weight)
    pre_other = swapped(pre_sent)
    out_terms, *out_sent = ffn_out(after(gated, pre_own), down_full)
    pre_scaled, *pre_sent = sum_and_cut(
        tensor_one, (ROWS,), (pre_own.reshape(4, ROWS, D), pre_other.reshape(4, ROWS, LANES))
    )
    for step, block in enumerate(pre_sent):
        pre_scaled = pre_scaled + shifted(block, "tensor", step + 1)[:, :D].astype(f32)
    part, *sent = sum_and_cut(x_one, (3 * shard,), (part, *received))
    owner_part = part + sum(
        along_x(block, step + 1)[: 3 * shard, :D].astype(f32) for step, block in enumerate(sent)
    )
    output = middle + return_ring(out_terms, out_sent)
    input_grad = mid_grad + normalize_back(pre_scaled, pre_normed, pre_invstd)

    up_sum = owner_part[:shard]
    down_sum = owner_part[shard : 2 * shard]
    midgain_part = jnp.sum(up_work * up_sum, axis=1, keepdims=True)
    merge_sum = sum(
        gather_ring(
            jnp.concatenate(
                [owner_part[2 * shard :], jnp.broadcast_to(midgain_part, (shard, HD))], axis=1
            )
        )
    )
    midgain_sum = merge_sum[:, D]
    merge_sum = merge_sum[:, :D]
    parts = jnp.stack(
        placed(
            gather_ring(
                jnp.concatenate(
                    [
                        weight_part[0, :, : 6 * HD],
                        weight_part[1, :, : 6 * HD],
                        weight_part[0, :, 6 * HD :] + weight_part[1, :, 6 * HD :],
                    ],
                    axis=1,
                )
            ),
            tensor_at,
        )
    )
    pairs_sum = jnp.transpose(
        parts[:, :, : 12 * HD].reshape(4, shard, 2, 3, 2 * HD), (1, 3, 2, 0, 4)
    ).reshape(shard, 3, 2 * PAIRS * HD)
    last_sum = jnp.sum(parts[:, :, 12 * HD :], axis=0).reshape(shard, 3, HD)
    qkv_sum = jnp.concatenate([pairs_sum, last_sum], axis=2).reshape(shard, 3 * D)

    grads = [
        jnp.sum(qkv_work * qkv_sum, axis=1)[None],
        (pregain * qkv_sum)[None],
        merge_sum[None],
        midgain_sum[None],
        (midgain * up_sum)[None],
        jnp.transpose(down_sum)[None],
    ]
    rates = learning_rates()
    decays = (0.0, decay_rate, decay_rate, 0.0, decay_rate, decay_rate)
    stepped = [
        adam_step(
            masters[index], grads[index], means[index], squares[index], rates[index], decays[index]
        )
        for index in range(6)
    ]
    return (
        output[None],
        input_grad[None],
        *grads,
        *[step[0] for step in stepped],
        *[step[1] for step in stepped],
        *[step[2] for step in stepped],
    )


def solution(mesh):
    rows = P("dp", ("ctx", "tensor"), None)
    gain = P(None, ("dp", "ctx"))
    whole = P(None, ("dp", "ctx"), None)
    wide = P(None, ("dp", "ctx"), "tensor")
    tall = P(None, "tensor", ("dp", "ctx"))
    weights = (gain, whole, whole, gain, wide, tall)
    moments = tuple(spec for spec in weights for _ in range(2))
    return jax.shard_map(
        body,
        mesh=mesh,
        in_specs=(rows, rows) + weights + moments,
        out_specs=(rows, rows) + weights * 4,
        check_vma=False,
    )
```

```python
import functools

import jax
import jax.numpy as jnp
from jax import lax
from jax.experimental import layout
from jax.experimental import pallas as pl
from jax.experimental.pallas import tpu as pltpu
from jax.sharding import PartitionSpec as P

H = 17
HD = 64
D = 1088
FF = 4352
PAIRS = 8
ROWS = 128
LEN = 1024

f32 = jnp.float32
bf16 = jnp.bfloat16

norm_eps = 1e-05
beta_one = 0.9
beta_two = 0.95
adam_eps = 1e-08
decay_rate = 0.1
step_count = 3.0

OWNERS = ("dp", "ctx")
TOKENS = ("ctx", "tensor")


def normalize(resid):
    center = resid - jnp.mean(resid, axis=-1, keepdims=True)
    invstd = lax.rsqrt(jnp.mean(center * center, axis=-1, keepdims=True) + norm_eps)
    return center * invstd, invstd


def normalize_back(scaled, normed, invstd):
    return invstd * (
        scaled
        - jnp.mean(scaled, axis=-1, keepdims=True)
        - normed * jnp.mean(scaled * normed, axis=-1, keepdims=True)
    )


def by_rows(values):
    return layout.with_layout_constraint(
        values, layout.Layout(major_to_minor=tuple(range(values.ndim)))
    )


def exchange(values, axes):
    return by_rows(lax.all_to_all(by_rows(values), axes, 0, 0))


def permuted(values, axis, pairs):
    return by_rows(lax.ppermute(by_rows(values), axis, pairs))


def shifted(values, axis, step):
    size = lax.axis_size(axis)
    return permuted(values, axis, [(at, (at + step) % size) for at in range(size)])


def swapped(values):
    return shifted(values, "ctx", 1)


def along_z(values, step):
    return permuted(
        values, "dp", [(at, (at // 4 + step) % 4 * 4 + at % 4) for at in range(16)]
    )


def along_x(values, step):
    return permuted(
        values, "dp", [(at, at // 4 * 4 + (at % 4 + step) % 4) for at in range(16)]
    )


def gather_ring(values):
    return [values] + [shifted(values, "tensor", step) for step in (1, 2, 3)]


def placed(blocks, at):
    return [lax.select_n((at - owner) % 4, *blocks) for owner in range(4)]


def return_ring(own, others):
    total = own
    for step in (1, 2, 3):
        total = total + shifted(others[step - 1], "tensor", -step).astype(f32)
    return total


def mm(left, right):
    return lax.dot_general(left, right, (((1,), (0,)), ((), ())), preferred_element_type=f32)


def mm_nt(left, right):
    return lax.dot_general(left, right, (((1,), (1,)), ((), ())), preferred_element_type=f32)


def mm_tn(left, right):
    return lax.dot_general(left, right, (((0,), (0,)), ((), ())), preferred_element_type=f32)


TILE = 256
SCALE = HD ** (-0.5)
BIG = 2.0**100
LANES = 1152


def padded(lead, rows):
    return jax.ShapeDtypeStruct((*lead, -(-rows // 8) * 8, LANES), bf16)


params = pltpu.CompilerParams(vmem_limit_bytes=56 * 2**20)


def estimate(flops, size):
    return pl.CostEstimate(flops=flops, bytes_accessed=size, transcendentals=0)


def in_memory(count, scalar=False):
    specs = [pl.BlockSpec(memory_space=pltpu.VMEM)] * count
    return ([pl.BlockSpec(memory_space=pltpu.SMEM)] if scalar else []) + specs


def causal_mask(shape, first_row, first_col):
    row_pos = first_row + lax.broadcasted_iota(jnp.int32, shape, 0)
    col_pos = first_col + lax.broadcasted_iota(jnp.int32, shape, 1)
    return col_pos <= row_pos


def column(part, head):
    at = part * 2 * HD + head * HD
    return slice(at, at + HD)


LAST_Q, LAST_K, LAST_V = (slice(6 * HD + part * HD, 7 * HD + part * HD) for part in range(3))


def soften(scores, values):
    top = scores[0].max(axis=1, keepdims=True)
    for score in scores[1:]:
        top = jnp.maximum(top, score.max(axis=1, keepdims=True))
    raised = [jnp.exp(score - top) for score in scores]
    total = sum(part.sum(axis=1, keepdims=True) for part in raised)
    inverse = 1.0 / total
    mixed = sum(mm((part * inverse).astype(bf16), value) for part, value in zip(raised, values))
    return mixed.astype(bf16), top + jnp.log(total)


def attend_kernel(place_ref, *refs):
    blocks, weight_ref, rows_ref, qkv_ref, mixed_ref, lse_ref = refs[:8], *refs[8:13]
    last_mixed_ref, last_lse_ref = refs[13:]
    core, tensor = place_ref[1], place_ref[2]
    for at, block in enumerate(blocks):
        half = core if at < 4 else 1 - core
        row = half * (4 * ROWS) + ((tensor - at) & 3) * ROWS
        rows_ref[pl.ds(pl.multiple_of(row, ROWS), ROWS)] = block[...]
    for start in range(0, LEN, TILE):
        cut = slice(start, start + TILE)
        qkv_ref[cut] = mm(rows_ref[cut], weight_ref[...]).astype(bf16)
    keep = causal_mask((TILE, TILE), 0, 0)
    for start in range(0, LEN, TILE):
        cut = slice(start, start + TILE)
        mixes, sums = [], []
        for head in range(2):
            query = qkv_ref[cut, column(0, head)] * SCALE
            scores, values = [], []
            for other in range(0, start + TILE, TILE):
                key_cut = slice(other, other + TILE)
                score = mm_nt(query, qkv_ref[key_cut, column(1, head)])
                scores.append(jnp.where(keep, score, -BIG) if other == start else score)
                values.append(qkv_ref[key_cut, column(2, head)])
            mixed, lse = soften(scores, values)
            mixes.append(mixed)
            sums.append(lse)
        mixed_ref[cut] = jnp.concatenate(mixes, axis=1)
        lse_ref[cut] = jnp.concatenate(sums, axis=1)
    first = pl.multiple_of(place_ref[0], ROWS)
    query = qkv_ref[pl.ds(first, ROWS), LAST_Q] * SCALE
    score = mm_nt(query, qkv_ref[:, LAST_K])
    score = jnp.where(causal_mask((ROWS, LEN), first, 0), score, -BIG)
    mixed, lse = soften([score], [qkv_ref[:, LAST_V]])
    last_mixed_ref[...] = mixed
    last_lse_ref[...] = lse


def attend(place, blocks, head_weight):
    width = head_weight.shape[1]
    return pl.pallas_call(
        attend_kernel,
        in_specs=in_memory(9, True),
        out_specs=in_memory(6),
        out_shape=[
            jax.ShapeDtypeStruct((LEN, D), bf16),
            jax.ShapeDtypeStruct((LEN, width), bf16),
            jax.ShapeDtypeStruct((LEN, 2 * HD), bf16),
            jax.ShapeDtypeStruct((LEN, 2), f32),
            jax.ShapeDtypeStruct((ROWS, HD), bf16),
            jax.ShapeDtypeStruct((ROWS, 1), f32),
        ],
        compiler_params=params,
        cost_estimate=estimate(2 * 10**9, 8 * 2**20),
        name="attend",
    )(place, *blocks, head_weight)


def score_back(query, keys, values, grad, lse, delta, keep):
    score = mm_nt(query, keys)
    probs = jnp.exp((score if keep is None else jnp.where(keep, score, -BIG)) - lse)
    score_grad = probs * (mm_nt(grad, values) - delta)
    return probs.astype(bf16), score_grad.astype(bf16)


def attend_back_kernel(
    first_ref,
    rows_ref,
    qkv_ref,
    mixed_ref,
    lse_ref,
    grad_ref,
    last_mixed_ref,
    last_lse_ref,
    last_grad_ref,
    out_ref,
    terms_ref,
    query_sum,
    key_sum,
    value_sum,
):
    keep = causal_mask((TILE, TILE), 0, 0)
    for head in range(2):
        lanes = slice(head * HD, (head + 1) * HD)
        for start in range(0, LEN, TILE):
            cut = slice(start, start + TILE)
            query = qkv_ref[cut, column(0, head)]
            grad = grad_ref[cut, lanes]
            delta = jnp.sum(
                grad.astype(f32) * mixed_ref[cut, lanes].astype(f32), axis=1, keepdims=True
            )
            lse = lse_ref[cut, head : head + 1]
            query_grad = None
            for other in range(0, start + TILE, TILE):
                key_cut = slice(other, other + TILE)
                keys = qkv_ref[key_cut, column(1, head)]
                probs, score_grad = score_back(
                    query * SCALE,
                    keys,
                    qkv_ref[key_cut, column(2, head)],
                    grad,
                    lse,
                    delta,
                    keep if other == start else None,
                )
                value_term = mm_tn(probs, grad)
                key_term = mm_tn(score_grad, query)
                query_term = mm(score_grad, keys)
                query_grad = query_term if query_grad is None else query_grad + query_term
                if other == start:
                    value_sum[key_cut, lanes] = value_term
                    key_sum[key_cut, lanes] = key_term
                else:
                    value_sum[key_cut, lanes] += value_term
                    key_sum[key_cut, lanes] += key_term
            query_sum[cut, lanes] = query_grad
    pair = 2 * HD
    out_ref[:, :pair] = (query_sum[...] * SCALE).astype(bf16)
    out_ref[:, pair : 2 * pair] = (key_sum[...] * SCALE).astype(bf16)
    out_ref[:, 2 * pair : 3 * pair] = value_sum[...].astype(bf16)

    first = pl.multiple_of(first_ref[0], ROWS)
    query = qkv_ref[pl.ds(first, ROWS), LAST_Q]
    keys = qkv_ref[:, LAST_K]
    grad = last_grad_ref[...]
    delta = jnp.sum(
        grad.astype(f32) * last_mixed_ref[...].astype(f32), axis=1, keepdims=True
    )
    probs, score_grad = score_back(
        query * SCALE,
        keys,
        qkv_ref[:, LAST_V],
        grad,
        last_lse_ref[...],
        delta,
        causal_mask((ROWS, LEN), first, 0),
    )
    query_sum[:, :HD] = jnp.zeros((LEN, HD), f32)
    query_sum[pl.ds(first, ROWS), :HD] = mm(score_grad, keys)
    key_term = mm_tn(score_grad, query)
    out_ref[:, 3 * pair : 4 * pair] = (
        jnp.concatenate([query_sum[:, :HD], key_term], axis=1) * SCALE
    ).astype(bf16)
    out_ref[:, 4 * pair :] = mm_tn(probs, grad).astype(bf16)

    owners, shard = terms_ref.shape[:2]
    for start in range(0, owners, 8):
        terms = mm(rows_ref[start * shard : (start + 8) * shard], out_ref[...])
        for block in range(8):
            terms_ref[start + block] = terms[block * shard : (block + 1) * shard].astype(bf16)


def attend_back(first_row, rows_turned, qkv, mixed, lse, grad, last, owners, shard):
    width = qkv.shape[1]
    return pl.pallas_call(
        attend_back_kernel,
        in_specs=in_memory(8, True),
        out_specs=in_memory(2),
        out_shape=[
            jax.ShapeDtypeStruct((LEN, width), bf16),
            jax.ShapeDtypeStruct((owners, shard, width), bf16),
        ],
        scratch_shapes=[pltpu.VMEM((LEN, 2 * HD), f32)] * 3,
        compiler_params=params,
        cost_estimate=estimate(3 * 10**9, 10 * 2**20),
        name="attend_back",
    )(first_row, rows_turned, qkv, mixed, lse, grad, *last)


def pre_terms_kernel(core_ref, qkv_grad_ref, weight_ref, own_ref, sent_ref):
    half = LEN // 2
    core = core_ref[0]
    mine = pl.multiple_of(core * half, half)
    other = pl.multiple_of((1 - core) * half, half)
    sent_ref[:, :D] = mm_nt(qkv_grad_ref[pl.ds(other, half)], weight_ref[...]).astype(bf16)
    own_ref[...] = mm_nt(qkv_grad_ref[pl.ds(mine, half)], weight_ref[...]).astype(bf16)


def pre_terms(core, qkv_grad, head_weight):
    half = jax.ShapeDtypeStruct((LEN // 2, D), bf16)
    return pl.pallas_call(
        pre_terms_kernel,
        in_specs=in_memory(2, True),
        out_specs=in_memory(2),
        out_shape=[half, padded((), LEN // 2)],
        compiler_params=params,
        cost_estimate=estimate(2 * LEN * D * 9 * HD, 5 * 2**20),
        name="pre_terms",
    )(core, qkv_grad, head_weight)


def split_out(terms, own_ref, *others):
    own_ref[...] = terms[:ROWS]
    for step, ref in enumerate(others):
        ref[...] = terms[(step + 1) * ROWS : (step + 2) * ROWS].astype(bf16)


def ffn_kernel(*refs):
    mids, grads, (up_ref, down_ref) = refs[:4], refs[4:8], refs[8:10]
    gated_ref, hidden_grad_ref = refs[10:12]
    outs, mid_all, grad_all = refs[12:16], refs[16], refs[17]
    for step in range(4):
        cut = slice(step * ROWS, (step + 1) * ROWS)
        mid_all[cut] = mids[step][...]
        grad_all[cut] = grads[step][...]
    slope = (2.0 / 3.141592653589793) ** 0.5
    for low, high in ((0, 256), (256, 512), (512, 768), (768, 1088)):
        units = slice(low, high)
        hidden = mm(mid_all[...], up_ref[:, units])
        gated_grad = mm(grad_all[...], down_ref[:, units])
        square = hidden * hidden
        bent = jnp.tanh(slope * hidden * (1.0 + 0.044715 * square))
        half = 0.5 * (1.0 + bent)
        gated_ref[:, units] = (hidden * half).astype(bf16)
        back = half + 0.5 * hidden * (1.0 - bent * bent) * (
            slope * (1.0 + 3.0 * 0.044715 * square)
        )
        hidden_grad_ref[:, units] = (gated_grad * back).astype(bf16)
    split_out(mm_nt(hidden_grad_ref[...], up_ref[...]), *outs)


def ffn(mids, grads, up_full, down_full):
    units = up_full.shape[1]
    tokens = 4 * ROWS
    block = jax.ShapeDtypeStruct((ROWS, D), bf16)
    wide = jax.ShapeDtypeStruct((tokens, units), bf16)
    return pl.pallas_call(
        ffn_kernel,
        in_specs=in_memory(10),
        out_specs=in_memory(6),
        out_shape=[wide, wide, jax.ShapeDtypeStruct((ROWS, D), f32), block, block, block],
        scratch_shapes=[pltpu.VMEM((tokens, D), bf16)] * 2,
        compiler_params=params,
        cost_estimate=estimate(6 * tokens * D * units, 10 * 2**20),
        name="ffn",
    )(*mids, *grads, up_full, down_full)


def ffn_out_kernel(gated_ref, down_ref, *outs):
    split_out(mm_nt(gated_ref[...], down_ref[...]), *outs)


def ffn_out(gated, down_full):
    block = jax.ShapeDtypeStruct((ROWS, D), bf16)
    return pl.pallas_call(
        ffn_out_kernel,
        in_specs=in_memory(2),
        out_specs=in_memory(4),
        out_shape=[jax.ShapeDtypeStruct((ROWS, D), f32), block, block, block],
        compiler_params=params,
        cost_estimate=estimate(2 * gated.shape[0] * gated.shape[1] * D, 5 * 2**20),
        name="ffn_out",
    )(gated, down_full)


def by_core(first, low, high, own_ref, sent_ref, at):
    rows = low.shape[0]
    own_ref[at, :rows, :D] = jnp.where(first, low, high).astype(bf16)
    sent_ref[at, :rows, :D] = jnp.where(first, high, low).astype(bf16)


def ffn_terms_kernel(
    rows, core_ref, mid_ref, hidden_grad_ref, grad_ref, gated_ref, own_ref, sent_ref
):
    first = core_ref[0] == 0
    up = mm(mid_ref[...], hidden_grad_ref[...])
    down = mm(grad_ref[...], gated_ref[...])
    for pair in range(own_ref.shape[0]):
        low, high = (
            jnp.concatenate([up[cut], down[cut]], axis=0)
            for cut in (
                slice(at * rows, (at + 1) * rows) for at in (2 * pair, 2 * pair + 1)
            )
        )
        by_core(first, low, high, own_ref, sent_ref, pair)


def ffn_terms(core, mid_turned, hidden_grad, grad_turned, gated, owners, shard):
    steps = 4
    tokens, units = hidden_grad.shape
    tall = pl.BlockSpec((D // steps, tokens), lambda step: (step, 0))
    wide = pl.BlockSpec((tokens, units), lambda step: (0, 0))
    blocks = padded((owners // 2,), 2 * shard)
    cut = pl.BlockSpec((owners // 2 // steps, *blocks.shape[1:]), lambda step: (step, 0, 0))
    return pl.pallas_call(
        functools.partial(ffn_terms_kernel, shard),
        grid=(steps,),
        in_specs=[pl.BlockSpec(memory_space=pltpu.SMEM), tall, wide, tall, wide],
        out_specs=[cut, cut],
        out_shape=[blocks, blocks],
        compiler_params=params,
        cost_estimate=estimate(4 * D * tokens * units, 10 * 2**20),
        name="ffn_terms",
    )(core, mid_turned, hidden_grad, grad_turned, gated)


def merge_terms_kernel(rows, core_ref, heads_ref, grad_ref, own_ref, sent_ref):
    first = core_ref[0] == 0
    pairs = own_ref.shape[0]
    for start in range(0, pairs, 4):
        terms = mm(heads_ref[start * 2 * rows : (start + 4) * 2 * rows], grad_ref[...])
        for pair in range(4):
            low = terms[pair * 2 * rows : pair * 2 * rows + rows]
            high = terms[pair * 2 * rows + rows : (pair + 1) * 2 * rows]
            at = start + pair
            by_core(first, low, high, own_ref, sent_ref, at % 4 * 4 + at // 4)


def merge_terms(core, heads_turned, mid_rounded, owners, shard):
    blocks = padded((owners // 2,), shard)
    return pl.pallas_call(
        functools.partial(merge_terms_kernel, shard),
        in_specs=in_memory(2, True),
        out_specs=in_memory(2),
        out_shape=[blocks, blocks],
        compiler_params=params,
        cost_estimate=estimate(2 * D * D * ROWS, 3 * 2**20),
        name="merge_terms",
    )(core, heads_turned, mid_rounded)


def join_kernel(blocks_ref, *outs):
    owners = blocks_ref.shape[0]
    rows = blocks_ref.shape[1] // len(outs)
    for at, ref in enumerate(outs):
        cut = slice(at * rows, (at + 1) * rows)
        ref[...] = jnp.concatenate([blocks_ref[owner, cut] for owner in range(owners)], axis=0)


def join(blocks, count):
    owners, rows, columns = blocks.shape
    steps = 4
    whole = jax.ShapeDtypeStruct((owners * rows // count, columns), bf16)
    return pl.pallas_call(
        join_kernel,
        grid=(steps,),
        in_specs=[pl.BlockSpec((owners // steps, rows, columns), lambda step: (step, 0, 0))],
        out_specs=[pl.BlockSpec((whole.shape[0] // steps, columns), lambda step: (step, 0))]
        * count,
        out_shape=[whole] * count,
        compiler_params=params,
        cost_estimate=estimate(0, 14 * 2**20),
        name="join",
    )(blocks)


def merge_norm_kernel(
    resid_ref, arrived_ref, last_ref, merge_ref, heads_ref, middle_ref, normed_ref, invstd_ref, act_ref
):
    heads_ref[...] = jnp.concatenate(
        [arrived_ref[group] for group in range(PAIRS)] + [last_ref[...]], axis=1
    )
    middle = resid_ref[...] + mm(heads_ref[...], merge_ref[...])
    normed, invstd = normalize(middle)
    middle_ref[...] = middle
    normed_ref[...] = normed
    invstd_ref[...] = invstd
    act_ref[...] = normed.astype(bf16)


def merge_norm(resid, arrived, last_mixed, merge_full):
    rows = jax.ShapeDtypeStruct((ROWS, D), f32)
    short = jax.ShapeDtypeStruct((ROWS, D), bf16)
    return pl.pallas_call(
        merge_norm_kernel,
        in_specs=in_memory(4),
        out_specs=in_memory(5),
        out_shape=[short, rows, rows, jax.ShapeDtypeStruct((ROWS, 1), f32), short],
        compiler_params=params,
        cost_estimate=estimate(2 * ROWS * D * D, 4 * 2**20),
        name="merge_norm",
    )(resid, arrived, last_mixed, merge_full)


def norm_back_kernel(
    grad_ref, own_ref, one_ref, two_ref, three_ref, normed_ref, invstd_ref, merge_ref,
    mid_grad_ref, rounded_ref, paired_ref, last_ref,
):
    scaled = own_ref[...]
    for ref in (one_ref, two_ref, three_ref):
        scaled = scaled + ref[...].astype(f32)
    mid_grad = grad_ref[...] + normalize_back(scaled, normed_ref[...], invstd_ref[...])
    mid_grad_ref[...] = mid_grad
    rounded_ref[...] = mid_grad.astype(bf16)
    heads_grad = mm_nt(rounded_ref[...], merge_ref[...]).astype(bf16)
    for group in range(PAIRS):
        paired_ref[group] = heads_grad[:, group * 2 * HD : (group + 1) * 2 * HD]
    last_ref[...] = heads_grad[:, PAIRS * 2 * HD :]


def norm_back(grad, own, received, normed, invstd, merge_full):
    return pl.pallas_call(
        norm_back_kernel,
        in_specs=in_memory(8),
        out_specs=in_memory(4),
        out_shape=[
            jax.ShapeDtypeStruct((ROWS, D), f32),
            jax.ShapeDtypeStruct((ROWS, D), bf16),
            jax.ShapeDtypeStruct((PAIRS, ROWS, 2 * HD), bf16),
            jax.ShapeDtypeStruct((ROWS, HD), bf16),
        ],
        compiler_params=params,
        cost_estimate=estimate(2 * ROWS * D * D, 5 * 2**20),
        name="norm_back",
    )(grad, own, *received, normed, invstd, merge_full)


def cut_kernel(rows, sizes, at_ref, *refs):
    addends, outs = refs[:-4], refs[-4:]

    def block(*index):
        parts, first = [], 0
        for count, size in zip(rows, sizes):
            cut = (*index, slice(0, count), slice(0, D))
            parts.append(sum(ref[cut].astype(f32) for ref in addends[first : first + size]))
            first += size
        return parts[0] if len(parts) == 1 else jnp.concatenate(parts, axis=0)

    for step, out in enumerate(outs):
        index = (at_ref[0] + step) & 3
        if len(out.shape) == 2:
            out[: sum(rows), :D] = block(index).astype(out.dtype)
        else:
            for inner in range(out.shape[0]):
                out[inner, : sum(rows), :D] = block(index, inner).astype(out.dtype)


def sum_and_cut(at, rows, *groups):
    addends = [array for group in groups for array in group]
    lead = addends[0].shape[1:-2]
    send = padded(lead, sum(rows))
    return pl.pallas_call(
        functools.partial(cut_kernel, rows, [len(group) for group in groups]),
        in_specs=in_memory(len(addends), True),
        out_specs=in_memory(4),
        out_shape=[jax.ShapeDtypeStruct((*lead, sum(rows), D), f32), send, send, send],
        compiler_params=params,
        cost_estimate=estimate(0, 4 * 2**20),
        name="sum_and_cut",
    )(at, *addends)


def after(values, earlier):
    return lax.optimization_barrier((values, earlier))[0]


def adam_step(weight, grad, mean, square, rate, decay):
    mean_next = beta_one * mean + (1.0 - beta_one) * grad
    square_next = beta_two * square + (1.0 - beta_two) * grad * grad
    mean_hat = mean_next / (1.0 - beta_one**step_count)
    square_hat = square_next / (1.0 - beta_two**step_count)
    weight_next = weight - rate * (mean_hat / (jnp.sqrt(square_hat) + adam_eps) + decay * weight)
    return (weight_next, mean_next, square_next)


def learning_rates():
    return (
        0.2,
        0.3 * D ** (-0.5),
        0.3 * max(1, D // 256) ** (-0.5),
        0.2,
        0.3 * D ** (-0.5),
        0.3 * FF ** (-0.5),
    )


def body(
    inputs,
    cotangent,
    prenorm,
    qkv_weight,
    merge_weight,
    midnorm,
    up_weight,
    down_weight,
    prenorm_mean,
    prenorm_square,
    qkv_mean,
    qkv_square,
    merge_mean,
    merge_square,
    midnorm_mean,
    midnorm_square,
    up_mean,
    up_square,
    down_mean,
    down_square,
):
    means = (prenorm_mean, qkv_mean, merge_mean, midnorm_mean, up_mean, down_mean)
    squares = (prenorm_square, qkv_square, merge_square, midnorm_square, up_square, down_square)
    masters = (prenorm, qkv_weight, merge_weight, midnorm, up_weight, down_weight)
    shard = prenorm.shape[1]
    owners = D // shard
    tensor_at = lax.axis_index("tensor")
    core_at = lax.axis_index("ctx")
    group = core_at * 4 + tensor_at
    first_row = group * ROWS

    pregain = prenorm[0].astype(bf16).astype(f32)[:, None]
    midgain = midnorm[0].astype(bf16).astype(f32)[:, None]
    qkv_work = qkv_weight[0].astype(bf16).astype(f32)
    up_work = up_weight[0].astype(bf16).astype(f32)
    qkv_scaled = (pregain * qkv_work).astype(bf16)
    up_scaled = (midgain * up_work).astype(bf16)
    merge_work = merge_weight[0].astype(bf16)
    down_work = jnp.transpose(down_weight[0]).astype(bf16)

    first_one = first_row[None].astype(jnp.int32)
    place_at = lax.axis_index("dp")
    core_one, tensor_one, z_one, x_one = (
        at[None].astype(jnp.int32) for at in (core_at, tensor_at, place_at // 4, place_at % 4)
    )
    place = jnp.stack([first_row, core_at, tensor_at]).astype(jnp.int32)

    split = qkv_scaled.reshape(shard, 3, D)
    paired = split[:, :, : 2 * PAIRS * HD].reshape(shard, 3, 2, 4, 2 * HD)
    mine = lax.dynamic_index_in_dim(paired, tensor_at, axis=3, keepdims=False)
    shared = split[:, :, 2 * PAIRS * HD :].reshape(shard, 3 * HD)
    sends = jnp.concatenate(
        [
            jnp.transpose(mine, (2, 0, 1, 3)).reshape(2, shard, 6 * HD),
            jnp.broadcast_to(shared[None], (2, shard, 3 * HD)),
        ],
        axis=2,
    )
    width = 9 * HD
    sends = jnp.broadcast_to(sends[None], (owners // 2, 2, shard, width))
    sends = sends.reshape(owners, shard, width)
    resid, grad, sends = lax.optimization_barrier((inputs[0], cotangent[0], sends))
    head_weight = exchange(sends, OWNERS).reshape(D, width)

    pre_normed, pre_invstd = normalize(resid)
    pre_blocks = gather_ring(pre_normed.astype(bf16))
    other_blocks = [swapped(block) for block in pre_blocks]

    others = lax.all_gather(
        jnp.concatenate([up_scaled, down_work, merge_work], axis=0), OWNERS, axis=0
    )
    grad_blocks = gather_ring(after(grad, pre_blocks[3]).astype(bf16))

    rows_all, qkv, mixed, lse, last_mixed, last_lse = attend(
        place, pre_blocks + other_blocks, head_weight
    )
    arrived = exchange(mixed.reshape(PAIRS, ROWS, 2 * HD), TOKENS)
    up_full, down_full, merge_full = join(after(others, mixed), 3)
    heads, middle, mid_normed, mid_invstd, mid_own = merge_norm(
        resid, arrived, last_mixed, merge_full
    )
    mid_blocks = gather_ring(mid_own)

    rows_turned = rows_all.T
    grad_blocks = after(grad_blocks, rows_turned)
    gated, hidden_grad, mid_terms, *mid_sent = ffn(mid_blocks, grad_blocks, up_full, down_full)
    mid_received = [shifted(block, "tensor", -step - 1) for step, block in enumerate(mid_sent)]
    ffn_own, ffn_sent = ffn_terms(
        core_one,
        jnp.concatenate([block.T for block in mid_blocks], axis=1),
        hidden_grad,
        jnp.concatenate([block.T for block in grad_blocks], axis=1),
        gated,
        owners,
        shard,
    )
    ffn_other = swapped(ffn_sent)
    mid_grad, mid_rounded, paired_grad, last_grad = norm_back(
        grad, mid_terms, mid_received, mid_normed, mid_invstd, merge_full
    )
    mixed_grad = exchange(paired_grad, TOKENS).reshape(LEN, 2 * HD)
    merge_own, merge_sent = merge_terms(core_one, heads.T, mid_rounded, owners, shard)
    merge_other = swapped(merge_sent)

    def on_grid(values):
        return values.reshape((4, 4) + values.shape[1:])

    ffn_part, *ffn_sent = sum_and_cut(
        z_one, (2 * shard,), (on_grid(ffn_own), on_grid(ffn_other))
    )
    ffn_received = [along_z(block, step + 1) for step, block in enumerate(ffn_sent)]

    qkv_grad, weight_terms = attend_back(
        first_one,
        rows_turned,
        qkv,
        mixed,
        lse,
        after(mixed_grad, (merge_sent, ffn_part)),
        (last_mixed, last_lse, last_grad),
        owners,
        shard,
    )
    weight_part = jnp.sum(
        exchange(weight_terms, OWNERS).astype(f32).reshape(owners // 2, 2, shard, width), axis=0
    )
    merge_part, *merge_sent = sum_and_cut(
        x_one, (shard,), (on_grid(after(merge_own, weight_terms)), on_grid(merge_other))
    )
    merge_received = [along_x(block, step + 1) for step, block in enumerate(merge_sent)]
    pre_own, pre_sent = pre_terms(core_one, after(qkv_grad, merge_part), head_weight)
    pre_other = swapped(pre_sent)
    out_terms, *out_sent = ffn_out(after(gated, pre_own), down_full)

    def last_stage(at, along, rows, part, received):
        part, *sent = sum_and_cut(at, (rows,), (part, *received))
        return part + sum(
            along(block, step + 1)[:rows, :D].astype(f32) for step, block in enumerate(sent)
        )

    ffn_sum = last_stage(x_one, along_x, 2 * shard, ffn_part, ffn_received)
    pre_scaled, *pre_sent = sum_and_cut(
        tensor_one, (ROWS,), (pre_own.reshape(4, ROWS, D), pre_other.reshape(4, ROWS, LANES))
    )
    for step, block in enumerate(pre_sent):
        pre_scaled = pre_scaled + shifted(block, "tensor", step + 1)[:, :D].astype(f32)
    merge_part = last_stage(z_one, along_z, shard, merge_part, merge_received)
    output = middle + return_ring(out_terms, out_sent)
    input_grad = mid_grad + normalize_back(pre_scaled, pre_normed, pre_invstd)

    up_sum = ffn_sum[:shard]
    down_sum = ffn_sum[shard:]
    midgain_part = jnp.sum(up_work * up_sum, axis=1, keepdims=True)
    merge_sum = sum(
        gather_ring(
            jnp.concatenate(
                [merge_part, jnp.broadcast_to(midgain_part, (shard, HD))], axis=1
            )
        )
    )
    midgain_sum = merge_sum[:, D]
    merge_sum = merge_sum[:, :D]
    parts = jnp.stack(
        placed(
            gather_ring(
                jnp.concatenate(
                    [
                        weight_part[0, :, : 6 * HD],
                        weight_part[1, :, : 6 * HD],
                        weight_part[0, :, 6 * HD :] + weight_part[1, :, 6 * HD :],
                    ],
                    axis=1,
                )
            ),
            tensor_at,
        )
    )
    pairs_sum = jnp.transpose(
        parts[:, :, : 12 * HD].reshape(4, shard, 2, 3, 2 * HD), (1, 3, 2, 0, 4)
    ).reshape(shard, 3, 2 * PAIRS * HD)
    last_sum = jnp.sum(parts[:, :, 12 * HD :], axis=0).reshape(shard, 3, HD)
    qkv_sum = jnp.concatenate([pairs_sum, last_sum], axis=2).reshape(shard, 3 * D)

    grads = [
        jnp.sum(qkv_work * qkv_sum, axis=1)[None],
        (pregain * qkv_sum)[None],
        merge_sum[None],
        midgain_sum[None],
        (midgain * up_sum)[None],
        jnp.transpose(down_sum)[None],
    ]
    grads = [
        layout.with_layout_constraint(grad, layout.Layout(major_to_minor=order))
        for grad, order in zip(
            grads, ((0, 1), (1, 0, 2), (1, 0, 2), (0, 1), (1, 0, 2), (2, 0, 1))
        )
    ]
    rates = learning_rates()
    decays = (0.0, decay_rate, decay_rate, 0.0, decay_rate, decay_rate)
    stepped = [
        adam_step(
            masters[index], grads[index], means[index], squares[index], rates[index], decays[index]
        )
        for index in range(6)
    ]
    return (
        output[None],
        input_grad[None],
        *grads,
        *[step[0] for step in stepped],
        *[step[1] for step in stepped],
        *[step[2] for step in stepped],
    )


def solution(mesh):
    rows = P("dp", ("ctx", "tensor"), None)
    gain = P(None, ("dp", "ctx"))
    whole = P(None, ("dp", "ctx"), None)
    wide = P(None, ("dp", "ctx"), "tensor")
    tall = P(None, "tensor", ("dp", "ctx"))
    weights = (gain, whole, whole, gain, wide, tall)
    moments = tuple(spec for spec in weights for _ in range(2))
    return jax.shard_map(
        body,
        mesh=mesh,
        in_specs=(rows, rows) + weights + moments,
        out_specs=(rows, rows) + weights * 4,
        check_vma=False,
    )
```

```python
import functools

import jax
import jax.numpy as jnp
from jax import lax
from jax.experimental import layout
from jax.experimental import pallas as pl
from jax.experimental.pallas import tpu as pltpu
from jax.sharding import PartitionSpec as P

H = 17
HD = 64
D = 1088
FF = 4352
PAIRS = 8
ROWS = 128
LEN = 1024

f32 = jnp.float32
bf16 = jnp.bfloat16

norm_eps = 1e-05
beta_one = 0.9
beta_two = 0.95
adam_eps = 1e-08
decay_rate = 0.1
step_count = 3.0

OWNERS = ("dp", "ctx")
TOKENS = ("ctx", "tensor")


def normalize(resid):
    center = resid - jnp.mean(resid, axis=-1, keepdims=True)
    invstd = lax.rsqrt(jnp.mean(center * center, axis=-1, keepdims=True) + norm_eps)
    return center * invstd, invstd


def normalize_back(scaled, normed, invstd):
    return invstd * (
        scaled
        - jnp.mean(scaled, axis=-1, keepdims=True)
        - normed * jnp.mean(scaled * normed, axis=-1, keepdims=True)
    )


def by_rows(values):
    return layout.with_layout_constraint(
        values, layout.Layout(major_to_minor=tuple(range(values.ndim)))
    )


def exchange(values, axes):
    return by_rows(lax.all_to_all(by_rows(values), axes, 0, 0))


def permuted(values, axis, pairs):
    return by_rows(lax.ppermute(by_rows(values), axis, pairs))


def shifted(values, axis, step):
    size = lax.axis_size(axis)
    return permuted(values, axis, [(at, (at + step) % size) for at in range(size)])


def swapped(values):
    return shifted(values, "ctx", 1)


def along_z(values, step):
    return permuted(
        values, "dp", [(at, (at // 4 + step) % 4 * 4 + at % 4) for at in range(16)]
    )


def along_x(values, step):
    return permuted(
        values, "dp", [(at, at // 4 * 4 + (at % 4 + step) % 4) for at in range(16)]
    )


def gather_ring(values):
    return [values] + [shifted(values, "tensor", step) for step in (1, 2, 3)]


def placed(blocks, at):
    return [lax.select_n((at - owner) % 4, *blocks) for owner in range(4)]


def mm(left, right):
    return lax.dot_general(left, right, (((1,), (0,)), ((), ())), preferred_element_type=f32)


def mm_nt(left, right):
    return lax.dot_general(left, right, (((1,), (1,)), ((), ())), preferred_element_type=f32)


def mm_tn(left, right):
    return lax.dot_general(left, right, (((0,), (0,)), ((), ())), preferred_element_type=f32)


TILE = 256
SCALE = HD ** (-0.5)
BIG = 2.0**100
LANES = 1152


def padded(lead, rows):
    return jax.ShapeDtypeStruct((*lead, -(-rows // 8) * 8, LANES), bf16)


params = pltpu.CompilerParams(vmem_limit_bytes=56 * 2**20)


def estimate(flops, size):
    return pl.CostEstimate(flops=1, bytes_accessed=1, transcendentals=0)


def in_memory(count, scalar=False):
    specs = [pl.BlockSpec(memory_space=pltpu.VMEM)] * count
    return ([pl.BlockSpec(memory_space=pltpu.SMEM)] if scalar else []) + specs


def causal_mask(shape, first_row, first_col):
    row_pos = first_row + lax.broadcasted_iota(jnp.int32, shape, 0)
    col_pos = first_col + lax.broadcasted_iota(jnp.int32, shape, 1)
    return col_pos <= row_pos


def column(part, head):
    at = part * 2 * HD + head * HD
    return slice(at, at + HD)


LAST_Q, LAST_K, LAST_V = (slice(6 * HD + part * HD, 7 * HD + part * HD) for part in range(3))


def soften(scores, values):
    top = scores[0].max(axis=1, keepdims=True)
    for score in scores[1:]:
        top = jnp.maximum(top, score.max(axis=1, keepdims=True))
    raised = [jnp.exp(score - top) for score in scores]
    total = sum(part.sum(axis=1, keepdims=True) for part in raised)
    inverse = 1.0 / total
    mixed = sum(mm((part * inverse).astype(bf16), value) for part, value in zip(raised, values))
    return mixed.astype(bf16), top + jnp.log(total)


def attend_kernel(place_ref, *refs):
    blocks, weight_ref, rows_ref, qkv_ref, mixed_ref, lse_ref = refs[:8], *refs[8:13]
    last_mixed_ref, last_lse_ref = refs[13:]
    core, tensor = place_ref[1], place_ref[2]
    for at, block in enumerate(blocks):
        half = core if at < 4 else 1 - core
        row = half * (4 * ROWS) + ((tensor - at) & 3) * ROWS
        rows_ref[pl.ds(pl.multiple_of(row, ROWS), ROWS)] = block[...]
    for start in range(0, LEN, TILE):
        cut = slice(start, start + TILE)
        qkv_ref[cut] = mm(rows_ref[cut], weight_ref[...]).astype(bf16)
    keep = causal_mask((TILE, TILE), 0, 0)
    for start in range(0, LEN, TILE):
        cut = slice(start, start + TILE)
        mixes, sums = [], []
        for head in range(2):
            query = qkv_ref[cut, column(0, head)] * SCALE
            scores, values = [], []
            for other in range(0, start + TILE, TILE):
                key_cut = slice(other, other + TILE)
                score = mm_nt(query, qkv_ref[key_cut, column(1, head)])
                scores.append(jnp.where(keep, score, -BIG) if other == start else score)
                values.append(qkv_ref[key_cut, column(2, head)])
            mixed, lse = soften(scores, values)
            mixes.append(mixed)
            sums.append(lse)
        mixed_ref[cut] = jnp.concatenate(mixes, axis=1)
        lse_ref[cut] = jnp.concatenate(sums, axis=1)
    first = pl.multiple_of(place_ref[0], ROWS)
    query = qkv_ref[pl.ds(first, ROWS), LAST_Q] * SCALE
    score = mm_nt(query, qkv_ref[:, LAST_K])
    score = jnp.where(causal_mask((ROWS, LEN), first, 0), score, -BIG)
    mixed, lse = soften([score], [qkv_ref[:, LAST_V]])
    last_mixed_ref[...] = mixed
    last_lse_ref[...] = lse


def attend(place, blocks, head_weight):
    width = head_weight.shape[1]
    return pl.pallas_call(
        attend_kernel,
        in_specs=in_memory(9, True),
        out_specs=in_memory(6),
        out_shape=[
            jax.ShapeDtypeStruct((LEN, D), bf16),
            jax.ShapeDtypeStruct((LEN, width), bf16),
            jax.ShapeDtypeStruct((LEN, 2 * HD), bf16),
            jax.ShapeDtypeStruct((LEN, 2), f32),
            jax.ShapeDtypeStruct((ROWS, HD), bf16),
            jax.ShapeDtypeStruct((ROWS, 1), f32),
        ],
        compiler_params=params,
        cost_estimate=estimate(2 * 10**9, 8 * 2**20),
        name="attend",
    )(place, *blocks, head_weight)


def score_back(query, keys, values, grad, lse, delta, keep):
    score = mm_nt(query, keys)
    probs = jnp.exp((score if keep is None else jnp.where(keep, score, -BIG)) - lse)
    score_grad = probs * (mm_nt(grad, values) - delta)
    return probs.astype(bf16), score_grad.astype(bf16)


def attend_back_kernel(
    first_ref,
    rows_ref,
    qkv_ref,
    mixed_ref,
    lse_ref,
    grad_ref,
    last_mixed_ref,
    last_lse_ref,
    last_grad_ref,
    out_ref,
    terms_ref,
    query_sum,
    key_sum,
    value_sum,
):
    keep = causal_mask((TILE, TILE), 0, 0)
    for head in range(2):
        lanes = slice(head * HD, (head + 1) * HD)
        for start in range(0, LEN, TILE):
            cut = slice(start, start + TILE)
            query = qkv_ref[cut, column(0, head)]
            grad = grad_ref[cut, lanes]
            delta = jnp.sum(
                grad.astype(f32) * mixed_ref[cut, lanes].astype(f32), axis=1, keepdims=True
            )
            lse = lse_ref[cut, head : head + 1]
            query_grad = None
            for other in range(0, start + TILE, TILE):
                key_cut = slice(other, other + TILE)
                keys = qkv_ref[key_cut, column(1, head)]
                probs, score_grad = score_back(
                    query * SCALE,
                    keys,
                    qkv_ref[key_cut, column(2, head)],
                    grad,
                    lse,
                    delta,
                    keep if other == start else None,
                )
                value_term = mm_tn(probs, grad)
                key_term = mm_tn(score_grad, query)
                query_term = mm(score_grad, keys)
                query_grad = query_term if query_grad is None else query_grad + query_term
                if other == start:
                    value_sum[key_cut, lanes] = value_term
                    key_sum[key_cut, lanes] = key_term
                else:
                    value_sum[key_cut, lanes] += value_term
                    key_sum[key_cut, lanes] += key_term
            query_sum[cut, lanes] = query_grad
    pair = 2 * HD
    out_ref[:, :pair] = (query_sum[...] * SCALE).astype(bf16)
    out_ref[:, pair : 2 * pair] = (key_sum[...] * SCALE).astype(bf16)
    out_ref[:, 2 * pair : 3 * pair] = value_sum[...].astype(bf16)

    first = pl.multiple_of(first_ref[0], ROWS)
    query = qkv_ref[pl.ds(first, ROWS), LAST_Q]
    keys = qkv_ref[:, LAST_K]
    grad = last_grad_ref[...]
    delta = jnp.sum(
        grad.astype(f32) * last_mixed_ref[...].astype(f32), axis=1, keepdims=True
    )
    probs, score_grad = score_back(
        query * SCALE,
        keys,
        qkv_ref[:, LAST_V],
        grad,
        last_lse_ref[...],
        delta,
        causal_mask((ROWS, LEN), first, 0),
    )
    query_sum[:, :HD] = jnp.zeros((LEN, HD), f32)
    query_sum[pl.ds(first, ROWS), :HD] = mm(score_grad, keys)
    key_term = mm_tn(score_grad, query)
    out_ref[:, 3 * pair : 4 * pair] = (
        jnp.concatenate([query_sum[:, :HD], key_term], axis=1) * SCALE
    ).astype(bf16)
    out_ref[:, 4 * pair :] = mm_tn(probs, grad).astype(bf16)

    owners, shard = terms_ref.shape[:2]
    for start in range(0, owners, 8):
        terms = mm(rows_ref[start * shard : (start + 8) * shard], out_ref[...])
        for block in range(8):
            terms_ref[start + block] = terms[block * shard : (block + 1) * shard].astype(bf16)


def attend_back(first_row, rows_turned, qkv, mixed, lse, grad, last, owners, shard):
    width = qkv.shape[1]
    return pl.pallas_call(
        attend_back_kernel,
        in_specs=in_memory(8, True),
        out_specs=in_memory(2),
        out_shape=[
            jax.ShapeDtypeStruct((LEN, width), bf16),
            jax.ShapeDtypeStruct((owners, shard, width), bf16),
        ],
        scratch_shapes=[pltpu.VMEM((LEN, 2 * HD), f32)] * 3,
        compiler_params=params,
        cost_estimate=estimate(3 * 10**9, 10 * 2**20),
        name="attend_back",
    )(first_row, rows_turned, qkv, mixed, lse, grad, *last)


def pre_terms_kernel(core_ref, qkv_grad_ref, weight_ref, own_ref, sent_ref):
    half = LEN // 2
    core = core_ref[0]
    mine = pl.multiple_of(core * half, half)
    other = pl.multiple_of((1 - core) * half, half)
    sent_ref[:, :D] = mm_nt(qkv_grad_ref[pl.ds(other, half)], weight_ref[...]).astype(bf16)
    own_ref[...] = mm_nt(qkv_grad_ref[pl.ds(mine, half)], weight_ref[...]).astype(bf16)


def pre_terms(core, qkv_grad, head_weight):
    half = jax.ShapeDtypeStruct((LEN // 2, D), bf16)
    return pl.pallas_call(
        pre_terms_kernel,
        in_specs=in_memory(2, True),
        out_specs=in_memory(2),
        out_shape=[half, padded((), LEN // 2)],
        compiler_params=params,
        cost_estimate=estimate(1, 1),
        name="pre_terms",
    )(core, qkv_grad, head_weight)


def split_out(terms, own_ref, *others):
    own_ref[...] = terms[:ROWS]
    for step, ref in enumerate(others):
        ref[...] = terms[(step + 1) * ROWS : (step + 2) * ROWS].astype(bf16)


def ffn_kernel(*refs):
    mids, grads, (up_ref, down_ref) = refs[:4], refs[4:8], refs[8:10]
    gated_ref, hidden_grad_ref, turned_ref = refs[10:13]
    outs, mid_all, grad_all = refs[13:17], refs[17], refs[18]
    for step in range(4):
        cut = slice(step * ROWS, (step + 1) * ROWS)
        mid_all[cut] = mids[step][...]
        turned_ref[:, cut] = mids[step][...].T
        grad_all[cut] = grads[step][...]
    slope = (2.0 / 3.141592653589793) ** 0.5
    for low, high in ((0, 256), (256, 512), (512, 768), (768, 1088)):
        units = slice(low, high)
        hidden = mm(mid_all[...], up_ref[:, units])
        gated_grad = mm(grad_all[...], down_ref[:, units])
        square = hidden * hidden
        bent = jnp.tanh(slope * hidden * (1.0 + 0.044715 * square))
        half = 0.5 * (1.0 + bent)
        gated_ref[:, units] = (hidden * half).astype(bf16)
        back = half + 0.5 * hidden * (1.0 - bent * bent) * (
            slope * (1.0 + 3.0 * 0.044715 * square)
        )
        hidden_grad_ref[:, units] = (gated_grad * back).astype(bf16)
    split_out(mm_nt(hidden_grad_ref[...], up_ref[...]), *outs)


def ffn(mids, grads, up_full, down_full):
    units = up_full.shape[1]
    tokens = 4 * ROWS
    block = jax.ShapeDtypeStruct((ROWS, D), bf16)
    wide = jax.ShapeDtypeStruct((tokens, units), bf16)
    return pl.pallas_call(
        ffn_kernel,
        in_specs=in_memory(10),
        out_specs=in_memory(7),
        out_shape=[
            wide,
            wide,
            jax.ShapeDtypeStruct((D, tokens), bf16),
            jax.ShapeDtypeStruct((ROWS, D), f32),
            block,
            block,
            block,
        ],
        scratch_shapes=[pltpu.VMEM((tokens, D), bf16)] * 2,
        compiler_params=params,
        cost_estimate=estimate(6 * tokens * D * units, 10 * 2**20),
        name="ffn",
    )(*mids, *grads, up_full, down_full)


def ffn_terms_kernel(mid_ref, hidden_grad_ref, grad_ref, gated_ref, out_ref):
    rows = out_ref.shape[1] // 2
    up = mm(mid_ref[...], hidden_grad_ref[...])
    down = mm(grad_ref[...], gated_ref[...])
    for block in range(out_ref.shape[0]):
        cut = slice(block * rows, (block + 1) * rows)
        out_ref[block] = jnp.concatenate([up[cut], down[cut]], axis=0).astype(bf16)


def ffn_terms(mid_turned, hidden_grad, grad_turned, gated, owners, shard):
    steps = 4
    tokens, units = hidden_grad.shape
    tall = pl.BlockSpec((D // steps, tokens), lambda step: (step, 0))
    wide = pl.BlockSpec((tokens, units), lambda step: (0, 0))
    return pl.pallas_call(
        ffn_terms_kernel,
        grid=(steps,),
        in_specs=[tall, wide, tall, wide],
        out_specs=pl.BlockSpec((owners // steps, 2 * shard, units), lambda step: (step, 0, 0)),
        out_shape=jax.ShapeDtypeStruct((owners, 2 * shard, units), bf16),
        compiler_params=params,
        cost_estimate=estimate(4 * D * tokens * units, 10 * 2**20),
        name="ffn_terms",
    )(mid_turned, hidden_grad, grad_turned, gated)


def merge_terms_kernel(rows, core_ref, heads_ref, grad_ref, gain_ref, own_ref, sent_ref):
    first = core_ref[0] == 0
    for start in range(0, own_ref.shape[0], 4):
        cut = slice(start * 2 * rows, (start + 4) * 2 * rows)
        terms = jnp.concatenate([mm(heads_ref[cut], grad_ref[...]), gain_ref[cut]], axis=1)
        for pair in range(4):
            low = terms[pair * 2 * rows : pair * 2 * rows + rows]
            high = terms[pair * 2 * rows + rows : (pair + 1) * 2 * rows]
            at = (start + pair) % 4 * 4 + (start + pair) // 4
            own_ref[at, :rows] = jnp.where(first, low, high).astype(bf16)
            sent_ref[at, :rows] = jnp.where(first, high, low).astype(bf16)


def merge_terms(core, heads_turned, mid_rounded, gain_column, owners, shard):
    blocks = padded((owners // 2,), shard)
    return pl.pallas_call(
        functools.partial(merge_terms_kernel, shard),
        in_specs=in_memory(3, True),
        out_specs=in_memory(2),
        out_shape=[blocks, blocks],
        compiler_params=params,
        cost_estimate=estimate(2 * D * D * ROWS, 3 * 2**20),
        name="merge_terms",
    )(core, heads_turned, mid_rounded, gain_column)


def join_kernel(blocks_ref, *outs):
    owners = blocks_ref.shape[0]
    rows = blocks_ref.shape[1] // len(outs)
    for at, ref in enumerate(outs):
        cut = slice(at * rows, (at + 1) * rows)
        ref[...] = jnp.concatenate([blocks_ref[owner, cut] for owner in range(owners)], axis=0)


def join(blocks, count):
    owners, rows, columns = blocks.shape
    steps = 4
    whole = jax.ShapeDtypeStruct((owners * rows // count, columns), bf16)
    return pl.pallas_call(
        join_kernel,
        grid=(steps,),
        in_specs=[pl.BlockSpec((owners // steps, rows, columns), lambda step: (step, 0, 0))],
        out_specs=[pl.BlockSpec((whole.shape[0] // steps, columns), lambda step: (step, 0))]
        * count,
        out_shape=[whole] * count,
        compiler_params=params,
        cost_estimate=estimate(0, 14 * 2**20),
        name="join",
    )(blocks)


def merge_norm_kernel(
    resid_ref, arrived_ref, last_ref, merge_ref, heads_ref, middle_ref, normed_ref, invstd_ref, act_ref
):
    heads_ref[...] = jnp.concatenate(
        [arrived_ref[group] for group in range(PAIRS)] + [last_ref[...]], axis=1
    )
    middle = resid_ref[...] + mm(heads_ref[...], merge_ref[...])
    normed, invstd = normalize(middle)
    middle_ref[...] = middle
    normed_ref[...] = normed
    invstd_ref[...] = invstd
    act_ref[...] = normed.astype(bf16)


def merge_norm(resid, arrived, last_mixed, merge_full):
    rows = jax.ShapeDtypeStruct((ROWS, D), f32)
    short = jax.ShapeDtypeStruct((ROWS, D), bf16)
    return pl.pallas_call(
        merge_norm_kernel,
        in_specs=in_memory(4),
        out_specs=in_memory(5),
        out_shape=[short, rows, rows, jax.ShapeDtypeStruct((ROWS, 1), f32), short],
        compiler_params=params,
        cost_estimate=estimate(2 * ROWS * D * D, 4 * 2**20),
        name="merge_norm",
    )(resid, arrived, last_mixed, merge_full)


def norm_back_kernel(
    grad_ref, own_ref, one_ref, two_ref, three_ref, normed_ref, invstd_ref, merge_ref,
    mid_grad_ref, rounded_ref, paired_ref, last_ref, gain_ref,
):
    scaled = own_ref[...]
    for ref in (one_ref, two_ref, three_ref):
        scaled = scaled + ref[...].astype(f32)
    mid_grad = grad_ref[...] + normalize_back(scaled, normed_ref[...], invstd_ref[...])
    mid_grad_ref[...] = mid_grad
    rounded_ref[...] = mid_grad.astype(bf16)
    heads_grad = mm_nt(rounded_ref[...], merge_ref[...]).astype(bf16)
    for group in range(PAIRS):
        paired_ref[group] = heads_grad[:, group * 2 * HD : (group + 1) * 2 * HD]
    last_ref[...] = heads_grad[:, PAIRS * 2 * HD :]
    gain_ref[...] = jnp.sum(scaled * normed_ref[...], axis=0, keepdims=True)


def norm_back(grad, own, received, normed, invstd, merge_full):
    return pl.pallas_call(
        norm_back_kernel,
        in_specs=in_memory(8),
        out_specs=in_memory(5),
        out_shape=[
            jax.ShapeDtypeStruct((ROWS, D), f32),
            jax.ShapeDtypeStruct((ROWS, D), bf16),
            jax.ShapeDtypeStruct((PAIRS, ROWS, 2 * HD), bf16),
            jax.ShapeDtypeStruct((ROWS, HD), bf16),
            jax.ShapeDtypeStruct((1, D), f32),
        ],
        compiler_params=params,
        cost_estimate=estimate(2 * ROWS * D * D, 5 * 2**20),
        name="norm_back",
    )(grad, own, *received, normed, invstd, merge_full)


def cut_kernel(rows, at_ref, *refs):
    addends, outs = refs[:-4], refs[-4:]
    columns = outs[0].shape[-1]
    for step, out in enumerate(outs):
        index = (at_ref[0] + step) & 3
        for inner in range(out.shape[0]):
            block = sum(ref[index, inner, :rows, :columns].astype(f32) for ref in addends)
            out[inner, :rows, :columns] = block.astype(out.dtype)


def sum_and_cut(at, rows, *addends):
    blocks = addends[0].shape[1]
    send = padded((blocks,), rows)
    return pl.pallas_call(
        functools.partial(cut_kernel, rows),
        in_specs=in_memory(len(addends), True),
        out_specs=in_memory(4),
        out_shape=[jax.ShapeDtypeStruct((blocks, rows, LANES), f32), send, send, send],
        compiler_params=params,
        cost_estimate=estimate(1, 1),
        name="sum_and_cut",
    )(at, *addends)


def ring_cut_kernel(
    at_ref, own_ref, other_ref, gated_ref, down_ref, pre_ref, out_ref, *sends
):
    out_terms = mm_nt(gated_ref[...], down_ref[...])
    out_ref[...] = out_terms[:ROWS]
    for step, send in enumerate((pre_ref,) + sends):
        index = (at_ref[0] - step) & 3
        block = own_ref[index].astype(f32) + other_ref[index, :, :D].astype(f32)
        if step == 0:
            pre_ref[...] = block
        else:
            send[:ROWS, :D] = block.astype(bf16)
            send[ROWS:, :D] = out_terms[step * ROWS : (step + 1) * ROWS].astype(bf16)


def ring_cut(at, pre_own, pre_other, gated, down_full):
    rows = jax.ShapeDtypeStruct((ROWS, D), f32)
    send = padded((), 2 * ROWS)
    return pl.pallas_call(
        ring_cut_kernel,
        in_specs=in_memory(4, True),
        out_specs=in_memory(5),
        out_shape=[rows, rows, send, send, send],
        compiler_params=params,
        cost_estimate=estimate(1, 1),
        name="ring_cut",
    )(at, pre_own, pre_other, gated, down_full)


def after(values, earlier):
    return lax.optimization_barrier((values, earlier))[0]


def adam_step(weight, grad, mean, square, rate, decay):
    mean_next = beta_one * mean + (1.0 - beta_one) * grad
    square_next = beta_two * square + (1.0 - beta_two) * grad * grad
    mean_hat = mean_next / (1.0 - beta_one**step_count)
    square_hat = square_next / (1.0 - beta_two**step_count)
    weight_next = weight - rate * (mean_hat / (jnp.sqrt(square_hat) + adam_eps) + decay * weight)
    return (weight_next, mean_next, square_next)


def learning_rates():
    return (
        0.2,
        0.3 * D ** (-0.5),
        0.3 * max(1, D // 256) ** (-0.5),
        0.2,
        0.3 * D ** (-0.5),
        0.3 * FF ** (-0.5),
    )


def body(
    inputs,
    cotangent,
    prenorm,
    qkv_weight,
    merge_weight,
    midnorm,
    up_weight,
    down_weight,
    prenorm_mean,
    prenorm_square,
    qkv_mean,
    qkv_square,
    merge_mean,
    merge_square,
    midnorm_mean,
    midnorm_square,
    up_mean,
    up_square,
    down_mean,
    down_square,
):
    means = (prenorm_mean, qkv_mean, merge_mean, midnorm_mean, up_mean, down_mean)
    squares = (prenorm_square, qkv_square, merge_square, midnorm_square, up_square, down_square)
    masters = (prenorm, qkv_weight, merge_weight, midnorm, up_weight, down_weight)
    shard = prenorm.shape[1]
    owners = D // shard
    tensor_at = lax.axis_index("tensor")
    core_at = lax.axis_index("ctx")
    group = core_at * 4 + tensor_at
    first_row = group * ROWS

    pregain = prenorm[0].astype(bf16).astype(f32)[:, None]
    midgain = midnorm[0].astype(bf16).astype(f32)[:, None]
    qkv_work = qkv_weight[0].astype(bf16).astype(f32)
    up_work = up_weight[0].astype(bf16).astype(f32)
    qkv_scaled = (pregain * qkv_work).astype(bf16)
    up_scaled = (midgain * up_work).astype(bf16)
    merge_work = merge_weight[0].astype(bf16)
    down_work = jnp.transpose(down_weight[0]).astype(bf16)

    first_one = first_row[None].astype(jnp.int32)
    place_at = lax.axis_index("dp")
    core_one, tensor_one, z_one, x_one = (
        at[None].astype(jnp.int32) for at in (core_at, tensor_at, place_at // 4, place_at % 4)
    )
    place = jnp.stack([first_row, core_at, tensor_at]).astype(jnp.int32)

    split = qkv_scaled.reshape(shard, 3, D)
    paired = split[:, :, : 2 * PAIRS * HD].reshape(shard, 3, 2, 4, 2 * HD)
    mine = lax.dynamic_index_in_dim(paired, tensor_at, axis=3, keepdims=False)
    shared = split[:, :, 2 * PAIRS * HD :].reshape(shard, 3 * HD)
    sends = jnp.concatenate(
        [
            jnp.transpose(mine, (2, 0, 1, 3)).reshape(2, shard, 6 * HD),
            jnp.broadcast_to(shared[None], (2, shard, 3 * HD)),
        ],
        axis=2,
    )
    width = 9 * HD
    sends = jnp.broadcast_to(sends[None], (owners // 2, 2, shard, width))
    sends = sends.reshape(owners, shard, width)
    resid, grad, sends = lax.optimization_barrier((inputs[0], cotangent[0], sends))
    head_weight = exchange(sends, OWNERS).reshape(D, width)

    pre_normed, pre_invstd = normalize(resid)
    pre_blocks = gather_ring(pre_normed.astype(bf16))
    other_blocks = [swapped(block) for block in pre_blocks]

    others = lax.all_gather(
        jnp.concatenate([up_scaled, down_work, merge_work], axis=0), OWNERS, axis=0
    )

    rows_all, qkv, mixed, lse, last_mixed, last_lse = attend(
        place, pre_blocks + other_blocks, head_weight
    )
    grad_blocks = gather_ring(after(grad, pre_blocks[3]).astype(bf16))
    arrived = exchange(mixed.reshape(PAIRS, ROWS, 2 * HD), TOKENS)
    up_full, down_full, merge_full = join(after(others, mixed), 3)
    heads, middle, mid_normed, mid_invstd, mid_own = merge_norm(
        resid, arrived, last_mixed, merge_full
    )
    mid_blocks = gather_ring(mid_own)

    rows_turned = rows_all.T
    grad_turned = jnp.concatenate([block.T for block in grad_blocks], axis=1)
    grad_blocks = after(grad_blocks, (rows_turned, grad_turned))
    gated, hidden_grad, mid_turned, mid_terms, *mid_sent = ffn(
        mid_blocks, grad_blocks, up_full, down_full
    )
    mid_received = [shifted(block, "tensor", -step - 1) for step, block in enumerate(mid_sent)]
    terms = ffn_terms(mid_turned, hidden_grad, grad_turned, gated, owners, shard)
    ffn_sum = lax.psum_scatter(terms, OWNERS, scatter_dimension=0).astype(f32)
    mid_terms = after(mid_terms, terms)
    mid_grad, mid_rounded, paired_grad, last_grad, gain_row = norm_back(
        grad, mid_terms, mid_received, mid_normed, mid_invstd, merge_full
    )
    mixed_grad = exchange(paired_grad, TOKENS).reshape(LEN, 2 * HD)
    gain_column = jnp.broadcast_to(gain_row.reshape(D, 1), (D, LANES - D))
    merge_own, merge_sent = merge_terms(
        core_one, heads.T, mid_rounded, gain_column, owners, shard
    )
    merge_other = swapped(merge_sent)

    qkv_grad, weight_terms = attend_back(
        first_one,
        rows_turned,
        qkv,
        mixed,
        lse,
        mixed_grad,
        (last_mixed, last_lse, last_grad),
        owners,
        shard,
    )
    weight_received = exchange(weight_terms, OWNERS)

    pre_own, pre_sent = pre_terms(core_one, qkv_grad, head_weight)
    pre_other = swapped(pre_sent)
    merge_part, *merge_sent = sum_and_cut(
        x_one,
        shard,
        after(merge_own, pre_sent).reshape(4, 4, -1, LANES),
        merge_other.reshape(4, 4, -1, LANES),
    )
    merge_received = [along_x(block, step + 1) for step, block in enumerate(merge_sent)]
    pre_scaled, out_terms, *ring_sent = ring_cut(
        tensor_one,
        after(pre_own, merge_part).reshape(4, ROWS, D),
        pre_other.reshape(4, ROWS, LANES),
        gated,
        down_full,
    )
    ring_received = [shifted(block, "tensor", -step - 1) for step, block in enumerate(ring_sent)]
    weight_part = jnp.sum(
        after(weight_received, (ring_sent, merge_received)).astype(f32).reshape(owners // 2, 2, shard, width), axis=0
    )
    merge_part, *merge_sent = sum_and_cut(
        z_one,
        shard,
        *(
            block.reshape(4, 1, -1, LANES)
            for block in after((merge_part, *merge_received), weight_part)
        ),
    )
    merge_part = merge_part[0]
    for step, block in enumerate(merge_sent):
        merge_part = merge_part + along_z(block, step + 1)[0, :shard].astype(f32)
    for block in ring_received:
        pre_scaled = pre_scaled + block[:ROWS, :D].astype(f32)
        out_terms = out_terms + block[ROWS:, :D].astype(f32)
    out_terms, pre_scaled = after((out_terms, pre_scaled), ffn_sum)
    output = middle + out_terms
    input_grad = mid_grad + normalize_back(pre_scaled, pre_normed, pre_invstd)

    up_sum = ffn_sum[:shard]
    down_sum = ffn_sum[shard:]
    merge_sum = after(sum(gather_ring(merge_part)), ffn_sum)
    midgain_sum = merge_sum[:, D] / midgain[:, 0]
    merge_sum = merge_sum[:, :D]
    parts = jnp.stack(
        placed(
            gather_ring(
                jnp.concatenate(
                    [
                        weight_part[0, :, : 6 * HD],
                        weight_part[1, :, : 6 * HD],
                        weight_part[0, :, 6 * HD :] + weight_part[1, :, 6 * HD :],
                    ],
                    axis=1,
                )
            ),
            tensor_at,
        )
    )
    parts = after(parts, ffn_sum)
    pairs_sum = jnp.transpose(
        parts[:, :, : 12 * HD].reshape(4, shard, 2, 3, 2 * HD), (1, 3, 2, 0, 4)
    ).reshape(shard, 3, 2 * PAIRS * HD)
    last_sum = jnp.sum(parts[:, :, 12 * HD :], axis=0).reshape(shard, 3, HD)
    qkv_sum = jnp.concatenate([pairs_sum, last_sum], axis=2).reshape(shard, 3 * D)

    grads = [
        jnp.sum(qkv_work * qkv_sum, axis=1)[None],
        (pregain * qkv_sum)[None],
        merge_sum[None],
        midgain_sum[None],
        (midgain * up_sum)[None],
        jnp.transpose(down_sum)[None],
    ]
    grads = [
        layout.with_layout_constraint(grad, layout.Layout(major_to_minor=order))
        for grad, order in zip(
            grads, ((0, 1), (1, 0, 2), (1, 0, 2), (0, 1), (1, 0, 2), (2, 0, 1))
        )
    ]
    rates = learning_rates()
    decays = (0.0, decay_rate, decay_rate, 0.0, decay_rate, decay_rate)
    stepped = [
        adam_step(
            masters[index], grads[index], means[index], squares[index], rates[index], decays[index]
        )
        for index in range(6)
    ]
    return (
        output[None],
        input_grad[None],
        *grads,
        *[step[0] for step in stepped],
        *[step[1] for step in stepped],
        *[step[2] for step in stepped],
    )


def solution(mesh):
    rows = P("dp", ("ctx", "tensor"), None)
    gain = P(None, ("dp", "ctx"))
    whole = P(None, ("dp", "ctx"), None)
    wide = P(None, ("dp", "ctx"), "tensor")
    tall = P(None, "tensor", ("dp", "ctx"))
    weights = (gain, whole, whole, gain, wide, tall)
    moments = tuple(spec for spec in weights for _ in range(2))
    return jax.shard_map(
        body,
        mesh=mesh,
        in_specs=(rows, rows) + weights + moments,
        out_specs=(rows, rows) + weights * 4,
        check_vma=False,
    )
```

```python
import functools

import jax
import jax.numpy as jnp
from jax import lax
from jax.experimental import layout
from jax.experimental import pallas as pl
from jax.experimental.pallas import tpu as pltpu
from jax.sharding import PartitionSpec as P

H = 17
HD = 64
D = 1088
FF = 4352
PAIRS = 8
ROWS = 128
LEN = 1024

f32 = jnp.float32
bf16 = jnp.bfloat16

norm_eps = 1e-05
beta_one = 0.9
beta_two = 0.95
adam_eps = 1e-08
decay_rate = 0.1
step_count = 3.0

OWNERS = ("dp", "ctx")
TOKENS = ("ctx", "tensor")


def normalize(resid):
    center = resid - jnp.mean(resid, axis=-1, keepdims=True)
    invstd = lax.rsqrt(jnp.mean(center * center, axis=-1, keepdims=True) + norm_eps)
    return center * invstd, invstd


def normalize_back(scaled, normed, invstd):
    return invstd * (
        scaled
        - jnp.mean(scaled, axis=-1, keepdims=True)
        - normed * jnp.mean(scaled * normed, axis=-1, keepdims=True)
    )


def by_rows(values):
    return layout.with_layout_constraint(
        values, layout.Layout(major_to_minor=tuple(range(values.ndim)))
    )


def exchange(values, axes):
    return by_rows(lax.all_to_all(by_rows(values), axes, 0, 0))


def permuted(values, axis, pairs):
    return by_rows(lax.ppermute(by_rows(values), axis, pairs))


def shifted(values, axis, step):
    size = lax.axis_size(axis)
    return permuted(values, axis, [(at, (at + step) % size) for at in range(size)])


def swapped(values):
    return shifted(values, "ctx", 1)


def gather_ring(values):
    return [values] + [shifted(values, "tensor", step) for step in (1, 2, 3)]


def placed(blocks, at):
    return [lax.select_n((at - owner) % 4, *blocks) for owner in range(4)]


def mm(left, right):
    return lax.dot_general(left, right, (((1,), (0,)), ((), ())), preferred_element_type=f32)


def mm_nt(left, right):
    return lax.dot_general(left, right, (((1,), (1,)), ((), ())), preferred_element_type=f32)


def mm_tn(left, right):
    return lax.dot_general(left, right, (((0,), (0,)), ((), ())), preferred_element_type=f32)


TILE = 256
SCALE = HD ** (-0.5)
BIG = 2.0**100
LANES = 1152


def padded(lead, rows):
    return jax.ShapeDtypeStruct((*lead, -(-rows // 8) * 8, LANES), bf16)


params = pltpu.CompilerParams(vmem_limit_bytes=56 * 2**20)


def estimate(flops, size):
    return pl.CostEstimate(flops=1, bytes_accessed=1, transcendentals=0)


def in_memory(count, scalar=False):
    specs = [pl.BlockSpec(memory_space=pltpu.VMEM)] * count
    return ([pl.BlockSpec(memory_space=pltpu.SMEM)] if scalar else []) + specs


def causal_mask(shape, first_row, first_col):
    row_pos = first_row + lax.broadcasted_iota(jnp.int32, shape, 0)
    col_pos = first_col + lax.broadcasted_iota(jnp.int32, shape, 1)
    return col_pos <= row_pos


def column(part, head):
    at = part * 2 * HD + head * HD
    return slice(at, at + HD)


LAST_Q, LAST_K, LAST_V = (slice(6 * HD + part * HD, 7 * HD + part * HD) for part in range(3))


def soften(scores, values):
    top = scores[0].max(axis=1, keepdims=True)
    for score in scores[1:]:
        top = jnp.maximum(top, score.max(axis=1, keepdims=True))
    raised = [jnp.exp(score - top) for score in scores]
    total = sum(part.sum(axis=1, keepdims=True) for part in raised)
    inverse = 1.0 / total
    mixed = sum(mm((part * inverse).astype(bf16), value) for part, value in zip(raised, values))
    return mixed.astype(bf16), top + jnp.log(total)


def attend_kernel(place_ref, *refs):
    blocks, weight_ref, rows_ref, qkv_ref, mixed_ref, lse_ref = refs[:8], *refs[8:13]
    last_mixed_ref, last_lse_ref = refs[13:]
    core, tensor = place_ref[1], place_ref[2]
    for at, block in enumerate(blocks):
        half = core if at < 4 else 1 - core
        row = half * (4 * ROWS) + ((tensor - at) & 3) * ROWS
        rows_ref[pl.ds(pl.multiple_of(row, ROWS), ROWS)] = block[...]
    for start in range(0, LEN, TILE):
        cut = slice(start, start + TILE)
        qkv_ref[cut] = mm(rows_ref[cut], weight_ref[...]).astype(bf16)
    keep = causal_mask((TILE, TILE), 0, 0)
    for start in range(0, LEN, TILE):
        cut = slice(start, start + TILE)
        mixes, sums = [], []
        for head in range(2):
            query = qkv_ref[cut, column(0, head)] * SCALE
            scores, values = [], []
            for other in range(0, start + TILE, TILE):
                key_cut = slice(other, other + TILE)
                score = mm_nt(query, qkv_ref[key_cut, column(1, head)])
                scores.append(jnp.where(keep, score, -BIG) if other == start else score)
                values.append(qkv_ref[key_cut, column(2, head)])
            mixed, lse = soften(scores, values)
            mixes.append(mixed)
            sums.append(lse)
        mixed_ref[cut] = jnp.concatenate(mixes, axis=1)
        lse_ref[cut] = jnp.concatenate(sums, axis=1)
    first = pl.multiple_of(place_ref[0], ROWS)
    query = qkv_ref[pl.ds(first, ROWS), LAST_Q] * SCALE
    score = mm_nt(query, qkv_ref[:, LAST_K])
    score = jnp.where(causal_mask((ROWS, LEN), first, 0), score, -BIG)
    mixed, lse = soften([score], [qkv_ref[:, LAST_V]])
    last_mixed_ref[...] = mixed
    last_lse_ref[...] = lse


def attend(place, blocks, head_weight):
    width = head_weight.shape[1]
    return pl.pallas_call(
        attend_kernel,
        in_specs=in_memory(9, True),
        out_specs=in_memory(6),
        out_shape=[
            jax.ShapeDtypeStruct((LEN, D), bf16),
            jax.ShapeDtypeStruct((LEN, width), bf16),
            jax.ShapeDtypeStruct((LEN, 2 * HD), bf16),
            jax.ShapeDtypeStruct((LEN, 2), f32),
            jax.ShapeDtypeStruct((ROWS, HD), bf16),
            jax.ShapeDtypeStruct((ROWS, 1), f32),
        ],
        compiler_params=params,
        cost_estimate=estimate(2 * 10**9, 8 * 2**20),
        name="attend",
    )(place, *blocks, head_weight)


def score_back(query, keys, values, grad, lse, delta, keep):
    score = mm_nt(query, keys)
    probs = jnp.exp((score if keep is None else jnp.where(keep, score, -BIG)) - lse)
    score_grad = probs * (mm_nt(grad, values) - delta)
    return probs.astype(bf16), score_grad.astype(bf16)


def attend_back_kernel(
    first_ref,
    rows_ref,
    qkv_ref,
    mixed_ref,
    lse_ref,
    grad_ref,
    last_mixed_ref,
    last_lse_ref,
    last_grad_ref,
    out_ref,
    terms_ref,
    query_sum,
    key_sum,
    value_sum,
):
    keep = causal_mask((TILE, TILE), 0, 0)
    for head in range(2):
        lanes = slice(head * HD, (head + 1) * HD)
        for start in range(0, LEN, TILE):
            cut = slice(start, start + TILE)
            query = qkv_ref[cut, column(0, head)]
            grad = grad_ref[cut, lanes]
            delta = jnp.sum(
                grad.astype(f32) * mixed_ref[cut, lanes].astype(f32), axis=1, keepdims=True
            )
            lse = lse_ref[cut, head : head + 1]
            query_grad = None
            for other in range(0, start + TILE, TILE):
                key_cut = slice(other, other + TILE)
                keys = qkv_ref[key_cut, column(1, head)]
                probs, score_grad = score_back(
                    query * SCALE,
                    keys,
                    qkv_ref[key_cut, column(2, head)],
                    grad,
                    lse,
                    delta,
                    keep if other == start else None,
                )
                value_term = mm_tn(probs, grad)
                key_term = mm_tn(score_grad, query)
                query_term = mm(score_grad, keys)
                query_grad = query_term if query_grad is None else query_grad + query_term
                if other == start:
                    value_sum[key_cut, lanes] = value_term
                    key_sum[key_cut, lanes] = key_term
                else:
                    value_sum[key_cut, lanes] += value_term
                    key_sum[key_cut, lanes] += key_term
            query_sum[cut, lanes] = query_grad
    pair = 2 * HD
    out_ref[:, :pair] = (query_sum[...] * SCALE).astype(bf16)
    out_ref[:, pair : 2 * pair] = (key_sum[...] * SCALE).astype(bf16)
    out_ref[:, 2 * pair : 3 * pair] = value_sum[...].astype(bf16)

    first = pl.multiple_of(first_ref[0], ROWS)
    query = qkv_ref[pl.ds(first, ROWS), LAST_Q]
    keys = qkv_ref[:, LAST_K]
    grad = last_grad_ref[...]
    delta = jnp.sum(
        grad.astype(f32) * last_mixed_ref[...].astype(f32), axis=1, keepdims=True
    )
    probs, score_grad = score_back(
        query * SCALE,
        keys,
        qkv_ref[:, LAST_V],
        grad,
        last_lse_ref[...],
        delta,
        causal_mask((ROWS, LEN), first, 0),
    )
    query_sum[:, :HD] = jnp.zeros((LEN, HD), f32)
    query_sum[pl.ds(first, ROWS), :HD] = mm(score_grad, keys)
    key_term = mm_tn(score_grad, query)
    out_ref[:, 3 * pair : 4 * pair] = (
        jnp.concatenate([query_sum[:, :HD], key_term], axis=1) * SCALE
    ).astype(bf16)
    out_ref[:, 4 * pair :] = mm_tn(probs, grad).astype(bf16)

    owners, shard = terms_ref.shape[:2]
    for start in range(0, owners, 8):
        terms = mm(rows_ref[start * shard : (start + 8) * shard], out_ref[...])
        for block in range(8):
            terms_ref[start + block] = terms[block * shard : (block + 1) * shard].astype(bf16)


def attend_back(first_row, rows_turned, qkv, mixed, lse, grad, last, owners, shard):
    width = qkv.shape[1]
    return pl.pallas_call(
        attend_back_kernel,
        in_specs=in_memory(8, True),
        out_specs=in_memory(2),
        out_shape=[
            jax.ShapeDtypeStruct((LEN, width), bf16),
            jax.ShapeDtypeStruct((owners, shard, width), bf16),
        ],
        scratch_shapes=[pltpu.VMEM((LEN, 2 * HD), f32)] * 3,
        compiler_params=params,
        cost_estimate=pl.CostEstimate(
            flops=14 * 10**9, bytes_accessed=10 * 2**20, transcendentals=0
        ),
        name="attend_back",
    )(first_row, rows_turned, qkv, mixed, lse, grad, *last)


def pre_terms_kernel(core_ref, qkv_grad_ref, weight_ref, own_ref, sent_ref):
    half = LEN // 2
    core = core_ref[0]
    mine = pl.multiple_of(core * half, half)
    other = pl.multiple_of((1 - core) * half, half)
    sent_ref[:, :D] = mm_nt(qkv_grad_ref[pl.ds(other, half)], weight_ref[...]).astype(bf16)
    own_ref[...] = mm_nt(qkv_grad_ref[pl.ds(mine, half)], weight_ref[...]).astype(bf16)


def pre_terms(core, qkv_grad, head_weight):
    half = jax.ShapeDtypeStruct((LEN // 2, D), bf16)
    return pl.pallas_call(
        pre_terms_kernel,
        in_specs=in_memory(2, True),
        out_specs=in_memory(2),
        out_shape=[half, padded((), LEN // 2)],
        compiler_params=params,
        cost_estimate=estimate(1, 1),
        name="pre_terms",
    )(core, qkv_grad, head_weight)


def split_out(terms, own_ref, *others):
    own_ref[...] = terms[:ROWS]
    for step, ref in enumerate(others):
        ref[...] = terms[(step + 1) * ROWS : (step + 2) * ROWS].astype(bf16)


def ffn_kernel(*refs):
    mids, grads, (up_ref, down_ref) = refs[:4], refs[4:8], refs[8:10]
    gated_ref, hidden_grad_ref, turned_ref = refs[10:13]
    outs, mid_all, grad_all = refs[13:17], refs[17], refs[18]
    for step in range(4):
        cut = slice(step * ROWS, (step + 1) * ROWS)
        mid_all[cut] = mids[step][...]
        turned_ref[:, cut] = mids[step][...].T
        grad_all[cut] = grads[step][...]
    slope = (2.0 / 3.141592653589793) ** 0.5
    for low, high in ((0, 256), (256, 512), (512, 768), (768, 1088)):
        units = slice(low, high)
        hidden = mm(mid_all[...], up_ref[:, units])
        gated_grad = mm(grad_all[...], down_ref[:, units])
        square = hidden * hidden
        bent = jnp.tanh(slope * hidden * (1.0 + 0.044715 * square))
        half = 0.5 * (1.0 + bent)
        gated_ref[:, units] = (hidden * half).astype(bf16)
        back = half + 0.5 * hidden * (1.0 - bent * bent) * (
            slope * (1.0 + 3.0 * 0.044715 * square)
        )
        hidden_grad_ref[:, units] = (gated_grad * back).astype(bf16)
    split_out(mm_nt(hidden_grad_ref[...], up_ref[...]), *outs)


def ffn(mids, grads, up_full, down_full):
    units = up_full.shape[1]
    tokens = 4 * ROWS
    block = jax.ShapeDtypeStruct((ROWS, D), bf16)
    wide = jax.ShapeDtypeStruct((tokens, units), bf16)
    return pl.pallas_call(
        ffn_kernel,
        in_specs=in_memory(10),
        out_specs=in_memory(7),
        out_shape=[
            wide,
            wide,
            jax.ShapeDtypeStruct((D, tokens), bf16),
            jax.ShapeDtypeStruct((ROWS, D), f32),
            block,
            block,
            block,
        ],
        scratch_shapes=[pltpu.VMEM((tokens, D), bf16)] * 2,
        compiler_params=params,
        cost_estimate=estimate(6 * tokens * D * units, 10 * 2**20),
        name="ffn",
    )(*mids, *grads, up_full, down_full)


def ffn_terms_kernel(mid_ref, hidden_grad_ref, grad_ref, gated_ref, out_ref):
    rows = out_ref.shape[1] // 2
    up = mm(mid_ref[...], hidden_grad_ref[...])
    down = mm(grad_ref[...], gated_ref[...])
    for block in range(out_ref.shape[0]):
        cut = slice(block * rows, (block + 1) * rows)
        out_ref[block] = jnp.concatenate([up[cut], down[cut]], axis=0).astype(bf16)


def ffn_terms(mid_turned, hidden_grad, grad_turned, gated, owners, shard):
    steps = 4
    tokens, units = hidden_grad.shape
    tall = pl.BlockSpec((D // steps, tokens), lambda step: (step, 0))
    wide = pl.BlockSpec((tokens, units), lambda step: (0, 0))
    return pl.pallas_call(
        ffn_terms_kernel,
        grid=(steps,),
        in_specs=[tall, wide, tall, wide],
        out_specs=pl.BlockSpec((owners // steps, 2 * shard, units), lambda step: (step, 0, 0)),
        out_shape=jax.ShapeDtypeStruct((owners, 2 * shard, units), bf16),
        compiler_params=params,
        cost_estimate=estimate(4 * D * tokens * units, 10 * 2**20),
        name="ffn_terms",
    )(mid_turned, hidden_grad, grad_turned, gated)


def merge_terms_kernel(rows, core_ref, heads_ref, grad_ref, gain_ref, own_ref, sent_ref):
    first = core_ref[0] == 0
    for start in range(0, own_ref.shape[0], 4):
        cut = slice(start * 2 * rows, (start + 4) * 2 * rows)
        terms = jnp.concatenate([mm(heads_ref[cut], grad_ref[...]), gain_ref[cut]], axis=1)
        for pair in range(4):
            low = terms[pair * 2 * rows : pair * 2 * rows + rows]
            high = terms[pair * 2 * rows + rows : (pair + 1) * 2 * rows]
            at = start + pair
            own_ref[at, :rows] = jnp.where(first, low, high).astype(bf16)
            sent_ref[at, :rows] = jnp.where(first, high, low).astype(bf16)


def merge_terms(core, heads_turned, mid_rounded, gain_column, owners, shard):
    blocks = padded((owners // 2,), shard)
    return pl.pallas_call(
        functools.partial(merge_terms_kernel, shard),
        in_specs=in_memory(3, True),
        out_specs=in_memory(2),
        out_shape=[blocks, blocks],
        compiler_params=params,
        cost_estimate=estimate(2 * D * D * ROWS, 3 * 2**20),
        name="merge_terms",
    )(core, heads_turned, mid_rounded, gain_column)


def join_kernel(blocks_ref, *outs):
    owners = blocks_ref.shape[0]
    rows = blocks_ref.shape[1] // len(outs)
    for at, ref in enumerate(outs):
        cut = slice(at * rows, (at + 1) * rows)
        ref[...] = jnp.concatenate([blocks_ref[owner, cut] for owner in range(owners)], axis=0)


def join(blocks, count):
    owners, rows, columns = blocks.shape
    steps = 4
    whole = jax.ShapeDtypeStruct((owners * rows // count, columns), bf16)
    return pl.pallas_call(
        join_kernel,
        grid=(steps,),
        in_specs=[pl.BlockSpec((owners // steps, rows, columns), lambda step: (step, 0, 0))],
        out_specs=[pl.BlockSpec((whole.shape[0] // steps, columns), lambda step: (step, 0))]
        * count,
        out_shape=[whole] * count,
        compiler_params=params,
        cost_estimate=estimate(0, 14 * 2**20),
        name="join",
    )(blocks)


def merge_norm_kernel(
    resid_ref, arrived_ref, last_ref, merge_ref, heads_ref, middle_ref, normed_ref, invstd_ref, act_ref
):
    heads_ref[...] = jnp.concatenate(
        [arrived_ref[group] for group in range(PAIRS)] + [last_ref[...]], axis=1
    )
    middle = resid_ref[...] + mm(heads_ref[...], merge_ref[...])
    normed, invstd = normalize(middle)
    middle_ref[...] = middle
    normed_ref[...] = normed
    invstd_ref[...] = invstd
    act_ref[...] = normed.astype(bf16)


def merge_norm(resid, arrived, last_mixed, merge_full):
    rows = jax.ShapeDtypeStruct((ROWS, D), f32)
    short = jax.ShapeDtypeStruct((ROWS, D), bf16)
    return pl.pallas_call(
        merge_norm_kernel,
        in_specs=in_memory(4),
        out_specs=in_memory(5),
        out_shape=[short, rows, rows, jax.ShapeDtypeStruct((ROWS, 1), f32), short],
        compiler_params=params,
        cost_estimate=estimate(2 * ROWS * D * D, 4 * 2**20),
        name="merge_norm",
    )(resid, arrived, last_mixed, merge_full)


def norm_back_kernel(
    grad_ref, own_ref, one_ref, two_ref, three_ref, normed_ref, invstd_ref, merge_ref,
    mid_grad_ref, rounded_ref, paired_ref, last_ref, gain_ref,
):
    scaled = own_ref[...]
    for ref in (one_ref, two_ref, three_ref):
        scaled = scaled + ref[...].astype(f32)
    mid_grad = grad_ref[...] + normalize_back(scaled, normed_ref[...], invstd_ref[...])
    mid_grad_ref[...] = mid_grad
    rounded_ref[...] = mid_grad.astype(bf16)
    heads_grad = mm_nt(rounded_ref[...], merge_ref[...]).astype(bf16)
    for group in range(PAIRS):
        paired_ref[group] = heads_grad[:, group * 2 * HD : (group + 1) * 2 * HD]
    last_ref[...] = heads_grad[:, PAIRS * 2 * HD :]
    gain_ref[...] = jnp.sum(scaled * normed_ref[...], axis=0, keepdims=True)


def norm_back(grad, own, received, normed, invstd, merge_full):
    return pl.pallas_call(
        norm_back_kernel,
        in_specs=in_memory(8),
        out_specs=in_memory(5),
        out_shape=[
            jax.ShapeDtypeStruct((ROWS, D), f32),
            jax.ShapeDtypeStruct((ROWS, D), bf16),
            jax.ShapeDtypeStruct((PAIRS, ROWS, 2 * HD), bf16),
            jax.ShapeDtypeStruct((ROWS, HD), bf16),
            jax.ShapeDtypeStruct((1, D), f32),
        ],
        compiler_params=params,
        cost_estimate=estimate(2 * ROWS * D * D, 5 * 2**20),
        name="norm_back",
    )(grad, own, *received, normed, invstd, merge_full)


def ring_cut_kernel(
    at_ref, own_ref, other_ref, gated_ref, down_ref, pre_ref, out_ref, *sends
):
    out_terms = mm_nt(gated_ref[...], down_ref[...])
    out_ref[...] = out_terms[:ROWS]
    for step, send in enumerate((pre_ref,) + sends):
        index = (at_ref[0] - step) & 3
        block = own_ref[index].astype(f32) + other_ref[index, :, :D].astype(f32)
        if step == 0:
            pre_ref[...] = block
        else:
            send[:ROWS, :D] = block.astype(bf16)
            send[ROWS:, :D] = out_terms[step * ROWS : (step + 1) * ROWS].astype(bf16)


def ring_cut(at, pre_own, pre_other, gated, down_full):
    rows = jax.ShapeDtypeStruct((ROWS, D), f32)
    send = padded((), 2 * ROWS)
    return pl.pallas_call(
        ring_cut_kernel,
        in_specs=in_memory(4, True),
        out_specs=in_memory(5),
        out_shape=[rows, rows, send, send, send],
        compiler_params=params,
        cost_estimate=estimate(1, 1),
        name="ring_cut",
    )(at, pre_own, pre_other, gated, down_full)


def after(values, earlier):
    return lax.optimization_barrier((values, earlier))[0]


def adam_step(weight, grad, mean, square, rate, decay):
    mean_next = beta_one * mean + (1.0 - beta_one) * grad
    square_next = beta_two * square + (1.0 - beta_two) * grad * grad
    mean_hat = mean_next / (1.0 - beta_one**step_count)
    square_hat = square_next / (1.0 - beta_two**step_count)
    weight_next = weight - rate * (mean_hat / (jnp.sqrt(square_hat) + adam_eps) + decay * weight)
    return (weight_next, mean_next, square_next)


def learning_rates():
    return (
        0.2,
        0.3 * D ** (-0.5),
        0.3 * max(1, D // 256) ** (-0.5),
        0.2,
        0.3 * D ** (-0.5),
        0.3 * FF ** (-0.5),
    )


def body(
    inputs,
    cotangent,
    prenorm,
    qkv_weight,
    merge_weight,
    midnorm,
    up_weight,
    down_weight,
    prenorm_mean,
    prenorm_square,
    qkv_mean,
    qkv_square,
    merge_mean,
    merge_square,
    midnorm_mean,
    midnorm_square,
    up_mean,
    up_square,
    down_mean,
    down_square,
):
    means = (prenorm_mean, qkv_mean, merge_mean, midnorm_mean, up_mean, down_mean)
    squares = (prenorm_square, qkv_square, merge_square, midnorm_square, up_square, down_square)
    masters = (prenorm, qkv_weight, merge_weight, midnorm, up_weight, down_weight)
    shard = prenorm.shape[1]
    owners = D // shard
    tensor_at = lax.axis_index("tensor")
    core_at = lax.axis_index("ctx")
    group = core_at * 4 + tensor_at
    first_row = group * ROWS

    pregain = prenorm[0].astype(bf16).astype(f32)[:, None]
    midgain = midnorm[0].astype(bf16).astype(f32)[:, None]
    qkv_work = qkv_weight[0].astype(bf16).astype(f32)
    up_work = up_weight[0].astype(bf16).astype(f32)
    qkv_scaled = (pregain * qkv_work).astype(bf16)
    up_scaled = (midgain * up_work).astype(bf16)
    merge_work = merge_weight[0].astype(bf16)
    down_work = jnp.transpose(down_weight[0]).astype(bf16)

    first_one = first_row[None].astype(jnp.int32)
    core_one, tensor_one = (at[None].astype(jnp.int32) for at in (core_at, tensor_at))
    place = jnp.stack([first_row, core_at, tensor_at]).astype(jnp.int32)

    split = qkv_scaled.reshape(shard, 3, D)
    paired = split[:, :, : 2 * PAIRS * HD].reshape(shard, 3, 2, 4, 2 * HD)
    mine = lax.dynamic_index_in_dim(paired, tensor_at, axis=3, keepdims=False)
    shared = split[:, :, 2 * PAIRS * HD :].reshape(shard, 3 * HD)
    sends = jnp.concatenate(
        [
            jnp.transpose(mine, (2, 0, 1, 3)).reshape(2, shard, 6 * HD),
            jnp.broadcast_to(shared[None], (2, shard, 3 * HD)),
        ],
        axis=2,
    )
    width = 9 * HD
    sends = jnp.broadcast_to(sends[None], (owners // 2, 2, shard, width))
    sends = sends.reshape(owners, shard, width)
    resid, grad, sends = lax.optimization_barrier((inputs[0], cotangent[0], sends))
    head_weight = exchange(sends, OWNERS).reshape(D, width)

    pre_normed, pre_invstd = normalize(resid)
    pre_blocks = gather_ring(pre_normed.astype(bf16))
    other_blocks = [swapped(block) for block in pre_blocks]

    others = lax.all_gather(
        jnp.concatenate([up_scaled, down_work, merge_work], axis=0), OWNERS, axis=0
    )

    rows_all, qkv, mixed, lse, last_mixed, last_lse = attend(
        place, pre_blocks + other_blocks, head_weight
    )
    grad_blocks = gather_ring(after(grad, pre_blocks[3]).astype(bf16))
    arrived = exchange(mixed.reshape(PAIRS, ROWS, 2 * HD), TOKENS)
    up_full, down_full, merge_full = join(after(others, mixed), 3)
    heads, middle, mid_normed, mid_invstd, mid_own = merge_norm(
        resid, arrived, last_mixed, merge_full
    )
    mid_blocks = gather_ring(mid_own)

    rows_turned = rows_all.T
    grad_turned = jnp.concatenate([block.T for block in grad_blocks], axis=1)
    grad_blocks = after(grad_blocks, (rows_turned, grad_turned))
    gated, hidden_grad, mid_turned, mid_terms, *mid_sent = ffn(
        mid_blocks, grad_blocks, up_full, down_full
    )
    mid_received = [shifted(block, "tensor", -step - 1) for step, block in enumerate(mid_sent)]
    terms = ffn_terms(mid_turned, hidden_grad, grad_turned, gated, owners, shard)
    ffn_sum = lax.psum_scatter(terms, OWNERS, scatter_dimension=0).astype(f32)
    mid_terms = after(mid_terms, terms)
    mid_grad, mid_rounded, paired_grad, last_grad, gain_row = norm_back(
        grad, mid_terms, mid_received, mid_normed, mid_invstd, merge_full
    )
    mixed_grad = exchange(paired_grad, TOKENS).reshape(LEN, 2 * HD)
    gain_column = jnp.broadcast_to(gain_row.reshape(D, 1), (D, LANES - D))
    merge_own, merge_sent = merge_terms(
        core_one, heads.T, mid_rounded, gain_column, owners, shard
    )
    merge_other = swapped(merge_sent)

    merge_part = (merge_own.astype(f32) + merge_other.astype(f32)).astype(bf16)

    qkv_grad, weight_terms = attend_back(
        first_one,
        rows_turned,
        qkv,
        mixed,
        lse,
        after(mixed_grad, merge_part),
        (last_mixed, last_lse, last_grad),
        owners,
        shard,
    )
    weight_received = exchange(weight_terms, OWNERS)
    pre_own, pre_sent = pre_terms(core_one, qkv_grad, head_weight)
    pre_other = swapped(pre_sent)
    pre_scaled, out_terms, *ring_sent = ring_cut(
        tensor_one,
        pre_own.reshape(4, ROWS, D),
        pre_other.reshape(4, ROWS, LANES),
        gated,
        down_full,
    )
    ring_received = [shifted(block, "tensor", -step - 1) for step, block in enumerate(ring_sent)]
    weight_part = jnp.sum(
        after(weight_received, ring_sent).astype(f32).reshape(owners // 2, 2, shard, width), axis=0
    )
    merge_part = jnp.sum(
        exchange(after(merge_part, weight_received), "dp")[:, :shard].astype(f32), axis=0
    )
    for block in ring_received:
        pre_scaled = pre_scaled + block[:ROWS, :D].astype(f32)
        out_terms = out_terms + block[ROWS:, :D].astype(f32)
    out_terms, pre_scaled = after((out_terms, pre_scaled), ffn_sum)
    output = middle + out_terms
    input_grad = mid_grad + normalize_back(pre_scaled, pre_normed, pre_invstd)

    up_sum = ffn_sum[:shard]
    down_sum = ffn_sum[shard:]
    merge_sum = sum(gather_ring(merge_part))
    midgain_sum = merge_sum[:, D] / midgain[:, 0]
    merge_sum = merge_sum[:, :D]
    parts = jnp.stack(
        placed(
            gather_ring(
                jnp.concatenate(
                    [
                        weight_part[0, :, : 6 * HD],
                        weight_part[1, :, : 6 * HD],
                        weight_part[0, :, 6 * HD :] + weight_part[1, :, 6 * HD :],
                    ],
                    axis=1,
                )
            ),
            tensor_at,
        )
    )
    parts = after(parts, ffn_sum)
    pairs_sum = jnp.transpose(
        parts[:, :, : 12 * HD].reshape(4, shard, 2, 3, 2 * HD), (1, 3, 2, 0, 4)
    ).reshape(shard, 3, 2 * PAIRS * HD)
    last_sum = jnp.sum(parts[:, :, 12 * HD :], axis=0).reshape(shard, 3, HD)
    qkv_sum = jnp.concatenate([pairs_sum, last_sum], axis=2).reshape(shard, 3 * D)

    grads = [
        jnp.sum(qkv_work * qkv_sum, axis=1)[None],
        (pregain * qkv_sum)[None],
        merge_sum[None],
        midgain_sum[None],
        (midgain * up_sum)[None],
        jnp.transpose(down_sum)[None],
    ]
    grads = [
        layout.with_layout_constraint(grad, layout.Layout(major_to_minor=order))
        for grad, order in zip(
            grads, ((0, 1), (1, 0, 2), (1, 0, 2), (0, 1), (1, 0, 2), (2, 0, 1))
        )
    ]
    rates = learning_rates()
    decays = (0.0, decay_rate, decay_rate, 0.0, decay_rate, decay_rate)
    stepped = [
        adam_step(
            masters[index], grads[index], means[index], squares[index], rates[index], decays[index]
        )
        for index in range(6)
    ]
    return (
        output[None],
        input_grad[None],
        *grads,
        *[step[0] for step in stepped],
        *[step[1] for step in stepped],
        *[step[2] for step in stepped],
    )


def solution(mesh):
    rows = P("dp", ("ctx", "tensor"), None)
    gain = P(None, ("dp", "ctx"))
    whole = P(None, ("dp", "ctx"), None)
    wide = P(None, ("dp", "ctx"), "tensor")
    tall = P(None, "tensor", ("dp", "ctx"))
    weights = (gain, whole, whole, gain, wide, tall)
    moments = tuple(spec for spec in weights for _ in range(2))
    return jax.shard_map(
        body,
        mesh=mesh,
        in_specs=(rows, rows) + weights + moments,
        out_specs=(rows, rows) + weights * 4,
        check_vma=False,
    )
```

```python
import functools

import jax
import jax.numpy as jnp
from jax import lax
from jax.experimental import layout
from jax.experimental import pallas as pl
from jax.experimental.pallas import tpu as pltpu
from jax.sharding import PartitionSpec as P

H = 17
HD = 64
D = 1088
FF = 4352
PAIRS = 8
ROWS = 128
LEN = 1024

f32 = jnp.float32
bf16 = jnp.bfloat16

norm_eps = 1e-05
beta_one = 0.9
beta_two = 0.95
adam_eps = 1e-08
decay_rate = 0.1
step_count = 3.0

OWNERS = ("dp", "ctx")
TOKENS = ("ctx", "tensor")


def normalize(resid):
    center = resid - jnp.mean(resid, axis=-1, keepdims=True)
    invstd = lax.rsqrt(jnp.mean(center * center, axis=-1, keepdims=True) + norm_eps)
    return center * invstd, invstd


def normalize_back(scaled, normed, invstd):
    return invstd * (
        scaled
        - jnp.mean(scaled, axis=-1, keepdims=True)
        - normed * jnp.mean(scaled * normed, axis=-1, keepdims=True)
    )


def by_rows(values):
    return layout.with_layout_constraint(
        values, layout.Layout(major_to_minor=tuple(range(values.ndim)))
    )


def exchange(values, axes):
    return by_rows(lax.all_to_all(by_rows(values), axes, 0, 0))


def permuted(values, axis, pairs):
    return by_rows(lax.ppermute(by_rows(values), axis, pairs))


def shifted(values, axis, step):
    size = lax.axis_size(axis)
    return permuted(values, axis, [(at, (at + step) % size) for at in range(size)])


def swapped(values):
    return shifted(values, "ctx", 1)


def gather_ring(values):
    return [values] + [shifted(values, "tensor", step) for step in (1, 2, 3)]


def placed(blocks, at):
    return [lax.select_n((at - owner) % 4, *blocks) for owner in range(4)]


def mm(left, right):
    return lax.dot_general(left, right, (((1,), (0,)), ((), ())), preferred_element_type=f32)


def mm_nt(left, right):
    return lax.dot_general(left, right, (((1,), (1,)), ((), ())), preferred_element_type=f32)


def mm_tn(left, right):
    return lax.dot_general(left, right, (((0,), (0,)), ((), ())), preferred_element_type=f32)


TILE = 256
SCALE = HD ** (-0.5)
BIG = 2.0**100
LANES = 1152


def padded(lead, rows):
    return jax.ShapeDtypeStruct((*lead, -(-rows // 8) * 8, LANES), bf16)


params = pltpu.CompilerParams(vmem_limit_bytes=56 * 2**20)


def estimate(flops, size):
    return pl.CostEstimate(flops=1, bytes_accessed=1, transcendentals=0)


def in_memory(count, scalar=False):
    specs = [pl.BlockSpec(memory_space=pltpu.VMEM)] * count
    return ([pl.BlockSpec(memory_space=pltpu.SMEM)] if scalar else []) + specs


def causal_mask(shape, first_row, first_col):
    row_pos = first_row + lax.broadcasted_iota(jnp.int32, shape, 0)
    col_pos = first_col + lax.broadcasted_iota(jnp.int32, shape, 1)
    return col_pos <= row_pos


def column(part, head):
    at = part * 2 * HD + head * HD
    return slice(at, at + HD)


LAST_Q, LAST_K, LAST_V = (slice(6 * HD + part * HD, 7 * HD + part * HD) for part in range(3))


def soften(scores, values):
    top = scores[0].max(axis=1, keepdims=True)
    for score in scores[1:]:
        top = jnp.maximum(top, score.max(axis=1, keepdims=True))
    raised = [jnp.exp(score - top) for score in scores]
    total = sum(part.sum(axis=1, keepdims=True) for part in raised)
    inverse = 1.0 / total
    mixed = sum(mm((part * inverse).astype(bf16), value) for part, value in zip(raised, values))
    return mixed.astype(bf16), top + jnp.log(total)


def attend_kernel(place_ref, *refs):
    blocks, weight_ref, rows_ref, qkv_ref, mixed_ref, lse_ref = refs[:8], *refs[8:13]
    last_mixed_ref, last_lse_ref = refs[13:]
    core, tensor = place_ref[1], place_ref[2]
    for at, block in enumerate(blocks):
        half = core if at < 4 else 1 - core
        row = half * (4 * ROWS) + ((tensor - at) & 3) * ROWS
        rows_ref[pl.ds(pl.multiple_of(row, ROWS), ROWS)] = block[...]
    for start in range(0, LEN, TILE):
        cut = slice(start, start + TILE)
        qkv_ref[cut] = mm(rows_ref[cut], weight_ref[...]).astype(bf16)
    keep = causal_mask((TILE, TILE), 0, 0)
    for start in range(0, LEN, TILE):
        cut = slice(start, start + TILE)
        mixes, sums = [], []
        for head in range(2):
            query = qkv_ref[cut, column(0, head)] * SCALE
            scores, values = [], []
            for other in range(0, start + TILE, TILE):
                key_cut = slice(other, other + TILE)
                score = mm_nt(query, qkv_ref[key_cut, column(1, head)])
                scores.append(jnp.where(keep, score, -BIG) if other == start else score)
                values.append(qkv_ref[key_cut, column(2, head)])
            mixed, lse = soften(scores, values)
            mixes.append(mixed)
            sums.append(lse)
        mixed_ref[cut] = jnp.concatenate(mixes, axis=1)
        lse_ref[cut] = jnp.concatenate(sums, axis=1)
    first = pl.multiple_of(place_ref[0], ROWS)
    query = qkv_ref[pl.ds(first, ROWS), LAST_Q] * SCALE
    score = mm_nt(query, qkv_ref[:, LAST_K])
    score = jnp.where(causal_mask((ROWS, LEN), first, 0), score, -BIG)
    mixed, lse = soften([score], [qkv_ref[:, LAST_V]])
    last_mixed_ref[...] = mixed
    last_lse_ref[...] = lse


def attend(place, blocks, head_weight):
    width = head_weight.shape[1]
    return pl.pallas_call(
        attend_kernel,
        in_specs=in_memory(9, True),
        out_specs=in_memory(6),
        out_shape=[
            jax.ShapeDtypeStruct((LEN, D), bf16),
            jax.ShapeDtypeStruct((LEN, width), bf16),
            jax.ShapeDtypeStruct((LEN, 2 * HD), bf16),
            jax.ShapeDtypeStruct((LEN, 2), f32),
            jax.ShapeDtypeStruct((ROWS, HD), bf16),
            jax.ShapeDtypeStruct((ROWS, 1), f32),
        ],
        compiler_params=params,
        cost_estimate=estimate(2 * 10**9, 8 * 2**20),
        name="attend",
    )(place, *blocks, head_weight)


def score_back(query, keys, values, grad, lse, delta, keep):
    score = mm_nt(query, keys)
    probs = jnp.exp((score if keep is None else jnp.where(keep, score, -BIG)) - lse)
    score_grad = probs * (mm_nt(grad, values) - delta)
    return probs.astype(bf16), score_grad.astype(bf16)


def attend_back_kernel(
    first_ref,
    rows_ref,
    qkv_ref,
    mixed_ref,
    lse_ref,
    grad_ref,
    last_mixed_ref,
    last_lse_ref,
    last_grad_ref,
    out_ref,
    terms_ref,
    query_sum,
    key_sum,
    value_sum,
):
    keep = causal_mask((TILE, TILE), 0, 0)
    for head in range(2):
        lanes = slice(head * HD, (head + 1) * HD)
        for start in range(0, LEN, TILE):
            cut = slice(start, start + TILE)
            query = qkv_ref[cut, column(0, head)]
            grad = grad_ref[cut, lanes]
            delta = jnp.sum(
                grad.astype(f32) * mixed_ref[cut, lanes].astype(f32), axis=1, keepdims=True
            )
            lse = lse_ref[cut, head : head + 1]
            query_grad = None
            for other in range(0, start + TILE, TILE):
                key_cut = slice(other, other + TILE)
                keys = qkv_ref[key_cut, column(1, head)]
                probs, score_grad = score_back(
                    query * SCALE,
                    keys,
                    qkv_ref[key_cut, column(2, head)],
                    grad,
                    lse,
                    delta,
                    keep if other == start else None,
                )
                value_term = mm_tn(probs, grad)
                key_term = mm_tn(score_grad, query)
                query_term = mm(score_grad, keys)
                query_grad = query_term if query_grad is None else query_grad + query_term
                if other == start:
                    value_sum[key_cut, lanes] = value_term
                    key_sum[key_cut, lanes] = key_term
                else:
                    value_sum[key_cut, lanes] += value_term
                    key_sum[key_cut, lanes] += key_term
            query_sum[cut, lanes] = query_grad
    pair = 2 * HD
    out_ref[:, :pair] = (query_sum[...] * SCALE).astype(bf16)
    out_ref[:, pair : 2 * pair] = (key_sum[...] * SCALE).astype(bf16)
    out_ref[:, 2 * pair : 3 * pair] = value_sum[...].astype(bf16)

    first = pl.multiple_of(first_ref[0], ROWS)
    query = qkv_ref[pl.ds(first, ROWS), LAST_Q]
    keys = qkv_ref[:, LAST_K]
    grad = last_grad_ref[...]
    delta = jnp.sum(
        grad.astype(f32) * last_mixed_ref[...].astype(f32), axis=1, keepdims=True
    )
    probs, score_grad = score_back(
        query * SCALE,
        keys,
        qkv_ref[:, LAST_V],
        grad,
        last_lse_ref[...],
        delta,
        causal_mask((ROWS, LEN), first, 0),
    )
    query_sum[:, :HD] = jnp.zeros((LEN, HD), f32)
    query_sum[pl.ds(first, ROWS), :HD] = mm(score_grad, keys)
    key_term = mm_tn(score_grad, query)
    out_ref[:, 3 * pair : 4 * pair] = (
        jnp.concatenate([query_sum[:, :HD], key_term], axis=1) * SCALE
    ).astype(bf16)
    out_ref[:, 4 * pair :] = mm_tn(probs, grad).astype(bf16)

    owners, shard = terms_ref.shape[:2]
    for start in range(0, owners, 8):
        terms = mm(rows_ref[start * shard : (start + 8) * shard], out_ref[...])
        for block in range(8):
            terms_ref[start + block] = terms[block * shard : (block + 1) * shard].astype(bf16)


def attend_back(first_row, rows_turned, qkv, mixed, lse, grad, last, owners, shard):
    width = qkv.shape[1]
    return pl.pallas_call(
        attend_back_kernel,
        in_specs=in_memory(8, True),
        out_specs=in_memory(2),
        out_shape=[
            jax.ShapeDtypeStruct((LEN, width), bf16),
            jax.ShapeDtypeStruct((owners, shard, width), bf16),
        ],
        scratch_shapes=[pltpu.VMEM((LEN, 2 * HD), f32)] * 3,
        compiler_params=params,
        cost_estimate=pl.CostEstimate(
            flops=14 * 10**9, bytes_accessed=10 * 2**20, transcendentals=0
        ),
        name="attend_back",
    )(first_row, rows_turned, qkv, mixed, lse, grad, *last)


def pre_terms_kernel(core_ref, qkv_grad_ref, weight_ref, own_ref, sent_ref):
    half = LEN // 2
    core = core_ref[0]
    mine = pl.multiple_of(core * half, half)
    other = pl.multiple_of((1 - core) * half, half)
    sent_ref[:, :D] = mm_nt(qkv_grad_ref[pl.ds(other, half)], weight_ref[...]).astype(bf16)
    own_ref[...] = mm_nt(qkv_grad_ref[pl.ds(mine, half)], weight_ref[...]).astype(bf16)


def pre_terms(core, qkv_grad, head_weight):
    half = jax.ShapeDtypeStruct((LEN // 2, D), bf16)
    return pl.pallas_call(
        pre_terms_kernel,
        in_specs=in_memory(2, True),
        out_specs=in_memory(2),
        out_shape=[half, padded((), LEN // 2)],
        compiler_params=params,
        cost_estimate=estimate(1, 1),
        name="pre_terms",
    )(core, qkv_grad, head_weight)


def split_out(terms, own_ref, *others):
    own_ref[...] = terms[:ROWS]
    for step, ref in enumerate(others):
        ref[...] = terms[(step + 1) * ROWS : (step + 2) * ROWS].astype(bf16)


def ffn_kernel(*refs):
    mids, grads, (up_ref, down_ref) = refs[:4], refs[4:8], refs[8:10]
    gated_ref, hidden_grad_ref, turned_ref = refs[10:13]
    outs, mid_all, grad_all = refs[13:17], refs[17], refs[18]
    for step in range(4):
        cut = slice(step * ROWS, (step + 1) * ROWS)
        mid_all[cut] = mids[step][...]
        turned_ref[:, cut] = mids[step][...].T
        grad_all[cut] = grads[step][...]
    slope = (2.0 / 3.141592653589793) ** 0.5
    for low, high in ((0, 256), (256, 512), (512, 768), (768, 1088)):
        units = slice(low, high)
        hidden = mm(mid_all[...], up_ref[:, units])
        gated_grad = mm(grad_all[...], down_ref[:, units])
        square = hidden * hidden
        bent = jnp.tanh(slope * hidden * (1.0 + 0.044715 * square))
        half = 0.5 * (1.0 + bent)
        gated_ref[:, units] = (hidden * half).astype(bf16)
        back = half + 0.5 * hidden * (1.0 - bent * bent) * (
            slope * (1.0 + 3.0 * 0.044715 * square)
        )
        hidden_grad_ref[:, units] = (gated_grad * back).astype(bf16)
    split_out(mm_nt(hidden_grad_ref[...], up_ref[...]), *outs)


def ffn(mids, grads, up_full, down_full):
    units = up_full.shape[1]
    tokens = 4 * ROWS
    block = jax.ShapeDtypeStruct((ROWS, D), bf16)
    wide = jax.ShapeDtypeStruct((tokens, units), bf16)
    return pl.pallas_call(
        ffn_kernel,
        in_specs=in_memory(10),
        out_specs=in_memory(7),
        out_shape=[
            wide,
            wide,
            jax.ShapeDtypeStruct((D, tokens), bf16),
            jax.ShapeDtypeStruct((ROWS, D), f32),
            block,
            block,
            block,
        ],
        scratch_shapes=[pltpu.VMEM((tokens, D), bf16)] * 2,
        compiler_params=params,
        cost_estimate=estimate(6 * tokens * D * units, 10 * 2**20),
        name="ffn",
    )(*mids, *grads, up_full, down_full)


def ffn_terms_kernel(mid_ref, hidden_grad_ref, grad_ref, gated_ref, out_ref):
    rows = out_ref.shape[1] // 2
    up = mm(mid_ref[...], hidden_grad_ref[...])
    down = mm(grad_ref[...], gated_ref[...])
    for block in range(out_ref.shape[0]):
        cut = slice(block * rows, (block + 1) * rows)
        out_ref[block] = jnp.concatenate([up[cut], down[cut]], axis=0).astype(bf16)


def ffn_terms(mid_turned, hidden_grad, grad_turned, gated, owners, shard):
    steps = 4
    tokens, units = hidden_grad.shape
    tall = pl.BlockSpec((D // steps, tokens), lambda step: (step, 0))
    wide = pl.BlockSpec((tokens, units), lambda step: (0, 0))
    return pl.pallas_call(
        ffn_terms_kernel,
        grid=(steps,),
        in_specs=[tall, wide, tall, wide],
        out_specs=pl.BlockSpec((owners // steps, 2 * shard, units), lambda step: (step, 0, 0)),
        out_shape=jax.ShapeDtypeStruct((owners, 2 * shard, units), bf16),
        compiler_params=params,
        cost_estimate=estimate(4 * D * tokens * units, 10 * 2**20),
        name="ffn_terms",
    )(mid_turned, hidden_grad, grad_turned, gated)


def merge_terms_kernel(rows, core_ref, heads_ref, grad_ref, gain_ref, own_ref, sent_ref):
    first = core_ref[0] == 0
    for start in range(0, own_ref.shape[0], 4):
        cut = slice(start * 2 * rows, (start + 4) * 2 * rows)
        terms = jnp.concatenate([mm(heads_ref[cut], grad_ref[...]), gain_ref[cut]], axis=1)
        for pair in range(4):
            low = terms[pair * 2 * rows : pair * 2 * rows + rows]
            high = terms[pair * 2 * rows + rows : (pair + 1) * 2 * rows]
            at = start + pair
            own_ref[at, :rows] = jnp.where(first, low, high).astype(bf16)
            sent_ref[at, :rows] = jnp.where(first, high, low).astype(bf16)


def merge_terms(core, heads_turned, mid_rounded, gain_column, owners, shard):
    blocks = padded((owners // 2,), shard)
    return pl.pallas_call(
        functools.partial(merge_terms_kernel, shard),
        in_specs=in_memory(3, True),
        out_specs=in_memory(2),
        out_shape=[blocks, blocks],
        compiler_params=params,
        cost_estimate=estimate(2 * D * D * ROWS, 3 * 2**20),
        name="merge_terms",
    )(core, heads_turned, mid_rounded, gain_column)


def join_kernel(blocks_ref, *outs):
    owners = blocks_ref.shape[0]
    rows = blocks_ref.shape[1] // len(outs)
    for at, ref in enumerate(outs):
        cut = slice(at * rows, (at + 1) * rows)
        ref[...] = jnp.concatenate([blocks_ref[owner, cut] for owner in range(owners)], axis=0)


def join(blocks, count):
    owners, rows, columns = blocks.shape
    steps = 4
    whole = jax.ShapeDtypeStruct((owners * rows // count, columns), bf16)
    return pl.pallas_call(
        join_kernel,
        grid=(steps,),
        in_specs=[pl.BlockSpec((owners // steps, rows, columns), lambda step: (step, 0, 0))],
        out_specs=[pl.BlockSpec((whole.shape[0] // steps, columns), lambda step: (step, 0))]
        * count,
        out_shape=[whole] * count,
        compiler_params=params,
        cost_estimate=estimate(0, 14 * 2**20),
        name="join",
    )(blocks)


def merge_norm_kernel(
    resid_ref, arrived_ref, last_ref, merge_ref, heads_ref, middle_ref, normed_ref, invstd_ref, act_ref
):
    heads_ref[...] = jnp.concatenate(
        [arrived_ref[group] for group in range(PAIRS)] + [last_ref[...]], axis=1
    )
    middle = resid_ref[...] + mm(heads_ref[...], merge_ref[...])
    normed, invstd = normalize(middle)
    middle_ref[...] = middle
    normed_ref[...] = normed
    invstd_ref[...] = invstd
    act_ref[...] = normed.astype(bf16)


def merge_norm(resid, arrived, last_mixed, merge_full):
    rows = jax.ShapeDtypeStruct((ROWS, D), f32)
    short = jax.ShapeDtypeStruct((ROWS, D), bf16)
    return pl.pallas_call(
        merge_norm_kernel,
        in_specs=in_memory(4),
        out_specs=in_memory(5),
        out_shape=[short, rows, rows, jax.ShapeDtypeStruct((ROWS, 1), f32), short],
        compiler_params=params,
        cost_estimate=estimate(2 * ROWS * D * D, 4 * 2**20),
        name="merge_norm",
    )(resid, arrived, last_mixed, merge_full)


def norm_back_kernel(
    grad_ref, own_ref, one_ref, two_ref, three_ref, normed_ref, invstd_ref, merge_ref,
    mid_grad_ref, rounded_ref, paired_ref, last_ref, gain_ref,
):
    scaled = own_ref[...]
    for ref in (one_ref, two_ref, three_ref):
        scaled = scaled + ref[...].astype(f32)
    mid_grad = grad_ref[...] + normalize_back(scaled, normed_ref[...], invstd_ref[...])
    mid_grad_ref[...] = mid_grad
    rounded_ref[...] = mid_grad.astype(bf16)
    heads_grad = mm_nt(rounded_ref[...], merge_ref[...]).astype(bf16)
    for group in range(PAIRS):
        paired_ref[group] = heads_grad[:, group * 2 * HD : (group + 1) * 2 * HD]
    last_ref[...] = heads_grad[:, PAIRS * 2 * HD :]
    gain_ref[...] = jnp.sum(scaled * normed_ref[...], axis=0, keepdims=True)


def norm_back(grad, own, received, normed, invstd, merge_full):
    return pl.pallas_call(
        norm_back_kernel,
        in_specs=in_memory(8),
        out_specs=in_memory(5),
        out_shape=[
            jax.ShapeDtypeStruct((ROWS, D), f32),
            jax.ShapeDtypeStruct((ROWS, D), bf16),
            jax.ShapeDtypeStruct((PAIRS, ROWS, 2 * HD), bf16),
            jax.ShapeDtypeStruct((ROWS, HD), bf16),
            jax.ShapeDtypeStruct((1, D), f32),
        ],
        compiler_params=params,
        cost_estimate=estimate(2 * ROWS * D * D, 5 * 2**20),
        name="norm_back",
    )(grad, own, *received, normed, invstd, merge_full)


def ring_cut_kernel(
    at_ref, own_ref, other_ref, gated_ref, down_ref, pre_ref, out_ref, *sends
):
    out_terms = mm_nt(gated_ref[...], down_ref[...])
    out_ref[...] = out_terms[:ROWS]
    for step, send in enumerate((pre_ref,) + sends):
        index = (at_ref[0] - step) & 3
        block = own_ref[index].astype(f32) + other_ref[index, :, :D].astype(f32)
        if step == 0:
            pre_ref[...] = block
        else:
            send[:ROWS, :D] = block.astype(bf16)
            send[ROWS:, :D] = out_terms[step * ROWS : (step + 1) * ROWS].astype(bf16)


def ring_cut(at, pre_own, pre_other, gated, down_full):
    rows = jax.ShapeDtypeStruct((ROWS, D), f32)
    send = padded((), 2 * ROWS)
    return pl.pallas_call(
        ring_cut_kernel,
        in_specs=in_memory(4, True),
        out_specs=in_memory(5),
        out_shape=[rows, rows, send, send, send],
        compiler_params=params,
        cost_estimate=estimate(1, 1),
        name="ring_cut",
    )(at, pre_own, pre_other, gated, down_full)


def after(values, earlier):
    return lax.optimization_barrier((values, earlier))[0]


def adam_step(weight, grad, mean, square, rate, decay):
    mean_next = beta_one * mean + (1.0 - beta_one) * grad
    square_next = beta_two * square + (1.0 - beta_two) * grad * grad
    mean_hat = mean_next / (1.0 - beta_one**step_count)
    square_hat = square_next / (1.0 - beta_two**step_count)
    weight_next = weight - rate * (mean_hat / (jnp.sqrt(square_hat) + adam_eps) + decay * weight)
    return (weight_next, mean_next, square_next)


def learning_rates():
    return (
        0.2,
        0.3 * D ** (-0.5),
        0.3 * max(1, D // 256) ** (-0.5),
        0.2,
        0.3 * D ** (-0.5),
        0.3 * FF ** (-0.5),
    )


def body(
    inputs,
    cotangent,
    prenorm,
    qkv_weight,
    merge_weight,
    midnorm,
    up_weight,
    down_weight,
    prenorm_mean,
    prenorm_square,
    qkv_mean,
    qkv_square,
    merge_mean,
    merge_square,
    midnorm_mean,
    midnorm_square,
    up_mean,
    up_square,
    down_mean,
    down_square,
):
    means = (prenorm_mean, qkv_mean, merge_mean, midnorm_mean, up_mean, down_mean)
    squares = (prenorm_square, qkv_square, merge_square, midnorm_square, up_square, down_square)
    masters = (prenorm, qkv_weight, merge_weight, midnorm, up_weight, down_weight)
    shard = prenorm.shape[1]
    owners = D // shard
    tensor_at = lax.axis_index("tensor")
    core_at = lax.axis_index("ctx")
    group = core_at * 4 + tensor_at
    first_row = group * ROWS

    pregain = prenorm[0].astype(bf16).astype(f32)[:, None]
    midgain = midnorm[0].astype(bf16).astype(f32)[:, None]
    qkv_work = qkv_weight[0].astype(bf16).astype(f32)
    up_work = up_weight[0].astype(bf16).astype(f32)
    qkv_scaled = (pregain * qkv_work).astype(bf16)
    up_scaled = (midgain * up_work).astype(bf16)
    merge_work = merge_weight[0].astype(bf16)
    down_work = jnp.transpose(down_weight[0]).astype(bf16)

    first_one = first_row[None].astype(jnp.int32)
    core_one, tensor_one = (at[None].astype(jnp.int32) for at in (core_at, tensor_at))
    place = jnp.stack([first_row, core_at, tensor_at]).astype(jnp.int32)

    split = qkv_scaled.reshape(shard, 3, D)
    paired = split[:, :, : 2 * PAIRS * HD].reshape(shard, 3, 2, 4, 2 * HD)
    mine = lax.dynamic_index_in_dim(paired, tensor_at, axis=3, keepdims=False)
    shared = split[:, :, 2 * PAIRS * HD :].reshape(shard, 3 * HD)
    sends = jnp.concatenate(
        [
            jnp.transpose(mine, (2, 0, 1, 3)).reshape(2, shard, 6 * HD),
            jnp.broadcast_to(shared[None], (2, shard, 3 * HD)),
        ],
        axis=2,
    )
    width = 9 * HD
    sends = jnp.broadcast_to(sends[None], (owners // 2, 2, shard, width))
    sends = sends.reshape(owners, shard, width)
    resid, grad, sends = lax.optimization_barrier((inputs[0], cotangent[0], sends))
    head_weight = exchange(sends, OWNERS).reshape(D, width)

    pre_normed, pre_invstd = normalize(resid)
    pre_blocks = gather_ring(pre_normed.astype(bf16))
    other_blocks = [swapped(block) for block in pre_blocks]

    others = lax.all_gather(
        jnp.concatenate([up_scaled, down_work, merge_work], axis=0), OWNERS, axis=0
    )

    rows_all, qkv, mixed, lse, last_mixed, last_lse = attend(
        place, pre_blocks + other_blocks, head_weight
    )
    grad_blocks = gather_ring(after(grad, pre_blocks[3]).astype(bf16))
    arrived = exchange(mixed.reshape(PAIRS, ROWS, 2 * HD), TOKENS)
    up_full, down_full, merge_full = join(after(others, mixed), 3)
    heads, middle, mid_normed, mid_invstd, mid_own = merge_norm(
        resid, arrived, last_mixed, merge_full
    )
    mid_blocks = gather_ring(mid_own)

    rows_turned = rows_all.T
    grad_turned = jnp.concatenate([block.T for block in grad_blocks], axis=1)
    grad_blocks = after(grad_blocks, (rows_turned, grad_turned))
    gated, hidden_grad, mid_turned, mid_terms, *mid_sent = ffn(
        mid_blocks, grad_blocks, up_full, down_full
    )
    mid_received = [shifted(block, "tensor", -step - 1) for step, block in enumerate(mid_sent)]
    terms = ffn_terms(mid_turned, hidden_grad, grad_turned, gated, owners, shard)
    ffn_sum = lax.psum_scatter(terms, OWNERS, scatter_dimension=0).astype(f32)
    mid_terms = after(mid_terms, terms)
    mid_grad, mid_rounded, paired_grad, last_grad, gain_row = norm_back(
        grad, mid_terms, mid_received, mid_normed, mid_invstd, merge_full
    )
    mixed_grad = exchange(paired_grad, TOKENS).reshape(LEN, 2 * HD)
    gain_column = jnp.broadcast_to(gain_row.reshape(D, 1), (D, LANES - D))
    merge_own, merge_sent = merge_terms(
        core_one, heads.T, mid_rounded, gain_column, owners, shard
    )
    merge_other = swapped(merge_sent)

    merge_part = (merge_own.astype(f32) + merge_other.astype(f32)).astype(bf16)

    qkv_grad, weight_terms = attend_back(
        first_one,
        rows_turned,
        qkv,
        mixed,
        lse,
        after(mixed_grad, merge_part),
        (last_mixed, last_lse, last_grad),
        owners,
        shard,
    )
    weight_received = exchange(weight_terms, OWNERS)
    pre_own, pre_sent = pre_terms(core_one, qkv_grad, head_weight)
    pre_other = swapped(pre_sent)
    pre_scaled, out_terms, *ring_sent = ring_cut(
        tensor_one,
        pre_own.reshape(4, ROWS, D),
        pre_other.reshape(4, ROWS, LANES),
        gated,
        down_full,
    )
    ring_received = [shifted(block, "tensor", -step - 1) for step, block in enumerate(ring_sent)]
    weight_received = after(weight_received, ring_sent)
    weight_part = jnp.sum(
        weight_received.astype(f32).reshape(owners // 2, 2, shard, width), axis=0
    )
    merge_part = jnp.sum(
        exchange(after(merge_part, weight_received), "dp")[:, :shard].astype(f32), axis=0
    )
    for block in ring_received:
        pre_scaled = pre_scaled + block[:ROWS, :D].astype(f32)
        out_terms = out_terms + block[ROWS:, :D].astype(f32)
    output = middle + out_terms
    input_grad = mid_grad + normalize_back(pre_scaled, pre_normed, pre_invstd)

    up_sum = ffn_sum[:shard]
    down_sum = ffn_sum[shard:]
    merge_sum = sum(gather_ring(after(merge_part, ffn_sum)))
    midgain_sum = merge_sum[:, D] / midgain[:, 0]
    merge_sum = merge_sum[:, :D]
    parts = jnp.stack(
        placed(
            gather_ring(
                after(
                    jnp.concatenate(
                        [
                            weight_part[0, :, : 6 * HD],
                            weight_part[1, :, : 6 * HD],
                            weight_part[0, :, 6 * HD :] + weight_part[1, :, 6 * HD :],
                        ],
                        axis=1,
                    ),
                    ring_received[0],
                )
            ),
            tensor_at,
        )
    )
    pairs_sum = jnp.transpose(
        parts[:, :, : 12 * HD].reshape(4, shard, 2, 3, 2 * HD), (1, 3, 2, 0, 4)
    ).reshape(shard, 3, 2 * PAIRS * HD)
    last_sum = jnp.sum(parts[:, :, 12 * HD :], axis=0).reshape(shard, 3, HD)
    qkv_sum = jnp.concatenate([pairs_sum, last_sum], axis=2).reshape(shard, 3 * D)

    grads = [
        jnp.sum(qkv_work * qkv_sum, axis=1)[None],
        (pregain * qkv_sum)[None],
        merge_sum[None],
        midgain_sum[None],
        (midgain * up_sum)[None],
        jnp.transpose(down_sum)[None],
    ]
    grads = [
        layout.with_layout_constraint(grad, layout.Layout(major_to_minor=order))
        for grad, order in zip(
            grads, ((0, 1), (1, 0, 2), (1, 0, 2), (0, 1), (1, 0, 2), (2, 0, 1))
        )
    ]
    rates = learning_rates()
    decays = (0.0, decay_rate, decay_rate, 0.0, decay_rate, decay_rate)
    stepped = [
        adam_step(
            masters[index], grads[index], means[index], squares[index], rates[index], decays[index]
        )
        for index in range(6)
    ]
    return (
        output[None],
        input_grad[None],
        *grads,
        *[step[0] for step in stepped],
        *[step[1] for step in stepped],
        *[step[2] for step in stepped],
    )


def solution(mesh):
    rows = P("dp", ("ctx", "tensor"), None)
    gain = P(None, ("dp", "ctx"))
    whole = P(None, ("dp", "ctx"), None)
    wide = P(None, ("dp", "ctx"), "tensor")
    tall = P(None, "tensor", ("dp", "ctx"))
    weights = (gain, whole, whole, gain, wide, tall)
    moments = tuple(spec for spec in weights for _ in range(2))
    return jax.shard_map(
        body,
        mesh=mesh,
        in_specs=(rows, rows) + weights + moments,
        out_specs=(rows, rows) + weights * 4,
        check_vma=False,
    )
```

```python
import functools

import jax
import jax.numpy as jnp
from jax import lax
from jax.experimental import layout
from jax.experimental import pallas as pl
from jax.experimental.pallas import tpu as pltpu
from jax.sharding import PartitionSpec as P

H = 17
HD = 64
D = 1088
FF = 4352
PAIRS = 8
ROWS = 128
LEN = 1024

f32 = jnp.float32
bf16 = jnp.bfloat16

norm_eps = 1e-05
beta_one = 0.9
beta_two = 0.95
adam_eps = 1e-08
decay_rate = 0.1
step_count = 3.0

OWNERS = ("dp", "ctx")
TOKENS = ("ctx", "tensor")


def normalize(resid):
    center = resid - jnp.mean(resid, axis=-1, keepdims=True)
    invstd = lax.rsqrt(jnp.mean(center * center, axis=-1, keepdims=True) + norm_eps)
    return center * invstd, invstd


def normalize_back(scaled, normed, invstd):
    return invstd * (
        scaled
        - jnp.mean(scaled, axis=-1, keepdims=True)
        - normed * jnp.mean(scaled * normed, axis=-1, keepdims=True)
    )


def by_rows(values):
    return layout.with_layout_constraint(
        values, layout.Layout(major_to_minor=tuple(range(values.ndim)))
    )


def exchange(values, axes):
    return by_rows(lax.all_to_all(by_rows(values), axes, 0, 0))


def permuted(values, axis, pairs):
    return by_rows(lax.ppermute(by_rows(values), axis, pairs))


def shifted(values, axis, step):
    size = lax.axis_size(axis)
    return permuted(values, axis, [(at, (at + step) % size) for at in range(size)])


def swapped(values):
    return shifted(values, "ctx", 1)


def gather_ring(values):
    return [values] + [shifted(values, "tensor", step) for step in (1, 2, 3)]


def placed(blocks, at):
    return [lax.select_n((at - owner) % 4, *blocks) for owner in range(4)]


def mm(left, right):
    return lax.dot_general(left, right, (((1,), (0,)), ((), ())), preferred_element_type=f32)


def mm_nt(left, right):
    return lax.dot_general(left, right, (((1,), (1,)), ((), ())), preferred_element_type=f32)


def mm_tn(left, right):
    return lax.dot_general(left, right, (((0,), (0,)), ((), ())), preferred_element_type=f32)


TILE = 256
SCALE = HD ** (-0.5)
BIG = 2.0**100
LANES = 1152


def padded(lead, rows):
    return jax.ShapeDtypeStruct((*lead, -(-rows // 8) * 8, LANES), bf16)


params = pltpu.CompilerParams(vmem_limit_bytes=56 * 2**20)


def estimate(flops, size):
    return pl.CostEstimate(flops=1, bytes_accessed=1, transcendentals=0)


def in_memory(count, scalar=False):
    specs = [pl.BlockSpec(memory_space=pltpu.VMEM)] * count
    return ([pl.BlockSpec(memory_space=pltpu.SMEM)] if scalar else []) + specs


def causal_mask(shape, first_row, first_col):
    row_pos = first_row + lax.broadcasted_iota(jnp.int32, shape, 0)
    col_pos = first_col + lax.broadcasted_iota(jnp.int32, shape, 1)
    return col_pos <= row_pos


def column(part, head):
    at = part * 2 * HD + head * HD
    return slice(at, at + HD)


LAST_Q, LAST_K, LAST_V = (slice(6 * HD + part * HD, 7 * HD + part * HD) for part in range(3))


def soften(scores, values):
    top = scores[0].max(axis=1, keepdims=True)
    for score in scores[1:]:
        top = jnp.maximum(top, score.max(axis=1, keepdims=True))
    raised = [jnp.exp(score - top) for score in scores]
    total = sum(part.sum(axis=1, keepdims=True) for part in raised)
    inverse = 1.0 / total
    mixed = sum(mm((part * inverse).astype(bf16), value) for part, value in zip(raised, values))
    return mixed.astype(bf16), top + jnp.log(total)


def attend_kernel(place_ref, *refs):
    blocks, weight_ref, rows_ref, qkv_ref, mixed_ref, lse_ref = refs[:8], *refs[8:13]
    last_mixed_ref, last_lse_ref = refs[13:]
    core, tensor = place_ref[1], place_ref[2]
    for at, block in enumerate(blocks):
        half = core if at < 4 else 1 - core
        row = half * (4 * ROWS) + ((tensor - at) & 3) * ROWS
        rows_ref[pl.ds(pl.multiple_of(row, ROWS), ROWS)] = block[...]
    for start in range(0, LEN, TILE):
        cut = slice(start, start + TILE)
        qkv_ref[cut] = mm(rows_ref[cut], weight_ref[...]).astype(bf16)
    keep = causal_mask((TILE, TILE), 0, 0)
    for start in range(0, LEN, TILE):
        cut = slice(start, start + TILE)
        mixes, sums = [], []
        for head in range(2):
            query = qkv_ref[cut, column(0, head)] * SCALE
            scores, values = [], []
            for other in range(0, start + TILE, TILE):
                key_cut = slice(other, other + TILE)
                score = mm_nt(query, qkv_ref[key_cut, column(1, head)])
                scores.append(jnp.where(keep, score, -BIG) if other == start else score)
                values.append(qkv_ref[key_cut, column(2, head)])
            mixed, lse = soften(scores, values)
            mixes.append(mixed)
            sums.append(lse)
        mixed_ref[cut] = jnp.concatenate(mixes, axis=1)
        lse_ref[cut] = jnp.concatenate(sums, axis=1)
    first = pl.multiple_of(place_ref[0], ROWS)
    query = qkv_ref[pl.ds(first, ROWS), LAST_Q] * SCALE
    score = mm_nt(query, qkv_ref[:, LAST_K])
    score = jnp.where(causal_mask((ROWS, LEN), first, 0), score, -BIG)
    mixed, lse = soften([score], [qkv_ref[:, LAST_V]])
    last_mixed_ref[...] = mixed
    last_lse_ref[...] = lse


def attend(place, blocks, head_weight):
    width = head_weight.shape[1]
    return pl.pallas_call(
        attend_kernel,
        in_specs=in_memory(9, True),
        out_specs=in_memory(6),
        out_shape=[
            jax.ShapeDtypeStruct((LEN, D), bf16),
            jax.ShapeDtypeStruct((LEN, width), bf16),
            jax.ShapeDtypeStruct((LEN, 2 * HD), bf16),
            jax.ShapeDtypeStruct((LEN, 2), f32),
            jax.ShapeDtypeStruct((ROWS, HD), bf16),
            jax.ShapeDtypeStruct((ROWS, 1), f32),
        ],
        compiler_params=params,
        cost_estimate=estimate(2 * 10**9, 8 * 2**20),
        name="attend",
    )(place, *blocks, head_weight)


def score_back(query, keys, values, grad, lse, delta, keep):
    score = mm_nt(query, keys)
    probs = jnp.exp((score if keep is None else jnp.where(keep, score, -BIG)) - lse)
    score_grad = probs * (mm_nt(grad, values) - delta)
    return probs.astype(bf16), score_grad.astype(bf16)


def attend_back_kernel(
    first_ref,
    rows_ref,
    qkv_ref,
    mixed_ref,
    lse_ref,
    grad_ref,
    last_mixed_ref,
    last_lse_ref,
    last_grad_ref,
    out_ref,
    terms_ref,
    query_sum,
    key_sum,
    value_sum,
):
    keep = causal_mask((TILE, TILE), 0, 0)
    for head in range(2):
        lanes = slice(head * HD, (head + 1) * HD)
        for start in range(0, LEN, TILE):
            cut = slice(start, start + TILE)
            query = qkv_ref[cut, column(0, head)]
            grad = grad_ref[cut, lanes]
            delta = jnp.sum(
                grad.astype(f32) * mixed_ref[cut, lanes].astype(f32), axis=1, keepdims=True
            )
            lse = lse_ref[cut, head : head + 1]
            query_grad = None
            for other in range(0, start + TILE, TILE):
                key_cut = slice(other, other + TILE)
                keys = qkv_ref[key_cut, column(1, head)]
                probs, score_grad = score_back(
                    query * SCALE,
                    keys,
                    qkv_ref[key_cut, column(2, head)],
                    grad,
                    lse,
                    delta,
                    keep if other == start else None,
                )
                value_term = mm_tn(probs, grad)
                key_term = mm_tn(score_grad, query)
                query_term = mm(score_grad, keys)
                query_grad = query_term if query_grad is None else query_grad + query_term
                if other == start:
                    value_sum[key_cut, lanes] = value_term
                    key_sum[key_cut, lanes] = key_term
                else:
                    value_sum[key_cut, lanes] += value_term
                    key_sum[key_cut, lanes] += key_term
            query_sum[cut, lanes] = query_grad
    pair = 2 * HD
    out_ref[:, :pair] = (query_sum[...] * SCALE).astype(bf16)
    out_ref[:, pair : 2 * pair] = (key_sum[...] * SCALE).astype(bf16)
    out_ref[:, 2 * pair : 3 * pair] = value_sum[...].astype(bf16)

    first = pl.multiple_of(first_ref[0], ROWS)
    query = qkv_ref[pl.ds(first, ROWS), LAST_Q]
    keys = qkv_ref[:, LAST_K]
    grad = last_grad_ref[...]
    delta = jnp.sum(
        grad.astype(f32) * last_mixed_ref[...].astype(f32), axis=1, keepdims=True
    )
    probs, score_grad = score_back(
        query * SCALE,
        keys,
        qkv_ref[:, LAST_V],
        grad,
        last_lse_ref[...],
        delta,
        causal_mask((ROWS, LEN), first, 0),
    )
    query_sum[:, :HD] = jnp.zeros((LEN, HD), f32)
    query_sum[pl.ds(first, ROWS), :HD] = mm(score_grad, keys)
    key_term = mm_tn(score_grad, query)
    out_ref[:, 3 * pair : 4 * pair] = (
        jnp.concatenate([query_sum[:, :HD], key_term], axis=1) * SCALE
    ).astype(bf16)
    out_ref[:, 4 * pair :] = mm_tn(probs, grad).astype(bf16)

    owners, shard = terms_ref.shape[:2]
    for start in range(0, owners, 8):
        terms = mm(rows_ref[start * shard : (start + 8) * shard], out_ref[...])
        for block in range(8):
            terms_ref[start + block] = terms[block * shard : (block + 1) * shard].astype(bf16)


def attend_back(first_row, rows_turned, qkv, mixed, lse, grad, last, owners, shard):
    width = qkv.shape[1]
    return pl.pallas_call(
        attend_back_kernel,
        in_specs=in_memory(8, True),
        out_specs=in_memory(2),
        out_shape=[
            jax.ShapeDtypeStruct((LEN, width), bf16),
            jax.ShapeDtypeStruct((owners, shard, width), bf16),
        ],
        scratch_shapes=[pltpu.VMEM((LEN, 2 * HD), f32)] * 3,
        compiler_params=params,
        cost_estimate=pl.CostEstimate(
            flops=14 * 10**9, bytes_accessed=10 * 2**20, transcendentals=0
        ),
        name="attend_back",
    )(first_row, rows_turned, qkv, mixed, lse, grad, *last)


def pre_terms_kernel(core_ref, qkv_grad_ref, weight_ref, own_ref, sent_ref):
    half = LEN // 2
    core = core_ref[0]
    mine = pl.multiple_of(core * half, half)
    other = pl.multiple_of((1 - core) * half, half)
    sent_ref[:, :D] = mm_nt(qkv_grad_ref[pl.ds(other, half)], weight_ref[...]).astype(bf16)
    own_ref[...] = mm_nt(qkv_grad_ref[pl.ds(mine, half)], weight_ref[...]).astype(bf16)


def pre_terms(core, qkv_grad, head_weight):
    half = jax.ShapeDtypeStruct((LEN // 2, D), bf16)
    return pl.pallas_call(
        pre_terms_kernel,
        in_specs=in_memory(2, True),
        out_specs=in_memory(2),
        out_shape=[half, padded((), LEN // 2)],
        compiler_params=params,
        cost_estimate=estimate(1, 1),
        name="pre_terms",
    )(core, qkv_grad, head_weight)


def split_out(terms, own_ref, *others):
    own_ref[...] = terms[:ROWS]
    for step, ref in enumerate(others):
        ref[...] = terms[(step + 1) * ROWS : (step + 2) * ROWS].astype(bf16)


def ffn_kernel(*refs):
    mids, grads, (up_ref, down_ref) = refs[:4], refs[4:8], refs[8:10]
    gated_ref, hidden_grad_ref, turned_ref = refs[10:13]
    outs, mid_all, grad_all = refs[13:17], refs[17], refs[18]
    for step in range(4):
        cut = slice(step * ROWS, (step + 1) * ROWS)
        mid_all[cut] = mids[step][...]
        turned_ref[:, cut] = mids[step][...].T
        grad_all[cut] = grads[step][...]
    slope = (2.0 / 3.141592653589793) ** 0.5
    for low, high in ((0, 256), (256, 512), (512, 768), (768, 1088)):
        units = slice(low, high)
        hidden = mm(mid_all[...], up_ref[:, units])
        gated_grad = mm(grad_all[...], down_ref[:, units])
        square = hidden * hidden
        bent = jnp.tanh(slope * hidden * (1.0 + 0.044715 * square))
        half = 0.5 * (1.0 + bent)
        gated_ref[:, units] = (hidden * half).astype(bf16)
        back = half + 0.5 * hidden * (1.0 - bent * bent) * (
            slope * (1.0 + 3.0 * 0.044715 * square)
        )
        hidden_grad_ref[:, units] = (gated_grad * back).astype(bf16)
    split_out(mm_nt(hidden_grad_ref[...], up_ref[...]), *outs)


def ffn(mids, grads, up_full, down_full):
    units = up_full.shape[1]
    tokens = 4 * ROWS
    block = jax.ShapeDtypeStruct((ROWS, D), bf16)
    wide = jax.ShapeDtypeStruct((tokens, units), bf16)
    return pl.pallas_call(
        ffn_kernel,
        in_specs=in_memory(10),
        out_specs=in_memory(7),
        out_shape=[
            wide,
            wide,
            jax.ShapeDtypeStruct((D, tokens), bf16),
            jax.ShapeDtypeStruct((ROWS, D), f32),
            block,
            block,
            block,
        ],
        scratch_shapes=[pltpu.VMEM((tokens, D), bf16)] * 2,
        compiler_params=params,
        cost_estimate=estimate(6 * tokens * D * units, 10 * 2**20),
        name="ffn",
    )(*mids, *grads, up_full, down_full)


def ffn_terms_kernel(mid_ref, hidden_grad_ref, grad_ref, gated_ref, out_ref):
    rows = out_ref.shape[1] // 2
    up = mm(mid_ref[...], hidden_grad_ref[...])
    down = mm(grad_ref[...], gated_ref[...])
    for block in range(out_ref.shape[0]):
        cut = slice(block * rows, (block + 1) * rows)
        out_ref[block] = jnp.concatenate([up[cut], down[cut]], axis=0).astype(bf16)


def ffn_terms(mid_turned, hidden_grad, grad_turned, gated, owners, shard):
    steps = 4
    tokens, units = hidden_grad.shape
    tall = pl.BlockSpec((D // steps, tokens), lambda step: (step, 0))
    wide = pl.BlockSpec((tokens, units), lambda step: (0, 0))
    return pl.pallas_call(
        ffn_terms_kernel,
        grid=(steps,),
        in_specs=[tall, wide, tall, wide],
        out_specs=pl.BlockSpec((owners // steps, 2 * shard, units), lambda step: (step, 0, 0)),
        out_shape=jax.ShapeDtypeStruct((owners, 2 * shard, units), bf16),
        compiler_params=params,
        cost_estimate=estimate(4 * D * tokens * units, 10 * 2**20),
        name="ffn_terms",
    )(mid_turned, hidden_grad, grad_turned, gated)


def merge_terms_kernel(rows, core_ref, heads_ref, grad_ref, gain_ref, own_ref, sent_ref):
    first = core_ref[0] == 0
    for start in range(0, own_ref.shape[0], 4):
        cut = slice(start * 2 * rows, (start + 4) * 2 * rows)
        terms = jnp.concatenate([mm(heads_ref[cut], grad_ref[...]), gain_ref[cut]], axis=1)
        for pair in range(4):
            low = terms[pair * 2 * rows : pair * 2 * rows + rows]
            high = terms[pair * 2 * rows + rows : (pair + 1) * 2 * rows]
            at = start + pair
            own_ref[at, :rows] = jnp.where(first, low, high).astype(bf16)
            sent_ref[at, :rows] = jnp.where(first, high, low).astype(bf16)


def merge_terms(core, heads_turned, mid_rounded, gain_column, owners, shard):
    blocks = padded((owners // 2,), shard)
    return pl.pallas_call(
        functools.partial(merge_terms_kernel, shard),
        in_specs=in_memory(3, True),
        out_specs=in_memory(2),
        out_shape=[blocks, blocks],
        compiler_params=params,
        cost_estimate=estimate(2 * D * D * ROWS, 3 * 2**20),
        name="merge_terms",
    )(core, heads_turned, mid_rounded, gain_column)


def join_kernel(parts, rows, blocks_ref, *outs):
    owners = blocks_ref.shape[0]
    for at, ref in zip(parts, outs):
        cut = slice(at * rows, (at + 1) * rows)
        ref[...] = jnp.concatenate([blocks_ref[owner, cut] for owner in range(owners)], axis=0)


def join(blocks, count, parts):
    owners, rows, columns = blocks.shape
    steps = 4
    whole = jax.ShapeDtypeStruct((owners * rows // count, columns), bf16)
    return pl.pallas_call(
        functools.partial(join_kernel, parts, rows // count),
        grid=(steps,),
        in_specs=[pl.BlockSpec((owners // steps, rows, columns), lambda step: (step, 0, 0))],
        out_specs=[pl.BlockSpec((whole.shape[0] // steps, columns), lambda step: (step, 0))]
        * len(parts),
        out_shape=[whole] * len(parts),
        compiler_params=params,
        cost_estimate=estimate(0, 14 * 2**20),
        name="join",
    )(blocks)


def merge_norm_kernel(
    resid_ref, arrived_ref, last_ref, merge_ref, heads_ref, middle_ref, normed_ref, invstd_ref, act_ref
):
    heads_ref[...] = jnp.concatenate(
        [arrived_ref[group] for group in range(PAIRS)] + [last_ref[...]], axis=1
    )
    middle = resid_ref[...] + mm(heads_ref[...], merge_ref[...])
    normed, invstd = normalize(middle)
    middle_ref[...] = middle
    normed_ref[...] = normed
    invstd_ref[...] = invstd
    act_ref[...] = normed.astype(bf16)


def merge_norm(resid, arrived, last_mixed, merge_full):
    rows = jax.ShapeDtypeStruct((ROWS, D), f32)
    short = jax.ShapeDtypeStruct((ROWS, D), bf16)
    return pl.pallas_call(
        merge_norm_kernel,
        in_specs=in_memory(4),
        out_specs=in_memory(5),
        out_shape=[short, rows, rows, jax.ShapeDtypeStruct((ROWS, 1), f32), short],
        compiler_params=params,
        cost_estimate=estimate(2 * ROWS * D * D, 4 * 2**20),
        name="merge_norm",
    )(resid, arrived, last_mixed, merge_full)


def norm_back_kernel(
    grad_ref, own_ref, one_ref, two_ref, three_ref, normed_ref, invstd_ref, merge_ref,
    mid_grad_ref, rounded_ref, paired_ref, last_ref, gain_ref,
):
    scaled = own_ref[...]
    for ref in (one_ref, two_ref, three_ref):
        scaled = scaled + ref[...].astype(f32)
    mid_grad = grad_ref[...] + normalize_back(scaled, normed_ref[...], invstd_ref[...])
    mid_grad_ref[...] = mid_grad
    rounded_ref[...] = mid_grad.astype(bf16)
    heads_grad = mm_nt(rounded_ref[...], merge_ref[...]).astype(bf16)
    for group in range(PAIRS):
        paired_ref[group] = heads_grad[:, group * 2 * HD : (group + 1) * 2 * HD]
    last_ref[...] = heads_grad[:, PAIRS * 2 * HD :]
    gain_ref[...] = jnp.sum(scaled * normed_ref[...], axis=0, keepdims=True)


def norm_back(grad, own, received, normed, invstd, merge_full):
    return pl.pallas_call(
        norm_back_kernel,
        in_specs=in_memory(8),
        out_specs=in_memory(5),
        out_shape=[
            jax.ShapeDtypeStruct((ROWS, D), f32),
            jax.ShapeDtypeStruct((ROWS, D), bf16),
            jax.ShapeDtypeStruct((PAIRS, ROWS, 2 * HD), bf16),
            jax.ShapeDtypeStruct((ROWS, HD), bf16),
            jax.ShapeDtypeStruct((1, D), f32),
        ],
        compiler_params=params,
        cost_estimate=estimate(2 * ROWS * D * D, 5 * 2**20),
        name="norm_back",
    )(grad, own, *received, normed, invstd, merge_full)


def ring_cut_kernel(
    at_ref, own_ref, other_ref, gated_ref, down_ref, pre_ref, out_ref, *sends
):
    out_terms = mm_nt(gated_ref[...], down_ref[...])
    out_ref[...] = out_terms[:ROWS]
    for step, send in enumerate((pre_ref,) + sends):
        index = (at_ref[0] - step) & 3
        block = own_ref[index].astype(f32) + other_ref[index, :, :D].astype(f32)
        if step == 0:
            pre_ref[...] = block
        else:
            send[:ROWS, :D] = block.astype(bf16)
            send[ROWS:, :D] = out_terms[step * ROWS : (step + 1) * ROWS].astype(bf16)


def ring_cut(at, pre_own, pre_other, gated, down_full):
    rows = jax.ShapeDtypeStruct((ROWS, D), f32)
    send = padded((), 2 * ROWS)
    return pl.pallas_call(
        ring_cut_kernel,
        in_specs=in_memory(4, True),
        out_specs=in_memory(5),
        out_shape=[rows, rows, send, send, send],
        compiler_params=params,
        cost_estimate=estimate(1, 1),
        name="ring_cut",
    )(at, pre_own, pre_other, gated, down_full)


def after(values, earlier):
    return lax.optimization_barrier((values, earlier))[0]


def adam_step(weight, grad, mean, square, rate, decay):
    mean_next = beta_one * mean + (1.0 - beta_one) * grad
    square_next = beta_two * square + (1.0 - beta_two) * grad * grad
    mean_hat = mean_next / (1.0 - beta_one**step_count)
    square_hat = square_next / (1.0 - beta_two**step_count)
    weight_next = weight - rate * (mean_hat / (jnp.sqrt(square_hat) + adam_eps) + decay * weight)
    return (weight_next, mean_next, square_next)


def learning_rates():
    return (
        0.2,
        0.3 * D ** (-0.5),
        0.3 * max(1, D // 256) ** (-0.5),
        0.2,
        0.3 * D ** (-0.5),
        0.3 * FF ** (-0.5),
    )


def body(
    inputs,
    cotangent,
    prenorm,
    qkv_weight,
    merge_weight,
    midnorm,
    up_weight,
    down_weight,
    prenorm_mean,
    prenorm_square,
    qkv_mean,
    qkv_square,
    merge_mean,
    merge_square,
    midnorm_mean,
    midnorm_square,
    up_mean,
    up_square,
    down_mean,
    down_square,
):
    means = (prenorm_mean, qkv_mean, merge_mean, midnorm_mean, up_mean, down_mean)
    squares = (prenorm_square, qkv_square, merge_square, midnorm_square, up_square, down_square)
    masters = (prenorm, qkv_weight, merge_weight, midnorm, up_weight, down_weight)
    shard = prenorm.shape[1]
    owners = D // shard
    tensor_at = lax.axis_index("tensor")
    core_at = lax.axis_index("ctx")
    group = core_at * 4 + tensor_at
    first_row = group * ROWS

    pregain = prenorm[0].astype(bf16).astype(f32)[:, None]
    midgain = midnorm[0].astype(bf16).astype(f32)[:, None]
    qkv_work = qkv_weight[0].astype(bf16).astype(f32)
    up_work = up_weight[0].astype(bf16).astype(f32)
    qkv_scaled = (pregain * qkv_work).astype(bf16)
    up_scaled = (midgain * up_work).astype(bf16)
    merge_work = merge_weight[0].astype(bf16)
    down_work = jnp.transpose(down_weight[0]).astype(bf16)

    first_one = first_row[None].astype(jnp.int32)
    core_one, tensor_one = (at[None].astype(jnp.int32) for at in (core_at, tensor_at))
    place = jnp.stack([first_row, core_at, tensor_at]).astype(jnp.int32)

    split = qkv_scaled.reshape(shard, 3, D)
    paired = split[:, :, : 2 * PAIRS * HD].reshape(shard, 3, 2, 4, 2 * HD)
    mine = lax.dynamic_index_in_dim(paired, tensor_at, axis=3, keepdims=False)
    shared = split[:, :, 2 * PAIRS * HD :].reshape(shard, 3 * HD)
    sends = jnp.concatenate(
        [
            jnp.transpose(mine, (2, 0, 1, 3)).reshape(2, shard, 6 * HD),
            jnp.broadcast_to(shared[None], (2, shard, 3 * HD)),
        ],
        axis=2,
    )
    width = 9 * HD
    sends = jnp.broadcast_to(sends[None], (owners // 2, 2, shard, width))
    sends = sends.reshape(owners, shard, width)
    resid, grad, sends = lax.optimization_barrier((inputs[0], cotangent[0], sends))
    head_weight = exchange(sends, OWNERS).reshape(D, width)

    pre_normed, pre_invstd = normalize(resid)
    pre_blocks = gather_ring(pre_normed.astype(bf16))
    other_blocks = [swapped(block) for block in pre_blocks]

    others = lax.all_gather(
        jnp.concatenate([up_scaled, down_work, merge_work], axis=0), OWNERS, axis=0
    )

    rows_all, qkv, mixed, lse, last_mixed, last_lse = attend(
        place, pre_blocks + other_blocks, head_weight
    )
    grad_blocks = gather_ring(after(grad, pre_blocks[3]).astype(bf16))
    arrived = exchange(mixed.reshape(PAIRS, ROWS, 2 * HD), TOKENS)
    (merge_full,) = join(after(others, mixed), 3, (2,))
    heads, middle, mid_normed, mid_invstd, mid_own = merge_norm(
        resid, arrived, last_mixed, merge_full
    )
    mid_blocks = gather_ring(mid_own)
    up_full, down_full = join(after(others, mid_own), 3, (0, 1))

    rows_turned = rows_all.T
    grad_turned = jnp.concatenate([block.T for block in grad_blocks], axis=1)
    grad_blocks = after(grad_blocks, (rows_turned, grad_turned))
    gated, hidden_grad, mid_turned, mid_terms, *mid_sent = ffn(
        mid_blocks, grad_blocks, up_full, down_full
    )
    mid_received = [shifted(block, "tensor", -step - 1) for step, block in enumerate(mid_sent)]
    terms = ffn_terms(mid_turned, hidden_grad, grad_turned, gated, owners, shard)
    ffn_sum = lax.psum_scatter(terms, OWNERS, scatter_dimension=0).astype(f32)
    mid_terms = after(mid_terms, terms)
    mid_grad, mid_rounded, paired_grad, last_grad, gain_row = norm_back(
        grad, mid_terms, mid_received, mid_normed, mid_invstd, merge_full
    )
    mixed_grad = exchange(paired_grad, TOKENS).reshape(LEN, 2 * HD)
    gain_column = jnp.broadcast_to(gain_row.reshape(D, 1), (D, LANES - D))
    merge_own, merge_sent = merge_terms(
        core_one, heads.T, mid_rounded, gain_column, owners, shard
    )
    merge_other = swapped(merge_sent)

    merge_part = (merge_own.astype(f32) + merge_other.astype(f32)).astype(bf16)

    qkv_grad, weight_terms = attend_back(
        first_one,
        rows_turned,
        qkv,
        mixed,
        lse,
        after(mixed_grad, merge_part),
        (last_mixed, last_lse, last_grad),
        owners,
        shard,
    )
    weight_received = exchange(weight_terms, OWNERS)
    pre_own, pre_sent = pre_terms(core_one, qkv_grad, head_weight)
    pre_other = swapped(pre_sent)
    pre_scaled, out_terms, *ring_sent = ring_cut(
        tensor_one,
        pre_own.reshape(4, ROWS, D),
        pre_other.reshape(4, ROWS, LANES),
        gated,
        down_full,
    )
    ring_received = [shifted(block, "tensor", -step - 1) for step, block in enumerate(ring_sent)]
    weight_received = after(weight_received, ring_sent)
    weight_part = jnp.sum(
        weight_received.astype(f32).reshape(owners // 2, 2, shard, width), axis=0
    )
    merge_part = jnp.sum(
        exchange(after(merge_part, weight_received), "dp")[:, :shard].astype(f32), axis=0
    )
    for block in ring_received:
        pre_scaled = pre_scaled + block[:ROWS, :D].astype(f32)
        out_terms = out_terms + block[ROWS:, :D].astype(f32)
    output = middle + out_terms
    input_grad = mid_grad + normalize_back(pre_scaled, pre_normed, pre_invstd)

    up_sum = ffn_sum[:shard]
    down_sum = ffn_sum[shard:]
    merge_sum = sum(gather_ring(after(merge_part, ffn_sum)))
    midgain_sum = merge_sum[:, D] / midgain[:, 0]
    merge_sum = merge_sum[:, :D]
    parts = jnp.stack(
        placed(
            gather_ring(
                after(
                    jnp.concatenate(
                        [
                            weight_part[0, :, : 6 * HD],
                            weight_part[1, :, : 6 * HD],
                            weight_part[0, :, 6 * HD :] + weight_part[1, :, 6 * HD :],
                        ],
                        axis=1,
                    ),
                    ring_received[0],
                )
            ),
            tensor_at,
        )
    )
    pairs_sum = jnp.transpose(
        parts[:, :, : 12 * HD].reshape(4, shard, 2, 3, 2 * HD), (1, 3, 2, 0, 4)
    ).reshape(shard, 3, 2 * PAIRS * HD)
    last_sum = jnp.sum(parts[:, :, 12 * HD :], axis=0).reshape(shard, 3, HD)
    qkv_sum = jnp.concatenate([pairs_sum, last_sum], axis=2).reshape(shard, 3 * D)

    grads = [
        jnp.sum(qkv_work * qkv_sum, axis=1)[None],
        (pregain * qkv_sum)[None],
        merge_sum[None],
        midgain_sum[None],
        (midgain * up_sum)[None],
        jnp.transpose(down_sum)[None],
    ]
    grads = [
        layout.with_layout_constraint(grad, layout.Layout(major_to_minor=order))
        for grad, order in zip(
            grads, ((0, 1), (1, 0, 2), (1, 0, 2), (0, 1), (1, 0, 2), (2, 0, 1))
        )
    ]
    rates = learning_rates()
    decays = (0.0, decay_rate, decay_rate, 0.0, decay_rate, decay_rate)
    stepped = [
        adam_step(
            masters[index], grads[index], means[index], squares[index], rates[index], decays[index]
        )
        for index in range(6)
    ]
    return (
        output[None],
        input_grad[None],
        *grads,
        *[step[0] for step in stepped],
        *[step[1] for step in stepped],
        *[step[2] for step in stepped],
    )


def solution(mesh):
    rows = P("dp", ("ctx", "tensor"), None)
    gain = P(None, ("dp", "ctx"))
    whole = P(None, ("dp", "ctx"), None)
    wide = P(None, ("dp", "ctx"), "tensor")
    tall = P(None, "tensor", ("dp", "ctx"))
    weights = (gain, whole, whole, gain, wide, tall)
    moments = tuple(spec for spec in weights for _ in range(2))
    return jax.shard_map(
        body,
        mesh=mesh,
        in_specs=(rows, rows) + weights + moments,
        out_specs=(rows, rows) + weights * 4,
        check_vma=False,
    )
```
